32 devices in a mesh: dp: 8 (over y, x, core), mp: 4 (over z).
Axes of the slice: x: 2, y: 2, z: 4, core: 2. Of those that a mesh axis runs over, the one named last changes fastest.
Arguments:
- inputs: bfloat16 [10240, 768], P(('dp', 'mp')), may hold values from -6 to 6
- encoded: bfloat16 [16384, 768], P(('dp', 'mp')), may hold values from -6 to 6
- cotangent: bfloat16 [10240, 768], P(('dp', 'mp')), may hold values from -6 to 6
- lengths: int32 [16], P('dp'), may hold values from 224 to 640, as said below
- buckets: int32 [640], replicated, may hold values from 0 to 31
- self_gain: float32 [768], replicated, may hold values from 0.5 to 1.5
- self_query: bfloat16 [768, 768], P(None, 'mp'), may hold values from -0.078125 to 0.078125
- self_key: bfloat16 [768, 768], P(None, 'mp'), may hold values from -0.078125 to 0.078125
- self_value: bfloat16 [768, 768], P(None, 'mp'), may hold values from -0.21875 to 0.21875
- self_output: bfloat16 [768, 768], P('mp'), may hold values from -3 to 3
- bias_table: float32 [32, 12], P(None, 'mp'), may hold values from -4 to 4
- cross_gain: float32 [768], replicated, may hold values from 0.5 to 1.5
- cross_query: bfloat16 [768, 768], P(None, 'mp'), may hold values from -0.078125 to 0.078125
- cross_key: bfloat16 [768, 768], P(None, 'mp'), may hold values from -0.078125 to 0.078125
- cross_value: bfloat16 [768, 768], P(None, 'mp'), may hold values from -0.21875 to 0.21875
- cross_output: bfloat16 [768, 768], P('mp'), may hold values from -3.5 to 3.5
- feed_gain: float32 [768], replicated, may hold values from 0.5 to 1.5
- feed_inner: bfloat16 [768, 3072], P(None, 'mp'), may hold values from -0.21875 to 0.21875
- feed_output_weight: bfloat16 [3072, 768], P('mp'), may hold values from -0.15625 to 0.15625
Outputs:
- result: bfloat16 [10240, 768], P(('dp', 'mp'))
- input_grad: bfloat16 [10240, 768], P(('dp', 'mp'))
- encoder_grad: bfloat16 [16384, 768], P(('dp', 'mp'))
- grad_self_gain: float32 [768], replicated
- grad_self_query: float32 [768, 768], P('dp', 'mp')
- grad_self_key: float32 [768, 768], P('dp', 'mp')
- grad_self_value: float32 [768, 768], P('dp', 'mp')
- grad_self_output: float32 [768, 768], P('mp', 'dp')
- grad_bias_table: float32 [32, 12], P(None, 'mp')
- grad_cross_gain: float32 [768], replicated
- grad_cross_query: float32 [768, 768], P('dp', 'mp')
- grad_cross_key: float32 [768, 768], P('dp', 'mp')
- grad_cross_value: float32 [768, 768], P('dp', 'mp')
- grad_cross_output: float32 [768, 768], P('mp', 'dp')
- grad_feed_gain: float32 [768], replicated
- grad_feed_inner: float32 [768, 3072], P('dp', 'mp')
- grad_feed_outer: float32 [3072, 768], P('mp', 'dp')
The draws below stay inside these ranges and needn't reach their ends.
Inputs may be any that keep to these rules, and one draw needn't show every extreme that they name: `lengths`: each length is 640 or 224; both occur.
All inputs are finite; a program needn't handle non-finite values.
Results may differ from the reference program's by a relative error of at most 0.024.
Values may be sent and summed in bfloat16 or wider, within the bound.
A program may use at most 384 MiB of HBM per device.

```python
import jax
import jax.numpy as jnp
from jax import lax

D = 768
H = 12
DH = 64
FF = 3072
BUCKETS = 32
SLOTS = 640
SHORT = 224
ENC = 1024
SEQ_GRP = 2
SEQS = 16
TOKENS = 10240
ENC_TOKENS = 16384
N_DP = 8


def draw_lengths(key, part):
    coin = jax.random.randint(key, (SEQS,), 0, 9)
    drawn = jnp.where(coin < 5, SLOTS, SHORT).astype(jnp.int32)
    drawn = drawn.at[0].set(SLOTS)
    return drawn.at[1].set(SHORT)


def touch_ends(result, key, least, top_value):
    extent = result.shape
    spot = [jax.random.randint(jax.random.fold_in(key, axis), (), 0, extent[axis]) for axis in range(len(extent))]
    result = result.at[tuple(spot)].set(least)
    longest = extent.index(max(extent))
    spot[longest] = (spot[longest] + 1) % extent[longest]
    return result.at[tuple(spot)].set(top_value)


def level_of(stream_key, shape, split, low, top_value):
    def one(position, shards_of):
        heights = jax.random.uniform(jax.random.fold_in(jax.random.fold_in(stream_key, 6), position), (shards_of,), jnp.float32, low / len(split), top_value / len(split))
        return jnp.repeat(jnp.exp(heights), shape[position] // shards_of).reshape((-1,) + (1,) * (len(shape) - position - 1))

    level = one(*split[0])
    for cut in split[1:]:
        level = level * one(*cut)
    return level


def normal_values(key, extent, width, reach, cuts=(), kind=jnp.bfloat16):
    entries = jax.random.normal(key, extent, jnp.float32) * width
    if len(cuts) > 0:
        entries = level_of(key, extent, cuts, -0.22, 0.18) * entries
    return jnp.clip(entries, min=-reach, max=reach).astype(kind)


def setup_inputs(seed: int = 0) -> dict:
    key_list = jax.random.split(jax.random.key(seed), 20)
    inputs = normal_values(key_list[0], (TOKENS, D), 1.0, 6.0, ((0, 32),))
    encoded = normal_values(key_list[1], (ENC_TOKENS, D), 1.0, 6.0, ((0, 32),))
    cotangent = normal_values(key_list[2], (TOKENS, D), 1.0, 6.0, ((0, 32),))
    lengths = draw_lengths(jax.random.fold_in(key_list[19], 71), 0)
    buckets = touch_ends(jax.random.randint(key_list[4], (SLOTS,), 0, BUCKETS), jax.random.fold_in(key_list[4], 1), 0, BUCKETS - 1).astype(jnp.int32)
    self_gain = jnp.clip(1.0 + 0.1 * jax.random.normal(key_list[5], (D,), jnp.float32), 0.5, 1.5)
    self_query = normal_values(key_list[6], (D, H * DH), (D * DH // 8) ** -0.5, 0.078125, ((1, 4),))
    self_key = normal_values(key_list[7], (D, H * DH), (D * DH // 8) ** -0.5, 0.078125, ((1, 4),))
    self_value = normal_values(key_list[8], (D, H * DH), D ** -0.5, 0.21875, ((1, 4),))
    self_output = normal_values(key_list[9], (H * DH, D), 4 ** -0.5, 3.0, ((0, 4),))
    bias_table = normal_values(key_list[10], (BUCKETS, H), 1.0, 4.0, ((1, 4),), jnp.float32)
    cross_gain = jnp.clip(1.0 + 0.1 * jax.random.normal(key_list[11], (D,), jnp.float32), 0.5, 1.5)
    cross_query = normal_values(key_list[12], (D, H * DH), (D * DH // 8) ** -0.5, 0.078125, ((1, 4),))
    cross_key = normal_values(key_list[13], (D, H * DH), (D * DH // 8) ** -0.5, 0.078125, ((1, 4),))
    cross_value = normal_values(key_list[14], (D, H * DH), D ** -0.5, 0.21875, ((1, 4),))
    cross_output = normal_values(key_list[15], (H * DH, D), 3 ** -0.5, 3.5, ((0, 4),))
    feed_gain = jnp.clip(1.0 + 0.1 * jax.random.normal(key_list[16], (D,), jnp.float32), 0.5, 1.5)
    feed_inner = normal_values(key_list[17], (D, FF), D ** -0.5, 0.21875, ((1, 4),))
    feed_output_weight = normal_values(key_list[18], (FF, D), (FF // 2) ** -0.5, 0.15625, ((0, 4),))
    return {"inputs": inputs, "encoded": encoded, "cotangent": cotangent, "lengths": lengths, "buckets": buckets, "self_gain": self_gain, "self_query": self_query, "self_key": self_key, "self_value": self_value, "self_output": self_output, "bias_table": bias_table, "cross_gain": cross_gain, "cross_query": cross_query, "cross_key": cross_key, "cross_value": cross_value, "cross_output": cross_output, "feed_gain": feed_gain, "feed_inner": feed_inner, "feed_output_weight": feed_output_weight}


@jax.custom_vjp
def low(v):
    return lax.optimization_barrier(v.astype(jnp.bfloat16)).astype(jnp.float32)

@jax.custom_vjp
def low_back(v):
    return v

def low_keep(v):
    return (low(v), None)

def low_pass(kept, grad):
    return (grad,)

def back_keep(v):
    return (v, None)

def back_low(kept, grad):
    return (low(grad),)
low.defvjp(low_keep, low_pass)
low_back.defvjp(back_keep, back_low)
eps_norm = 1e-06
masked_value = -1e+30
highest = lax.Precision.HIGHEST

def matrix_product(left_side, right_side):
    return jnp.dot(left_side, right_side, precision=highest)

def rms_norm(values, gain):
    return values * lax.rsqrt(lax.optimization_barrier(jnp.mean(values * values, axis=-1, keepdims=True)) + eps_norm) * gain

def attend(query_rows, key_rows, value_rows, bias_grid, valid_mask):
    scores = low_back(jnp.einsum('qhd,khd->hqk', query_rows, key_rows, precision=highest) + bias_grid)
    scores = jnp.where(valid_mask[None], scores, masked_value)
    weights = jax.nn.softmax(scores, axis=-1)
    mixed = jnp.einsum('hqk,khd->qhd', low(weights), value_rows, precision=highest)
    return low_back(low(mixed))

def layer(rows_in, enc_in, group_lengths, buckets, params):
    self_gain, self_query, self_key, self_value, self_output, bias_table, cross_gain, cross_query, cross_key, cross_value, cross_output, feed_gain, feed_inner, feed_output_weight = params
    positions = jnp.arange(SLOTS, dtype=jnp.int32)
    offsets = jnp.maximum(positions[:, None] - positions[None, :], 0)
    bias_grid = jnp.transpose(bias_table[buckets[offsets]], (2, 0, 1))
    causal = positions[None, :] <= positions[:, None]
    normed = low(rms_norm(rows_in, self_gain))
    queries = low_back(low(matrix_product(normed, self_query))).reshape(SEQ_GRP, SLOTS, H, DH)
    keys_all = low_back(low(matrix_product(normed, self_key))).reshape(SEQ_GRP, SLOTS, H, DH)
    values_all = low_back(low(matrix_product(normed, self_value))).reshape(SEQ_GRP, SLOTS, H, DH)

    def self_one(sequence_in):
        query_rows, key_rows, value_rows, length = sequence_in
        return attend(query_rows, key_rows, value_rows, bias_grid, causal & (positions[None, :] < length))
    mixed = lax.map(jax.checkpoint(self_one), (queries, keys_all, values_all, group_lengths))
    mixed = mixed.reshape(SEQ_GRP * SLOTS, H * DH)
    resid_one = rows_in + low_back(matrix_product(mixed, self_output))
    normed = low(rms_norm(resid_one, cross_gain))
    queries = low_back(low(matrix_product(normed, cross_query))).reshape(SEQ_GRP, SLOTS, H, DH)
    keys_all = low_back(low(matrix_product(enc_in, cross_key))).reshape(SEQ_GRP, ENC, H, DH)
    values_all = low_back(low(matrix_product(enc_in, cross_value))).reshape(SEQ_GRP, ENC, H, DH)
    every_key = jnp.ones((SLOTS, ENC), dtype=jnp.bool_)

    def cross_one(sequence_in):
        query_rows, key_rows, value_rows = sequence_in
        return attend(query_rows, key_rows, value_rows, 0.0, every_key)
    mixed = lax.map(jax.checkpoint(cross_one), (queries, keys_all, values_all))
    mixed = mixed.reshape(SEQ_GRP * SLOTS, H * DH)
    resid_two = resid_one + low_back(matrix_product(mixed, cross_output))
    normed = low(rms_norm(resid_two, feed_gain))
    before_act = low_back(matrix_product(normed, feed_inner))
    hidden = low_back(low(jax.nn.gelu(before_act, approximate=True)))
    return resid_two + low_back(matrix_product(hidden, feed_output_weight))

def reference(inputs, encoded, cotangent, lengths, buckets, self_gain, self_query, self_key, self_value, self_output, bias_table, cross_gain, cross_query, cross_key, cross_value, cross_output, feed_gain, feed_inner, feed_output_weight):
    params = tuple((weight_in.astype(jnp.float32) for weight_in in (self_gain, self_query, self_key, self_value, self_output, bias_table, cross_gain, cross_query, cross_key, cross_value, cross_output, feed_gain, feed_inner, feed_output_weight)))
    rows_all = inputs.astype(jnp.float32).reshape(N_DP, SEQ_GRP * SLOTS, D)
    enc_all = encoded.astype(jnp.float32).reshape(N_DP, SEQ_GRP * ENC, D)
    cot_all = cotangent.astype(jnp.float32).reshape(N_DP, SEQ_GRP * SLOTS, D)
    len_all = lengths.reshape(N_DP, SEQ_GRP)

    def group_step(totals, group_in):
        rows_in, enc_in, cot_in, group_lengths = group_in

        def apply_layer(rows_arg, enc_arg, *weights):
            return layer(rows_arg, enc_arg, group_lengths, buckets, weights)
        outcome, pullback = jax.vjp(apply_layer, rows_in, enc_in, *params)
        grads = pullback(cot_in)
        totals = tuple((first_term + second_term for first_term, second_term in zip(totals, grads[2:])))
        return (totals, (outcome, grads[0], grads[1]))
    zero_grads = tuple((jnp.zeros_like(weight_in) for weight_in in params))
    totals, (outcome, input_grad, encoder_grad) = lax.scan(group_step, zero_grads, (rows_all, enc_all, cot_all, len_all))
    return (outcome.reshape(TOKENS, D).astype(jnp.bfloat16), input_grad.reshape(TOKENS, D).astype(jnp.bfloat16), encoder_grad.reshape(ENC_TOKENS, D).astype(jnp.bfloat16), totals[0], totals[1], totals[2], totals[3], totals[4], totals[5], totals[6], totals[7], totals[8], totals[9], totals[10], totals[11], totals[12], totals[13])
```

```python
import functools

import jax
import jax.numpy as jnp
from jax import lax
from jax.experimental import pallas as pl
from jax.experimental.pallas import tpu as pltpu
from jax.sharding import PartitionSpec as P

EPS = 1e-06
MASKED = -1e30
DH = 64
F32 = jnp.float32
BF16 = jnp.bfloat16
VMEM_BYTES = 62 << 20
ROOT = 0.7978845608028654
CUBE = 0.044715


def mm(a, b):
    return jnp.dot(a, b, preferred_element_type=F32)


def mm_nt(a, b):
    return lax.dot_general(a, b, (((1,), (1,)), ((), ())), preferred_element_type=F32)


def low(v):
    return v.astype(BF16)


def flip(v):
    return jnp.transpose(v.astype(F32)).astype(BF16)


def norm_rows(v, gain):
    root = lax.rsqrt(jnp.mean(v * v, axis=-1, keepdims=True) + EPS)
    unit = v * root
    return unit * gain, unit, root


def norm_back(grad, v, gain):
    _, unit, root = norm_rows(v, gain)
    scaled = grad * gain
    back = root * (scaled - unit * jnp.mean(scaled * unit, axis=-1, keepdims=True))
    return back, jnp.sum(grad * unit, axis=0, keepdims=True)


def half_of_sequence(halves):
    return lax.rem(lax.axis_index("mp"), halves)


def chunks(rows, step):
    return [(r, min(step, rows - r)) for r in range(0, rows, step)]


def forward_kernel(
    halves,
    len_ref,
    x_ref,
    xa_ref,
    enc_hbm,
    gains_ref,
    diag_ref,
    w_hbm,
    result_ref,
    n1_out,
    q1_out,
    kv1_out,
    p1_out,
    o1_out,
    l1_out,
    x1_out,
    n2_out,
    q2_out,
    kv2_out,
    p2_out,
    o2_out,
    l2_out,
    x2_out,
    n3_out,
    hid_out,
    slope_out,
    w,
    enc,
    mask,
    s_buf,
    n1,
    q1,
    kv1,
    p1,
    o1,
    x1,
    n2,
    q2,
    kv2,
    p2,
    o2,
    x2,
    n3,
    hid,
    slope,
    l1,
    l2,
    acc,
    w_sem,
    enc_sem,
    out_sem,
):
    rows = x_ref.shape[0]
    parts = w.shape[1]
    half = half_of_sequence(halves)

    def fetch(g, z):
        return pltpu.make_async_copy(w_hbm.at[g, z], w.at[g, z], w_sem.at[g, z])

    enc_copy = pltpu.make_async_copy(enc_hbm, enc, enc_sem)
    for g in range(4):
        for z in range(parts):
            fetch(g, z).start()
        if g == 0:
            enc_copy.start()

    saves = []

    def save(src, dst):
        copy = pltpu.make_async_copy(src, dst, out_sem.at[len(saves)])
        copy.start()
        saves.append(copy)

    n1[0:rows, :] = low(norm_rows(xa_ref[...].astype(F32), gains_ref[0:1, :])[0])
    n1[rows : 2 * rows, :] = low(norm_rows(x_ref[...].astype(F32), gains_ref[0:1, :])[0])
    save(n1, n1_out)

    length = len_ref[0]
    i = lax.broadcasted_iota(jnp.int32, mask.shape, 0)
    c = lax.broadcasted_iota(jnp.int32, mask.shape, 1)
    own = c - rows
    limit = jnp.where(half > 0, length, 0)
    ok = ((own < 0) & (c < limit)) | ((own >= 0) & (own <= i) & (own + half * rows < length))
    mask[...] = jnp.where(ok, 0.0, MASKED)

    def heads(z, q, kv, p, o, l, keys, with_bias):
        outs = []
        for j in range(3):
            h = z * 3 + j
            q_h = q[z, :, DH * j : DH * (j + 1)]
            k_h = kv[z, :, DH * j : DH * (j + 1)]
            v_h = kv[z, :, DH * (3 + j) : DH * (4 + j)]
            s_buf[j, :, 0:keys] = mm_nt(q_h, k_h)
            for r, n in chunks(rows, 32):
                s = s_buf[j, r : r + n, 0:keys]
                if with_bias:
                    line = jnp.broadcast_to(diag_ref[pl.ds(h, 1), :], (n, diag_ref.shape[1]))
                    grid = pltpu.roll(line, r, 1, stride=1, stride_axis=0)
                    s = s + grid[:, 0:keys] + mask[r : r + n, :]
                top = jnp.max(s, axis=1, keepdims=True)
                p[h, r : r + n, :] = low(jnp.exp(s - top))
            wide = jnp.concatenate([v_h, jnp.ones_like(v_h)], axis=1)
            mixed = mm(p[h], wide)
            outs.append(low(mixed[:, 0:DH] / mixed[:, DH : 2 * DH]))
            l[z, :, 32 * j : 32 * (j + 1)] = mixed[:, DH : DH + 32]
        o[z] = jnp.concatenate(outs, axis=1)

    acc[...] = x_ref[...].astype(F32)

    def self_step(z, carry):
        fetch(0, z).wait()
        kv1[z] = low(mm(n1[...], w[0, z, :, 0:384]))
        q1[z] = low(mm(n1[rows : 2 * rows, :], w[0, z, :, 384:576]))
        heads(z, q1, kv1, p1, o1, l1, 2 * rows, True)
        acc[...] += mm_nt(o1[z], w[0, z, :, 576:768])
        return carry

    lax.fori_loop(0, parts, self_step, 0)
    for src, dst in ((q1, q1_out), (kv1, kv1_out), (p1, p1_out), (o1, o1_out), (l1, l1_out)):
        save(src, dst)
    x1[...] = acc[...]
    n2[...] = low(norm_rows(acc[...], gains_ref[1:2, :])[0])
    save(x1, x1_out)
    save(n2, n2_out)
    enc_copy.wait()
    keys = enc.shape[0]

    def cross_step(z, carry):
        fetch(1, z).wait()
        kv2[z] = low(mm(enc[...], w[1, z, :, 0:384]))
        q2[z] = low(mm(n2[...], w[1, z, :, 384:576]))
        heads(z, q2, kv2, p2, o2, l2, keys, False)
        acc[...] += mm_nt(o2[z], w[1, z, :, 576:768])
        return carry

    lax.fori_loop(0, parts, cross_step, 0)
    for src, dst in ((q2, q2_out), (kv2, kv2_out), (p2, p2_out), (o2, o2_out), (l2, l2_out)):
        save(src, dst)
    x2[...] = acc[...]
    n3[...] = low(norm_rows(acc[...], gains_ref[2:3, :])[0])
    save(x2, x2_out)
    save(n3, n3_out)

    def feed_step(z, carry):
        fetch(2, z).wait()
        fetch(3, z).wait()
        for r, n in chunks(rows, 64):
            a = mm(n3[r : r + n, :], w[2, z])
            sq = a * a
            t = jnp.tanh(a * (ROOT + ROOT * CUBE * sq))
            cdf = 0.5 + 0.5 * t
            hid[z, r : r + n, :] = low(a * cdf)
            slope[z, r : r + n, :] = low(
                cdf + 0.5 * a * (1.0 - t * t) * (ROOT + 3.0 * ROOT * CUBE * sq)
            )
        acc[...] += mm_nt(hid[z], w[3, z])
        return carry

    lax.fori_loop(0, parts, feed_step, 0)
    save(hid, hid_out)
    save(slope, slope_out)
    result_ref[...] = low(acc[...])
    for copy in saves:
        copy.wait()


def backward_kernel(
    x_ref,
    xa_ref,
    cot_ref,
    gains_ref,
    onehot_ref,
    enc_hbm,
    w_hbm,
    n1_hbm,
    q1_hbm,
    kv1_hbm,
    p1_hbm,
    o1_hbm,
    l1_hbm,
    x1_hbm,
    n2_hbm,
    q2_hbm,
    kv2_hbm,
    p2_hbm,
    o2_hbm,
    l2_hbm,
    x2_hbm,
    n3_hbm,
    hid_hbm,
    slope_hbm,
    dx_ref,
    dxa_ref,
    denc_ref,
    small_ref,
    table_ref,
    g_hbm,
    w,
    enc,
    n1,
    q1,
    kv1,
    p1,
    o1,
    l1,
    n2,
    q2,
    kv2,
    p2,
    o2,
    l2,
    x2,
    n3,
    hid,
    slope,
    g_buf,
    rows_t,
    rows_t2,
    keys_t,
    dp_buf,
    ds_buf,
    dkv_t,
    dn,
    acc,
    enc_acc,
    diag_acc,
    w_sem,
    in_sem,
    p_sem,
    g_sem,
):
    rows = x_ref.shape[0]
    parts = w.shape[0]

    order = [(3, 2), (1,), (0,)]
    seq = [g for gs in order for g in gs]

    def fetch(slot, g, z):
        return pltpu.make_async_copy(w_hbm.at[g, z], w.at[z, slot], w_sem.at[z, slot])

    loads = {}
    names = [
        (n3_hbm, n3), (hid_hbm, hid), (slope_hbm, slope), (x2_hbm, x2),
        (o2_hbm, o2), (l2_hbm, l2), (q2_hbm, q2), (kv2_hbm, kv2),
        (n2_hbm, n2), (enc_hbm, enc),
        (o1_hbm, o1), (l1_hbm, l1), (q1_hbm, q1), (kv1_hbm, kv1), (n1_hbm, n1),
    ]

    for z in range(parts):
        fetch(0, 3, z).start()
        fetch(1, 2, z).start()
    for k, (src, dst) in enumerate(names):
        loads[id(dst)] = pltpu.make_async_copy(src, dst, in_sem.at[k])
        loads[id(dst)].start()

    def need(*refs):
        for ref in refs:
            loads[id(ref)].wait()

    def fetch_p(src, dst, k, z):
        slot = lax.rem(z, 2)
        return pltpu.make_async_copy(src.at[pl.ds(3 * z, 3)], dst.at[slot], p_sem.at[k, slot])

    def turn_p(src, dst, k, z):
        fetch_p(src, dst, k, z).wait()

        @pl.when(z + 1 < parts)
        def _():
            fetch_p(src, dst, k, z + 1).start()

    fetch_p(p2_hbm, p2, 0, 0).start()
    fetch_p(p1_hbm, p1, 1, 0).start()

    def store(slot, g, z):
        return pltpu.make_async_copy(g_buf.at[slot], g_hbm.at[g, z], g_sem.at[slot])

    e3 = cot_ref[...]
    rows_t[...] = flip(e3)
    need(n3, hid, slope)
    rows_t2[...] = flip(n3[...])
    acc[...] = jnp.zeros_like(acc)

    def feed_step(z, carry):
        fetch(0, 3, z).wait()
        fetch(1, 2, z).wait()
        dh = low(mm(cot_ref[...], w[z, 0]))
        da = low(dh.astype(F32) * slope[z].astype(F32))
        hid_z = hid[z]
        slope[z] = da
        acc[...] += mm_nt(slope[z], w[z, 1])

        @pl.when(z > 0)
        def _():
            store(0, 3, z - 1).wait()
            store(1, 2, z - 1).wait()

        g_buf[0] = low(mm(rows_t[...], hid_z))
        store(0, 3, z).start()
        g_buf[1] = low(mm(rows_t2[...], slope[z]))
        store(1, 2, z).start()
        fetch(0, 1, z).start()
        fetch(1, 0, z).start()
        return carry

    lax.fori_loop(0, parts, feed_step, 0)
    store(0, 3, parts - 1).wait()
    store(1, 2, parts - 1).wait()
    need(x2)
    back, gain3 = norm_back(acc[...], x2[...], gains_ref[2:3, :])
    x1_copy = pltpu.make_async_copy(x1_hbm, x2, in_sem.at[len(names)])
    gx = cot_ref[...].astype(F32) + back
    dn[...] = gx
    x1_copy.start()
    small_ref[2:3, :] = gain3

    def heads_back(z, do, q, kv, p, o, l, keys, with_diag):
        do_all = []
        delta_all = []
        for j in range(3):
            do_h = do[:, DH * j : DH * (j + 1)]
            inv = 1.0 / l[z, :, 32 * j : 32 * j + 1]
            o_h = o[z, :, DH * j : DH * (j + 1)].astype(F32)
            delta_all.append(jnp.sum(do_h * o_h * inv, axis=1, keepdims=True))
            do_all.append(do_h * inv)
        do_z = jnp.concatenate(do_all, axis=1)
        do_t = low(jnp.transpose(do_z))
        q_t = flip(q[z])
        dq = []
        for j in range(3):
            h = z * 3 + j
            p_h = p.at[lax.rem(z, 2), j]
            k_h = kv[z, :, DH * j : DH * (j + 1)]
            v_h = kv[z, :, DH * (3 + j) : DH * (4 + j)]
            dp_buf[j % 2, :, 0:keys] = mm_nt(low(do_all[j]), v_h)
            total = None
            for r, n in chunks(rows, 32):
                ds = low(
                    p_h[r : r + n, :].astype(F32)
                    * (dp_buf[j % 2, r : r + n, 0:keys] - delta_all[j][r : r + n, :])
                )
                ds_buf[j % 2, r : r + n, 0:keys] = ds
                if with_diag:
                    width = diag_acc.shape[2]
                    wide = jnp.concatenate(
                        [ds.astype(F32), jnp.zeros((n, width - keys), F32)], axis=1
                    )
                    for b in range(0, n, 8):
                        turned = pltpu.roll(wide[b : b + 8, :], (width - r - b) % width, 1)
                        total = turned if total is None else total + turned
            if with_diag:
                diag_acc[h] = total
            ds_h = ds_buf[j % 2, :, 0:keys]
            dq.append(low(mm(ds_h, k_h)))
            dkv_t[DH * j : DH * (j + 1), 0:keys] = mm(q_t[DH * j : DH * (j + 1), :], ds_h)
            dkv_t[DH * (3 + j) : DH * (4 + j), 0:keys] = mm(do_t[DH * j : DH * (j + 1), :], p_h[...])
        dkv = low(jnp.transpose(dkv_t[:, 0:keys]))
        return jnp.concatenate(dq, axis=1), dkv

    e2 = low(dn[...])
    rows_t[...] = flip(e2)
    need(o2, l2, q2, kv2, n2, enc)
    rows_t2[...] = flip(n2[...])
    keys_t[...] = flip(enc[...])
    keys = enc.shape[0]
    acc[...] = jnp.zeros_like(acc)
    enc_acc[...] = jnp.zeros_like(enc_acc)

    def cross_step(z, carry):
        fetch(0, 1, z).wait()
        turn_p(p2_hbm, p2, 0, z)
        do = low(mm(low(dn[...]), w[z, 0, :, 576:768])).astype(F32)
        dq, dkv = heads_back(z, do, q2, kv2, p2, o2, l2, keys, False)

        @pl.when(z > 0)
        def _():
            store(0, 1, z - 1).wait()

        g_buf[0, :, 0:384] = low(mm(keys_t[...], dkv))
        g_buf[0, :, 384:768] = jnp.concatenate(
            [low(mm(rows_t2[...], dq)), low(mm(rows_t[...], o2[z]))], axis=1
        )
        store(0, 1, z).start()
        acc[...] += mm_nt(dq, w[z, 0, :, 384:576])
        enc_acc[...] += mm_nt(dkv, w[z, 0, :, 0:384])
        return carry

    lax.fori_loop(0, parts, cross_step, 0)
    store(0, 1, parts - 1).wait()
    denc_ref[...] = low(enc_acc[...])
    x1_copy.wait()
    back, gain2 = norm_back(acc[...], x2[...], gains_ref[1:2, :])
    dn[...] += back
    small_ref[1:2, :] = gain2

    rows_t[...] = flip(low(dn[...]))
    need(o1, l1, q1, kv1, n1)
    rows_t2[...] = flip(n1[rows : 2 * rows, :])
    keys_t[:, 0 : 2 * rows] = flip(n1[...])
    acc[...] = jnp.zeros_like(acc)
    enc_acc[0 : 2 * rows, :] = jnp.zeros((2 * rows, enc_acc.shape[1]), F32)

    def self_step(z, carry):
        fetch(1, 0, z).wait()
        turn_p(p1_hbm, p1, 1, z)
        do = low(mm(low(dn[...]), w[z, 1, :, 576:768])).astype(F32)
        dq, dkv = heads_back(z, do, q1, kv1, p1, o1, l1, 2 * rows, True)

        @pl.when(z > 0)
        def _():
            store(0, 0, z - 1).wait()

        g_buf[0, :, 0:384] = low(mm(keys_t[:, 0 : 2 * rows], dkv))
        g_buf[0, :, 384:768] = jnp.concatenate(
            [low(mm(rows_t2[...], dq)), low(mm(rows_t[...], o1[z]))], axis=1
        )
        store(0, 0, z).start()
        acc[...] += mm_nt(dq, w[z, 1, :, 384:576])
        enc_acc[0 : 2 * rows, :] += mm_nt(dkv, w[z, 1, :, 0:384])
        return carry

    lax.fori_loop(0, parts, self_step, 0)
    store(0, 0, parts - 1).wait()
    gain = gains_ref[0:1, :]
    back, gain1 = norm_back(
        acc[...] + enc_acc[rows : 2 * rows, :], x_ref[...].astype(F32), gain
    )
    dx_ref[...] = dn[...] + back
    back, gain1a = norm_back(enc_acc[0:rows, :], xa_ref[...].astype(F32), gain)
    dxa_ref[...] = low(back)
    small_ref[0:1, :] = gain1 + gain1a
    small_ref[3:8, :] = jnp.zeros((5, small_ref.shape[1]), F32)
    width = diag_acc.shape[2]
    lines = []
    for h in range(diag_acc.shape[0]):
        block = diag_acc[h]
        line = block[0:1, :]
        for b in range(1, 8):
            line = line + pltpu.roll(block[b : b + 1, :], width - b, 1)
        lines.append(line)
    lines.append(jnp.zeros((16 - len(lines), width), F32))
    table_ref[...] = jnp.dot(
        jnp.concatenate(lines, axis=0), onehot_ref[...], precision=lax.Precision.HIGHEST, preferred_element_type=F32
    )


def body(
    inputs, encoded, cotangent, lengths, buckets,
    self_gain, self_query, self_key, self_value, self_output, bias_table,
    cross_gain, cross_query, cross_key, cross_value, cross_output,
    feed_gain, feed_inner, feed_output_weight,
):
    rows, width = inputs.shape
    parts = lax.axis_size("mp")
    n_dp = lax.axis_size("dp")
    halves = parts // lengths.shape[0]
    assert halves == 2 and buckets.shape[0] == 2 * rows and parts == 4
    z = lax.axis_index("mp")
    enc_rows = encoded.shape[0]
    vmem = pl.BlockSpec(memory_space=pltpu.VMEM)
    smem = pl.BlockSpec(memory_space=pltpu.SMEM)
    hbm = pl.BlockSpec(memory_space=pl.ANY)
    sds = jax.ShapeDtypeStruct

    packed = jnp.stack(
        [
            jnp.concatenate([self_key, self_value, self_query, self_output.T], axis=1),
            jnp.concatenate([cross_key, cross_value, cross_query, cross_output.T], axis=1),
            feed_inner,
            feed_output_weight.T,
        ]
    )
    share = width // n_dp
    piece = lax.dynamic_slice_in_dim(packed, lax.axis_index("dp") * share, share, 1)
    gathered = lax.all_gather(piece, ("dp", "mp"), axis=0, tiled=False)
    weights = jnp.transpose(
        gathered.reshape(n_dp, parts, 4, share, width), (2, 1, 0, 3, 4)
    ).reshape(4, parts, width, width)
    table = jnp.transpose(lax.all_gather(bias_table, "mp", axis=1, tiled=True))
    swap = [(s, s ^ 1) for s in range(parts)]
    both = lax.ppermute(encoded, "mp", swap)
    other = lax.ppermute(inputs, "mp", swap)
    half = lax.rem(z, 2)
    enc_all = jnp.where(
        half == 0,
        jnp.concatenate([encoded, both], axis=0),
        jnp.concatenate([both, encoded], axis=0),
    )
    length = lax.dynamic_slice_in_dim(lengths, z // 2, 1)
    gains = jnp.concatenate(
        [jnp.stack([self_gain, cross_gain, feed_gain]), jnp.zeros((5, width), F32)]
    )
    diag = 1024
    line = jnp.concatenate(
        [
            buckets[0 : rows + 1][::-1],
            jnp.full((diag - 2 * rows,), -1, jnp.int32),
            buckets[rows + 1 :][::-1],
        ]
    )
    onehot = (line[:, None] == lax.iota(jnp.int32, 128)[None, :]).astype(F32)
    heads = table.shape[0]
    table_pad = jnp.pad(table, ((0, 16 - heads), (0, 128 - table.shape[1])))
    diag_rows = lax.dot_general(
        table_pad, onehot, (((1,), (1,)), ((), ())), precision=lax.Precision.HIGHEST
    )

    keys = enc_all.shape[0]
    saved = [
        ((2 * rows, width), BF16),
        ((parts, rows, 192), BF16),
        ((parts, 2 * rows, 384), BF16),
        ((heads, rows, 2 * rows), BF16),
        ((parts, rows, 192), BF16),
        ((parts, rows, 128), F32),
        ((rows, width), F32),
        ((rows, width), BF16),
        ((parts, rows, 192), BF16),
        ((parts, keys, 384), BF16),
        ((heads, rows, keys), BF16),
        ((parts, rows, 192), BF16),
        ((parts, rows, 128), F32),
        ((rows, width), F32),
        ((rows, width), BF16),
        ((parts, rows, width), BF16),
        ((parts, rows, width), BF16),
    ]
    n1s, q1s, kv1s, p1s, o1s, l1s, x1s, n2s, q2s, kv2s, p2s, o2s, l2s, x2s, n3s, hids, slopes = [
        pltpu.VMEM(*s) for s in saved
    ]
    result, *kept = pl.pallas_call(
        functools.partial(forward_kernel, halves),
        out_shape=[sds((rows, width), BF16)] + [sds(*s) for s in saved],
        in_specs=[smem, vmem, vmem, hbm, vmem, vmem, hbm],
        out_specs=[vmem] + [hbm] * len(saved),
        scratch_shapes=[
            pltpu.VMEM((4, parts, width, width), BF16),
            pltpu.VMEM((keys, width), BF16),
            pltpu.VMEM((rows, 2 * rows), F32),
            pltpu.VMEM((3, rows, keys), F32),
            n1s, q1s, kv1s, p1s, o1s, x1s, n2s, q2s, kv2s, p2s, o2s, x2s, n3s, hids, slopes,
            l1s, l2s,
            pltpu.VMEM((rows, width), F32),
            pltpu.SemaphoreType.DMA((4, parts)),
            pltpu.SemaphoreType.DMA,
            pltpu.SemaphoreType.DMA((len(saved),)),
        ],
        compiler_params=pltpu.CompilerParams(vmem_limit_bytes=VMEM_BYTES),
        name="forward",
    )(length, inputs, other, enc_all, gains, diag_rows, weights)

    dx, dxa, denc, small, table_grad, grads = pl.pallas_call(
        backward_kernel,
        out_shape=[
            sds((rows, width), F32),
            sds((rows, width), BF16),
            sds((keys, width), BF16),
            sds((8, width), F32),
            sds((16, 128), F32),
            sds((4, parts, width, width), BF16),
        ],
        in_specs=[vmem, vmem, vmem, vmem, vmem] + [hbm] * 19,
        out_specs=[vmem] * 5 + [hbm],
        scratch_shapes=[
            pltpu.VMEM((parts, 2, width, width), BF16),
            pltpu.VMEM((keys, width), BF16),
            n1s, q1s, kv1s, pltpu.VMEM((2, 3, rows, 2 * rows), BF16), o1s, l1s, n2s, q2s, kv2s, pltpu.VMEM((2, 3, rows, keys), BF16), o2s, l2s, x2s, n3s,
            hids, slopes,
            pltpu.VMEM((2, width, width), BF16),
            pltpu.VMEM((width, rows), BF16),
            pltpu.VMEM((width, rows), BF16),
            pltpu.VMEM((width, keys), BF16),
            pltpu.VMEM((2, rows, keys), F32),
            pltpu.VMEM((2, rows, keys), BF16),
            pltpu.VMEM((384, keys), F32),
            pltpu.VMEM((rows, width), F32),
            pltpu.VMEM((rows, width), F32),
            pltpu.VMEM((keys, width), F32),
            pltpu.VMEM((heads, 8, diag), F32),
            pltpu.SemaphoreType.DMA((parts, 2)),
            pltpu.SemaphoreType.DMA((18,)),
            pltpu.SemaphoreType.DMA((2, 2)),
            pltpu.SemaphoreType.DMA((2,)),
        ],
        compiler_params=pltpu.CompilerParams(vmem_limit_bytes=VMEM_BYTES),
        name="backward",
    )(inputs, other, cotangent, gains, onehot, enc_all, weights, *kept)

    input_grad = dx + lax.ppermute(dxa, "mp", swap).astype(F32)
    mine = lax.dynamic_slice_in_dim(denc, half * enc_rows, enc_rows)
    theirs = lax.dynamic_slice_in_dim(denc, (1 - half) * enc_rows, enc_rows)
    encoder_grad = mine.astype(F32) + lax.ppermute(theirs, "mp", swap).astype(F32)
    shares = jnp.transpose(
        grads.reshape(4, parts, n_dp, share, width), (2, 1, 0, 3, 4)
    ).reshape(n_dp * parts, 4 * share, width)
    summed = (
        lax.psum_scatter(shares, ("dp", "mp"), scatter_dimension=0, tiled=True)
        .astype(F32)
        .reshape(4, share, width)
    )
    small, table_grad = lax.psum((small, table_grad), ("dp", "mp"))
    table_mine = lax.dynamic_slice_in_dim(
        jnp.transpose(table_grad[0:heads, 0 : bias_table.shape[0]]), z * 3, 3, 1
    )
    gs, gc = summed[0], summed[1]
    return (
        result,
        low(input_grad),
        low(encoder_grad),
        small[0],
        gs[:, 384:576],
        gs[:, 0:192],
        gs[:, 192:384],
        gs[:, 576:768].T,
        table_mine,
        small[1],
        gc[:, 384:576],
        gc[:, 0:192],
        gc[:, 192:384],
        gc[:, 576:768].T,
        small[2],
        summed[2],
        summed[3].T,
    )


def solution(mesh):
    rows = P(("dp", "mp"), None)
    across, down = P(None, "mp"), P("mp", None)
    return jax.shard_map(
        body,
        mesh=mesh,
        in_specs=(
            rows, rows, rows, P("dp"), P(),
            P(), across, across, across, down, across,
            P(), across, across, across, down,
            P(), across, down,
        ),
        out_specs=(
            rows, rows, rows,
            P(), P("dp", "mp"), P("dp", "mp"), P("dp", "mp"), P("mp", "dp"), P(None, "mp"),
            P(), P("dp", "mp"), P("dp", "mp"), P("dp", "mp"), P("mp", "dp"),
            P(), P("dp", "mp"), P("mp", "dp"),
        ),
        check_vma=False,
    )
```

```python
import functools

import jax
import jax.numpy as jnp
from jax import lax
from jax.experimental import pallas as pl
from jax.experimental.pallas import tpu as pltpu
from jax.sharding import PartitionSpec as P

EPS = 1e-06
MASKED = -1e30
DH = 64
F32 = jnp.float32
BF16 = jnp.bfloat16
VMEM_BYTES = 62 << 20
ROOT = 0.7978845608028654
CUBE = 0.044715


def mm(a, b):
    return jnp.dot(a, b, preferred_element_type=F32)


def mm_nt(a, b):
    return lax.dot_general(a, b, (((1,), (1,)), ((), ())), preferred_element_type=F32)


def low(v):
    return v.astype(BF16)


def flip(v):
    return jnp.transpose(v.astype(F32)).astype(BF16)


def norm_rows(v, gain):
    root = lax.rsqrt(jnp.mean(v * v, axis=-1, keepdims=True) + EPS)
    unit = v * root
    return unit * gain, unit, root


def norm_back(grad, v, gain):
    _, unit, root = norm_rows(v, gain)
    scaled = grad * gain
    back = root * (scaled - unit * jnp.mean(scaled * unit, axis=-1, keepdims=True))
    return back, jnp.sum(grad * unit, axis=0, keepdims=True)


def block(w, i, j, start=0, stop=None):
    part = w[i, j, :, :, :, start:stop]
    return part.reshape(part.shape[0] * part.shape[1] * part.shape[2], part.shape[3])


def half_of_sequence(halves):
    return lax.rem(lax.axis_index("mp"), halves)


def chunks(rows, step):
    return [(r, min(step, rows - r)) for r in range(0, rows, step)]


MESH_ID = pl.DeviceIdType.MESH


def places():
    d = lax.axis_index("dp")
    z = lax.axis_index("mp")
    lo = lax.rem(d, 8)
    core = lax.rem(lo, 2)
    x = lax.rem(lax.div(lo, 2), 2)
    y = lax.div(lo, 4)
    d_core = d + 1 - 2 * core
    d_x = d + 2 - 4 * x
    d_y = d + 4 - 8 * y
    return d, z, core, x, y, d_core, d_x, d_y


def greet(z_parts):
    d, z, _, _, _, d_core, d_x, d_y = places()
    barrier = pltpu.get_barrier_semaphore()
    for who in (d_core, d_x, d_y):
        pl.semaphore_signal(barrier, inc=1, device_id=(who, z), device_id_type=MESH_ID)
    for step in range(1, z_parts):
        pl.semaphore_signal(
            barrier, inc=1, device_id=(d, lax.rem(z + step, z_parts)), device_id_type=MESH_ID
        )
    pl.semaphore_wait(barrier, 2 + z_parts)


def remote(src, dst, send, recv, who):
    return pltpu.make_async_remote_copy(
        src_ref=src, dst_ref=dst, send_sem=send, recv_sem=recv, device_id=who, device_id_type=MESH_ID
    )


class Gather:
    def __init__(self, packed, wg, z_send, z_recv, s_send, s_recv):
        self.packed, self.wg = packed, wg
        self.z_sems, self.s_sems = (z_send, z_recv), (s_send, s_recv)
        self.parts = wg.shape[1]
        self.place = places()

    def z_copy(self, g, step):
        d, z, core, x, y, *_ = self.place
        yx = 2 * y + x
        return remote(
            self.packed.at[g, yx, core],
            self.wg.at[g, self.parts - step, yx, core],
            self.z_sems[0].at[g, step - 1],
            self.z_sems[1].at[g, step - 1],
            (d, lax.rem(z + step, self.parts)),
        )

    def s_copy(self, g, k):
        d, z, core, x, y, d_core, d_x, d_y = self.place
        rest = pl.ds(1, self.parts - 1)
        share = self.wg.shape[4]
        first, second = pl.ds(0, share // 2), pl.ds(share // 2, share // 2)
        if k < 2:
            ref = self.wg.at[g, rest, 2 * y + x, core]
            who = (d_x, d_y)[k]
        elif k == 2:
            ref = self.wg.at[g, rest, 2 * y + 1 - x, core, first]
            who = d_y
        elif k == 3:
            ref = self.wg.at[g, rest, 2 * (1 - y) + x, core, second]
            who = d_x
        else:
            ref = self.wg.at[g, rest, :, core]
            who = d_core
        return remote(ref, ref, self.s_sems[0].at[g, k], self.s_sems[1].at[g, k], (who, z))

    def z_start(self, g):
        for step in range(1, self.parts):
            self.z_copy(g, step).start()

    def xy_start(self, g):
        for step in range(1, self.parts):
            self.z_copy(g, step).wait_recv()
        self.s_copy(g, 0).start()
        self.s_copy(g, 1).start()

    def corner_start(self, g):
        self.s_copy(g, 0).wait_recv()
        self.s_copy(g, 2).start()
        self.s_copy(g, 1).wait_recv()
        self.s_copy(g, 3).start()

    def core_start(self, g):
        self.s_copy(g, 2).wait_recv()
        self.s_copy(g, 3).wait_recv()
        self.s_copy(g, 4).start()

    def arrived(self, g):
        self.s_copy(g, 4).wait_recv()

    def sent(self):
        for g in range(4):
            for step in range(1, self.parts):
                self.z_copy(g, step).wait_send()
            for k in range(5):
                self.s_copy(g, k).wait_send()


def gather_kernel(
    packed, x_in, enc_in, table_in, wg, x_out, enc_out, table_out,
    z_send, z_recv, s_send, s_recv, e_send, e_recv,
):
    parts = wg.shape[1]
    d, z = places()[:2]
    mate = z + 1 - 2 * lax.rem(z, 2)
    greet(parts)
    gather = Gather(packed, wg, z_send, z_recv, s_send, s_recv)
    x_copy = remote(x_in, x_out, e_send.at[0], e_recv.at[0], (d, mate))
    enc_copy = remote(enc_in, enc_out, e_send.at[1], e_recv.at[1], (d, mate))
    tables = [
        remote(
            table_in, table_out.at[parts - step], e_send.at[1 + step], e_recv.at[1 + step],
            (d, lax.rem(z + step, parts)),
        )
        for step in range(1, parts)
    ]
    gather.z_start(0)
    for copy in tables:
        copy.start()
    x_copy.start()
    for t in range(7):
        if t >= 3:
            gather.arrived(t - 3)
        if 2 <= t < 6:
            gather.core_start(t - 2)
        if 1 <= t < 5:
            gather.corner_start(t - 1)
        if t < 4:
            gather.xy_start(t)
        if t < 3:
            gather.z_start(t + 1)
        if t == 0:
            enc_copy.start()
    for copy in tables + [x_copy, enc_copy]:
        copy.wait()
    gather.sent()


C_RING = 4
TICKS = 16


class Scatter:
    def __init__(self, bufs, sems, credit):
        (
            self.c_in, self.a_in, self.b_in, self.z_in,
            self.a_out, self.a_keep, self.b_out, self.b_keep, self.z_out, self.total,
        ) = bufs
        self.sems, self.credit = sems, credit
        self.parts = 4
        self.share = self.z_out.shape[1]
        self.place = places()

    def block(self, t):
        feed = 1 - lax.div(t, 8)
        r = feed * lax.div(t, 2) + (1 - feed) * lax.rem(t, 4)
        g = feed * (3 - lax.rem(t, 2)) + (1 - feed) * (3 - lax.div(t, 4))
        return g, r

    def copy(self, k, t, src, dst, who):
        return remote(src, dst, self.sems.at[0, k, t], self.sems.at[1, k, t], who)

    def c_copy(self, t, src):
        z, d_core = self.place[1], self.place[5]
        return self.copy(0, t, src, self.c_in.at[lax.rem(t, C_RING)], (d_core, z))

    def a_copy(self, t, q):
        _, z, *_, d_x, d_y = self.place
        src, dst = self.a_out.at[lax.rem(t, 2), q], self.a_in.at[t, q]
        return self.copy(1 + q, t, src, dst, ((d_x, d_y)[q], z))

    def b_copy(self, t, q):
        _, z, *_, d_x, d_y = self.place
        src, dst = self.b_out.at[lax.rem(t, 2), q], self.b_in.at[t, q]
        return self.copy(3 + q, t, src, dst, ((d_y, d_x)[q], z))

    def z_copy(self, t):
        d, z = self.place[:2]
        who = (d, lax.rem(z + self.block(t)[1], self.parts))
        return self.copy(5, t, self.z_out.at[lax.rem(t, 2)], self.z_in.at[t], who)

    def rows(self, q):
        return pl.ds(q * (self.share // 2), self.share // 2)

    def c_start(self, t, src):
        @pl.when(t >= C_RING)
        def _():
            pl.semaphore_wait(self.credit, 1)

        self.c_copy(t, src).start()

    def a_start(self, t, mine, src):
        _, z, _, x, y, d_core, *_ = self.place
        slot, ring = lax.rem(t, 2), lax.rem(t, C_RING)

        @pl.when(t >= 2)
        def _():
            self.a_copy(t - 2, 0).wait_send()
            self.a_copy(t - 2, 1).wait_send()

        self.c_copy(t, src).wait_recv()
        for q in range(2):
            rows = self.rows(q)
            for k in range(2):
                send = (2 * k + 1 - x, 2 * (1 - y) + k)[q]
                keep = (2 * k + x, 2 * y + k)[q]
                self.a_out[slot, q, k] = low(
                    mine[send, rows].astype(F32) + self.c_in[ring, send, rows].astype(F32)
                )
                self.a_keep[slot, q, k] = mine[keep, rows].astype(F32) + self.c_in[
                    ring, keep, rows
                ].astype(F32)
            self.a_copy(t, q).start()

        @pl.when(t < TICKS - C_RING)
        def _():
            pl.semaphore_signal(
                self.credit, inc=1, device_id=(d_core, z), device_id_type=MESH_ID
            )

    def b_start(self, t):
        _, _, _, x, y, *_ = self.place
        slot = lax.rem(t, 2)

        @pl.when(t >= 2)
        def _():
            self.b_copy(t - 2, 0).wait_send()
            self.b_copy(t - 2, 1).wait_send()

        for q in range(2):
            keep = (y, x)[q]
            send = 1 - keep
            self.a_copy(t, q).wait_recv()
            self.b_out[slot, q] = low(
                self.a_keep[slot, q, send] + self.a_in[t, q, send].astype(F32)
            )
            self.b_keep[slot, q] = self.a_keep[slot, q, keep] + self.a_in[t, q, keep].astype(F32)
            self.b_copy(t, q).start()

    def z_start(self, t):
        slot = lax.rem(t, 2)
        g, r = self.block(t)

        @pl.when((t >= 2) & (self.block(t - 2)[1] > 0))
        def _():
            self.z_copy(t - 2).wait_send()

        for q in range(2):
            self.b_copy(t, q).wait_recv()
            done = self.b_keep[slot, q] + self.b_in[t, q].astype(F32)

            @pl.when(r == 0)
            def _():
                self.total[g, self.rows(q)] = done

            @pl.when(r > 0)
            def _():
                self.z_out[slot, self.rows(q)] = low(done)

        @pl.when(r > 0)
        def _():
            self.z_copy(t).start()

    def step(self, t, mine, src):
        @pl.when((t >= 1) & (t < TICKS + 1))
        def _():
            self.a_start(t - 1, mine, src)

        @pl.when((t >= 2) & (t < TICKS + 2))
        def _():
            self.b_start(t - 2)

        @pl.when((t >= 3) & (t < TICKS + 3))
        def _():
            self.z_start(t - 3)

    def finish(self):
        def drain(t, carry):
            self.a_copy(t, 0).wait_send()
            self.a_copy(t, 1).wait_send()
            self.b_copy(t, 0).wait_send()
            self.b_copy(t, 1).wait_send()
            self.z_copy(t).wait_send()
            return carry

        lax.fori_loop(TICKS - 2, TICKS, drain, 0)

        def add(t, carry):
            g, r = self.block(t)

            @pl.when(r > 0)
            def _():
                self.z_copy(t).wait_recv()
                self.total[g] += self.z_in[t].astype(F32)

            return carry

        lax.fori_loop(0, TICKS, add, 0)


class Sum:
    def __init__(self, out, into, ring, send, recv):
        self.out, self.into, self.ring = out, into, ring
        self.send, self.recv = send, recv
        self.place = places()

    def pair(self, k):
        z, who = self.place[1], self.place[5 + k]
        return remote(
            self.out.at[k], self.into.at[k], self.send.at[k], self.recv.at[k], (who, z)
        )

    def along(self, step):
        d, z = self.place[:2]
        parts = self.ring.shape[0]
        return remote(
            self.ring.at[z], self.ring.at[z], self.send.at[2 + step], self.recv.at[2 + step],
            (d, lax.rem(z + step, parts)),
        )

    def start(self, value):
        self.out[0] = value
        self.pair(0).start()

    def turn(self, k):
        self.pair(k).wait()
        value = self.out[k] + self.into[k]
        if k < 2:
            self.out[k + 1] = value
            self.pair(k + 1).start()
            return
        self.ring[self.place[1]] = value
        for step in range(1, self.ring.shape[0]):
            self.along(step).start()

    def result(self):
        parts = self.ring.shape[0]
        z = self.place[1]
        for step in range(1, parts):
            self.along(step).wait_send()
            sender = lax.rem(z + parts - step, parts)
            remote(
                self.ring.at[sender], self.ring.at[sender],
                self.send.at[2 + step], self.recv.at[2 + step], (self.place[0], sender),
            ).wait_recv()
        value = self.ring[0]
        for k in range(1, parts):
            value = value + self.ring[k]
        return value


def scatter_kernel(
    g_hbm, small_ref, dx_ref, dxa_ref, denc_ref,
    total_out, small_out, dx_out, denc_out,
    g_buf, c_in, a_in, b_in, z_in, a_out, a_keep, b_out, b_keep, z_out,
    s_out, s_in, s_ring, dxa_in, denc_in,
    sems, credit, s_send, s_recv, e_send, e_recv, g_sem,
):
    parts = s_ring.shape[0]
    place = places()
    d, z, core = place[:3]
    half = lax.rem(z, 2)
    mate = z + 1 - 2 * half
    enc_rows = denc_out.shape[0]
    greet(parts)
    scatter = Scatter(
        (c_in, a_in, b_in, z_in, a_out, a_keep, b_out, b_keep, z_out, total_out), sems, credit
    )
    sums = Sum(s_out, s_in, s_ring, s_send, s_recv)
    dxa_copy = remote(dxa_ref, dxa_in, e_send.at[0], e_recv.at[0], (d, mate))
    denc_copy = remote(
        denc_ref.at[1 - half], denc_in, e_send.at[1], e_recv.at[1], (d, mate)
    )

    def load(t):
        slot = lax.rem(t, 2)
        return pltpu.make_async_copy(g_hbm.at[t, :, core], g_buf.at[slot], g_sem.at[slot])

    def tick(t, carry):
        @pl.when(t < TICKS)
        def _():
            scatter.c_start(t, g_hbm.at[t, :, 1 - core])

        @pl.when((t >= 1) & (t < TICKS + 1))
        def _():
            load(t - 1).wait()

        @pl.when(t < TICKS)
        def _():
            load(t).start()

        scatter.step(t, g_buf.at[lax.rem(t + 1, 2)], g_hbm.at[lax.rem(t + 15, 16), :, 1 - core])

        @pl.when(t == 4)
        def _():
            denc_copy.start()
            dxa_copy.start()
            sums.start(small_ref[...])

        for k in range(3):

            @pl.when(t == 6 + k)
            def _():
                sums.turn(k)

        return carry

    lax.fori_loop(0, TICKS + 3, tick, 0)
    scatter.finish()
    small_out[...] = sums.result()
    denc_copy.wait()
    dxa_copy.wait()
    denc_out[...] = low(denc_ref[half].astype(F32) + denc_in[...].astype(F32))
    dx_out[...] = low(dx_ref[...] + dxa_in[...].astype(F32))

    def drain(t, carry):
        scatter.c_copy(t, g_hbm.at[t, :, 1 - core]).wait_send()
        return carry

    lax.fori_loop(0, TICKS, drain, 0)


def forward_kernel(
    halves,
    len_ref,
    x_ref,
    xa_ref,
    enc_own,
    enc_other,
    gains_ref,
    table_own,
    table_ref,
    onehot_ref,
    packed,
    w_hbm,
    result_ref,
    n1_out,
    q1_out,
    kv1_out,
    p1_out,
    o1_out,
    l1_out,
    x1_out,
    n2_out,
    q2_out,
    kv2_out,
    p2_out,
    o2_out,
    l2_out,
    x2_out,
    n3_out,
    hid_out,
    slope_out,
    w,
    enc,
    diag,
    mask,
    s_buf,
    n1,
    q1,
    kv1,
    p1,
    o1,
    x1,
    n2,
    q2,
    kv2,
    p2,
    o2,
    x2,
    n3,
    hid,
    slope,
    l1,
    l2,
    acc,
    w_sem,
    enc_sem,
    out_sem,
):
    rows = x_ref.shape[0]
    parts = w.shape[1]
    half = half_of_sequence(halves)

    def fetch(g, r, src=w_hbm):
        src = packed.at[g] if src is packed else src.at[g, r]
        return pltpu.make_async_copy(src, w.at[g, r], w_sem.at[g, r])

    enc_copies = [
        pltpu.make_async_copy(enc_own, enc.at[half], enc_sem.at[0]),
        pltpu.make_async_copy(enc_other, enc.at[1 - half], enc_sem.at[1]),
    ]
    for g in range(4):
        fetch(g, 0, packed).start()
        for r in range(1, parts):
            fetch(g, r).start()
        if g == 0:
            for copy in enc_copies:
                copy.start()
    for r in range(parts):
        lines = table_own[...] if r == 0 else table_ref[r]
        diag[r] = jnp.dot(
            lines, onehot_ref[...], precision=lax.Precision.HIGHEST, preferred_element_type=F32
        )

    saves = []

    def save(src, dst):
        copy = pltpu.make_async_copy(src, dst, out_sem.at[len(saves)])
        copy.start()
        saves.append(copy)

    n1[0:rows, :] = low(norm_rows(xa_ref[...].astype(F32), gains_ref[0:1, :])[0])
    n1[rows : 2 * rows, :] = low(norm_rows(x_ref[...].astype(F32), gains_ref[0:1, :])[0])
    save(n1, n1_out)

    length = len_ref[0]
    i = lax.broadcasted_iota(jnp.int32, mask.shape, 0)
    c = lax.broadcasted_iota(jnp.int32, mask.shape, 1)
    own = c - rows
    limit = jnp.where(half > 0, length, 0)
    ok = ((own < 0) & (c < limit)) | ((own >= 0) & (own <= i) & (own + half * rows < length))
    mask[...] = jnp.where(ok, 0.0, MASKED)

    def heads(z, q, kv, p, o, l, keys, with_bias):
        outs = []
        for j in range(3):
            h = z * 3 + j
            q_h = q[z, :, DH * j : DH * (j + 1)]
            k_h = kv[z, :, DH * j : DH * (j + 1)]
            v_h = kv[z, :, DH * (3 + j) : DH * (4 + j)]
            s_buf[j, :, 0:keys] = mm_nt(q_h, k_h)
            for r, n in chunks(rows, 32):
                s = s_buf[j, r : r + n, 0:keys]
                if with_bias:
                    line = jnp.broadcast_to(diag[z, j : j + 1, :], (n, diag.shape[2]))
                    grid = pltpu.roll(line, r, 1, stride=1, stride_axis=0)
                    s = s + grid[:, 0:keys] + mask[r : r + n, :]
                top = jnp.max(s, axis=1, keepdims=True)
                p[h, r : r + n, :] = low(jnp.exp(s - top))
            wide = jnp.concatenate([v_h, jnp.ones_like(v_h)], axis=1)
            mixed = mm(p[h], wide)
            outs.append(low(mixed[:, 0:DH] / mixed[:, DH : 2 * DH]))
            l[z, :, 32 * j : 32 * (j + 1)] = mixed[:, DH : DH + 32]
        o[z] = jnp.concatenate(outs, axis=1)

    acc[...] = x_ref[...].astype(F32)

    def self_step(z, carry):
        fetch(0, z).wait()
        kv1[z] = low(mm(n1[...], block(w, 0, z, 0, 384)))
        q1[z] = low(mm(n1[rows : 2 * rows, :], block(w, 0, z, 384, 576)))
        heads(z, q1, kv1, p1, o1, l1, 2 * rows, True)
        acc[...] += mm_nt(o1[z], block(w, 0, z, 576, 768))
        return carry

    lax.fori_loop(0, parts, self_step, 0)
    for src, dst in ((q1, q1_out), (kv1, kv1_out), (p1, p1_out), (o1, o1_out), (l1, l1_out)):
        save(src, dst)
    x1[...] = acc[...]
    n2[...] = low(norm_rows(acc[...], gains_ref[1:2, :])[0])
    save(x1, x1_out)
    save(n2, n2_out)
    for copy in enc_copies:
        copy.wait()
    keys = 2 * enc.shape[1]

    def cross_step(z, carry):
        fetch(1, z).wait()
        kv2[z] = low(mm(enc[...].reshape(keys, enc.shape[2]), block(w, 1, z, 0, 384)))
        q2[z] = low(mm(n2[...], block(w, 1, z, 384, 576)))
        heads(z, q2, kv2, p2, o2, l2, keys, False)
        acc[...] += mm_nt(o2[z], block(w, 1, z, 576, 768))
        return carry

    lax.fori_loop(0, parts, cross_step, 0)
    for src, dst in ((q2, q2_out), (kv2, kv2_out), (p2, p2_out), (o2, o2_out), (l2, l2_out)):
        save(src, dst)
    x2[...] = acc[...]
    n3[...] = low(norm_rows(acc[...], gains_ref[2:3, :])[0])
    save(x2, x2_out)
    save(n3, n3_out)

    def feed_step(z, carry):
        fetch(2, z).wait()
        fetch(3, z).wait()
        for r, n in chunks(rows, 64):
            a = mm(n3[r : r + n, :], block(w, 2, z))
            sq = a * a
            t = jnp.tanh(a * (ROOT + ROOT * CUBE * sq))
            cdf = 0.5 + 0.5 * t
            hid[z, r : r + n, :] = low(a * cdf)
            slope[z, r : r + n, :] = low(
                cdf + 0.5 * a * (1.0 - t * t) * (ROOT + 3.0 * ROOT * CUBE * sq)
            )
        acc[...] += mm_nt(hid[z], block(w, 3, z))
        return carry

    lax.fori_loop(0, parts, feed_step, 0)
    save(hid, hid_out)
    save(slope, slope_out)
    result_ref[...] = low(acc[...])
    for copy in saves:
        copy.wait()


def backward_kernel(
    x_ref,
    xa_ref,
    cot_ref,
    gains_ref,
    onehot_ref,
    enc_own,
    enc_other,
    packed,
    w_hbm,
    n1_hbm,
    q1_hbm,
    kv1_hbm,
    p1_hbm,
    o1_hbm,
    l1_hbm,
    x1_hbm,
    n2_hbm,
    q2_hbm,
    kv2_hbm,
    p2_hbm,
    o2_hbm,
    l2_hbm,
    x2_hbm,
    n3_hbm,
    hid_hbm,
    slope_hbm,
    dx_ref,
    dxa_ref,
    denc_ref,
    small_ref,
    g_hbm,
    w,
    enc,
    n1,
    q1,
    kv1,
    p1,
    o1,
    l1,
    n2,
    q2,
    kv2,
    p2,
    o2,
    l2,
    x2,
    n3,
    hid,
    slope,
    g_buf,
    rows_t,
    rows_t2,
    keys_t,
    dp_buf,
    ds_buf,
    dkv_t,
    dn,
    acc,
    enc_acc,
    diag_acc,
    w_sem,
    in_sem,
    p_sem,
    g_sem,
):
    rows, width_all = x_ref.shape
    parts = w.shape[0]

    order = [(3, 2), (1,), (0,)]
    seq = [g for gs in order for g in gs]

    half = lax.rem(lax.axis_index("mp"), 2)

    def fetch(slot, g, z, src=w_hbm):
        src = packed.at[g] if src is packed else src.at[g, z]
        return pltpu.make_async_copy(src, w.at[z, slot], w_sem.at[z, slot])

    def refetch(slot, g, z):
        @pl.when(z == 0)
        def _():
            fetch(slot, g, z, packed).start()

        @pl.when(z > 0)
        def _():
            fetch(slot, g, z).start()

    loads = {}
    names = [
        (n3_hbm, n3), (hid_hbm, hid), (slope_hbm, slope), (x2_hbm, x2),
        (o2_hbm, o2), (l2_hbm, l2), (q2_hbm, q2), (kv2_hbm, kv2),
        (n2_hbm, n2), (enc_own, enc.at[half]), (enc_other, enc.at[1 - half]),
        (o1_hbm, o1), (l1_hbm, l1), (q1_hbm, q1), (kv1_hbm, kv1), (n1_hbm, n1),
    ]

    for z in range(parts):
        fetch(0, 3, z, packed if z == 0 else w_hbm).start()
        fetch(1, 2, z, packed if z == 0 else w_hbm).start()
    for k, (src, dst) in enumerate(names):
        loads[id(src)] = pltpu.make_async_copy(src, dst, in_sem.at[k])
        loads[id(src)].start()

    def need(*refs):
        for ref in refs:
            loads[id(ref)].wait()

    def fetch_p(src, dst, k, z):
        slot = lax.rem(z, 2)
        return pltpu.make_async_copy(src.at[pl.ds(3 * z, 3)], dst.at[slot], p_sem.at[k, slot])

    def turn_p(src, dst, k, z):
        fetch_p(src, dst, k, z).wait()

        @pl.when(z + 1 < parts)
        def _():
            fetch_p(src, dst, k, z + 1).start()

    fetch_p(p2_hbm, p2, 0, 0).start()
    fetch_p(p1_hbm, p1, 1, 0).start()

    def store(slot, g, z):
        t = 2 * z + (3 - g) if g >= 2 else 12 - 4 * g + z
        return pltpu.make_async_copy(g_buf.at[slot], g_hbm.at[t], g_sem.at[slot])

    def put(slot, value, start=0):
        shape = g_buf.shape[1:4] + (value.shape[1],)
        g_buf[slot, :, :, :, start : start + value.shape[1]] = value.reshape(shape)

    e3 = cot_ref[...]
    rows_t[...] = flip(e3)
    need(n3_hbm, hid_hbm, slope_hbm)
    rows_t2[...] = flip(n3[...])
    acc[...] = jnp.zeros_like(acc)

    def feed_step(z, carry):
        fetch(0, 3, z).wait()
        fetch(1, 2, z).wait()
        dh = low(mm(cot_ref[...], block(w, z, 0)))
        da = low(dh.astype(F32) * slope[z].astype(F32))
        hid_z = hid[z]
        slope[z] = da
        acc[...] += mm_nt(slope[z], block(w, z, 1))

        @pl.when(z > 0)
        def _():
            store(0, 3, z - 1).wait()
            store(1, 2, z - 1).wait()

        put(0, low(mm(rows_t[...], hid_z)))
        store(0, 3, z).start()
        put(1, low(mm(rows_t2[...], slope[z])))
        store(1, 2, z).start()
        refetch(0, 1, z)
        refetch(1, 0, z)
        return carry

    lax.fori_loop(0, parts, feed_step, 0)
    store(0, 3, parts - 1).wait()
    store(1, 2, parts - 1).wait()
    need(x2_hbm)
    back, gain3 = norm_back(acc[...], x2[...], gains_ref[2:3, :])
    x1_copy = pltpu.make_async_copy(x1_hbm, x2, in_sem.at[len(names)])
    gx = cot_ref[...].astype(F32) + back
    dn[...] = gx
    x1_copy.start()
    small_ref[...] = jnp.zeros_like(small_ref)
    small_ref[2:3, 0:width_all] = gain3

    def heads_back(z, do, q, kv, p, o, l, keys, with_diag):
        do_all = []
        delta_all = []
        for j in range(3):
            do_h = do[:, DH * j : DH * (j + 1)]
            inv = 1.0 / l[z, :, 32 * j : 32 * j + 1]
            o_h = o[z, :, DH * j : DH * (j + 1)].astype(F32)
            delta_all.append(jnp.sum(do_h * o_h * inv, axis=1, keepdims=True))
            do_all.append(do_h * inv)
        do_z = jnp.concatenate(do_all, axis=1)
        do_t = low(jnp.transpose(do_z))
        q_t = flip(q[z])
        dq = []
        for j in range(3):
            h = z * 3 + j
            p_h = p.at[lax.rem(z, 2), j]
            k_h = kv[z, :, DH * j : DH * (j + 1)]
            v_h = kv[z, :, DH * (3 + j) : DH * (4 + j)]
            dp_buf[j % 2, :, 0:keys] = mm_nt(low(do_all[j]), v_h)
            total = None
            for r, n in chunks(rows, 32):
                ds = low(
                    p_h[r : r + n, :].astype(F32)
                    * (dp_buf[j % 2, r : r + n, 0:keys] - delta_all[j][r : r + n, :])
                )
                ds_buf[j % 2, r : r + n, 0:keys] = ds
                if with_diag:
                    width = diag_acc.shape[2]
                    wide = jnp.concatenate(
                        [ds.astype(F32), jnp.zeros((n, width - keys), F32)], axis=1
                    )
                    for b in range(0, n, 8):
                        turned = pltpu.roll(wide[b : b + 8, :], (width - r - b) % width, 1)
                        total = turned if total is None else total + turned
            if with_diag:
                diag_acc[h] = total
            ds_h = ds_buf[j % 2, :, 0:keys]
            dq.append(low(mm(ds_h, k_h)))
            dkv_t[DH * j : DH * (j + 1), 0:keys] = mm(q_t[DH * j : DH * (j + 1), :], ds_h)
            dkv_t[DH * (3 + j) : DH * (4 + j), 0:keys] = mm(do_t[DH * j : DH * (j + 1), :], p_h[...])
        dkv = low(jnp.transpose(dkv_t[:, 0:keys]))
        return jnp.concatenate(dq, axis=1), dkv

    e2 = low(dn[...])
    rows_t[...] = flip(e2)
    need(o2_hbm, l2_hbm, q2_hbm, kv2_hbm, n2_hbm, enc_own, enc_other)
    rows_t2[...] = flip(n2[...])
    keys = 2 * enc.shape[1]
    keys_t[...] = flip(enc[...].reshape(keys, enc.shape[2]))
    acc[...] = jnp.zeros_like(acc)
    enc_acc[...] = jnp.zeros_like(enc_acc)

    def cross_step(z, carry):
        fetch(0, 1, z).wait()
        turn_p(p2_hbm, p2, 0, z)
        do = low(mm(low(dn[...]), block(w, z, 0, 576, 768))).astype(F32)
        dq, dkv = heads_back(z, do, q2, kv2, p2, o2, l2, keys, False)

        @pl.when(z > 0)
        def _():
            store(0, 1, z - 1).wait()

        put(0, low(mm(keys_t[...], dkv)))
        put(
            0,
            jnp.concatenate(
                [low(mm(rows_t2[...], dq)), low(mm(rows_t[...], o2[z]))], axis=1
            ),
            384,
        )
        store(0, 1, z).start()
        acc[...] += mm_nt(dq, block(w, z, 0, 384, 576))
        enc_acc[...] += mm_nt(dkv, block(w, z, 0, 0, 384))
        return carry

    lax.fori_loop(0, parts, cross_step, 0)
    store(0, 1, parts - 1).wait()
    denc_ref[...] = low(enc_acc[...]).reshape(denc_ref.shape)
    x1_copy.wait()
    back, gain2 = norm_back(acc[...], x2[...], gains_ref[1:2, :])
    dn[...] += back
    small_ref[1:2, 0:width_all] = gain2

    rows_t[...] = flip(low(dn[...]))
    need(o1_hbm, l1_hbm, q1_hbm, kv1_hbm, n1_hbm)
    rows_t2[...] = flip(n1[rows : 2 * rows, :])
    keys_t[:, 0 : 2 * rows] = flip(n1[...])
    acc[...] = jnp.zeros_like(acc)
    enc_acc[0 : 2 * rows, :] = jnp.zeros((2 * rows, enc_acc.shape[1]), F32)

    def self_step(z, carry):
        fetch(1, 0, z).wait()
        turn_p(p1_hbm, p1, 1, z)
        do = low(mm(low(dn[...]), block(w, z, 1, 576, 768))).astype(F32)
        dq, dkv = heads_back(z, do, q1, kv1, p1, o1, l1, 2 * rows, True)

        @pl.when(z > 0)
        def _():
            store(0, 0, z - 1).wait()

        put(0, low(mm(keys_t[:, 0 : 2 * rows], dkv)))
        put(
            0,
            jnp.concatenate(
                [low(mm(rows_t2[...], dq)), low(mm(rows_t[...], o1[z]))], axis=1
            ),
            384,
        )
        store(0, 0, z).start()
        acc[...] += mm_nt(dq, block(w, z, 1, 384, 576))
        enc_acc[0 : 2 * rows, :] += mm_nt(dkv, block(w, z, 1, 0, 384))
        return carry

    lax.fori_loop(0, parts, self_step, 0)
    store(0, 0, parts - 1).wait()
    gain = gains_ref[0:1, :]
    back, gain1 = norm_back(
        acc[...] + enc_acc[rows : 2 * rows, :], x_ref[...].astype(F32), gain
    )
    dx_ref[...] = dn[...] + back
    back, gain1a = norm_back(enc_acc[0:rows, :], xa_ref[...].astype(F32), gain)
    dxa_ref[...] = low(back)
    small_ref[0:1, 0:width_all] = gain1 + gain1a
    width = diag_acc.shape[2]
    lines = []
    for r in range(parts):
        for j in range(3):
            part = diag_acc[3 * r + j]
            line = part[0:1, :]
            for k in range(1, 8):
                line = line + pltpu.roll(part[k : k + 1, :], width - k, 1)
            lines.append(line)
    lines.append(jnp.zeros((16 - len(lines), width), F32))
    table = lax.dot_general(
        jnp.concatenate(lines, axis=0),
        onehot_ref[...],
        (((1,), (1,)), ((), ())),
        precision=lax.Precision.HIGHEST,
        preferred_element_type=F32,
    )
    me = lax.axis_index("mp")
    for r in range(parts):
        at = lax.rem(me + r, parts)
        for p in range(parts):

            @pl.when(at == p)
            def _(r=r, p=p):
                small_ref[3 + p : 4 + p, width_all : width_all + 128] = table[3 * r : 3 * r + 1]
                small_ref[3 + p : 4 + p, width_all + 128 :] = table[3 * r + 1 : 3 * r + 2]
                small_ref[3 + p : 4 + p, 0:128] = table[3 * r + 2 : 3 * r + 3]


def across_groups(summed, small, n_dp):
    groups = n_dp // 8
    d = lax.axis_index("dp")
    whole = lax.all_gather(summed, "dp", axis=0, tiled=False)
    share, width = summed.shape[1:]
    whole = whole.reshape(groups, 8, 4, share, width).sum(0)
    whole = jnp.transpose(whole, (1, 0, 2, 3)).reshape(4, 8 * share, width)
    rows = 8 * share // n_dp
    small = lax.all_gather(small, "dp", axis=0, tiled=False).reshape(groups, 8, *small.shape)[:, 0]
    return lax.dynamic_slice_in_dim(whole, d * rows, rows, 1), small.sum(0)


def body(
    inputs, encoded, cotangent, lengths, buckets,
    self_gain, self_query, self_key, self_value, self_output, bias_table,
    cross_gain, cross_query, cross_key, cross_value, cross_output,
    feed_gain, feed_inner, feed_output_weight,
):
    rows, width = inputs.shape
    parts = lax.axis_size("mp")
    n_dp = lax.axis_size("dp")
    halves = parts // lengths.shape[0]
    assert halves == 2 and buckets.shape[0] == 2 * rows and parts == 4
    z = lax.axis_index("mp")
    enc_rows = encoded.shape[0]
    vmem = pl.BlockSpec(memory_space=pltpu.VMEM)
    smem = pl.BlockSpec(memory_space=pltpu.SMEM)
    hbm = pl.BlockSpec(memory_space=pl.ANY)
    sds = jax.ShapeDtypeStruct

    share = width // 8
    packed = jnp.stack(
        [
            jnp.concatenate([self_key, self_value, self_query, self_output.T], axis=1),
            jnp.concatenate([cross_key, cross_value, cross_query, cross_output.T], axis=1),
            feed_inner,
            feed_output_weight.T,
        ]
    ).reshape(4, 4, 2, share, width)
    table_own = jnp.pad(bias_table.T, ((0, 8 - bias_table.shape[1]), (0, 128 - bias_table.shape[0])))
    weights, other, enc_other, table_all = pl.pallas_call(
        gather_kernel,
        out_shape=[
            sds((4, parts, 4, 2, share, width), BF16),
            sds((rows, width), BF16),
            sds((enc_rows, width), BF16),
            sds((parts, 8, 128), F32),
        ],
        in_specs=[hbm] * 4,
        out_specs=[hbm] * 4,
        scratch_shapes=[
            pltpu.SemaphoreType.DMA((4, parts - 1)),
            pltpu.SemaphoreType.DMA((4, parts - 1)),
            pltpu.SemaphoreType.DMA((4, 5)),
            pltpu.SemaphoreType.DMA((4, 5)),
            pltpu.SemaphoreType.DMA((5,)),
            pltpu.SemaphoreType.DMA((5,)),
        ],
        compiler_params=pltpu.CompilerParams(collective_id=1, has_side_effects=True),
        name="gather",
    )(packed, inputs, encoded, table_own)
    half = lax.rem(z, 2)
    length = lax.dynamic_slice_in_dim(lengths, lax.div(z, 2), 1)
    gains = jnp.concatenate(
        [jnp.stack([self_gain, cross_gain, feed_gain]), jnp.zeros((5, width), F32)]
    )
    diag = 1024
    line = jnp.concatenate(
        [
            buckets[0 : rows + 1][::-1],
            jnp.full((diag - 2 * rows,), -1, jnp.int32),
            buckets[rows + 1 :][::-1],
        ]
    )
    onehot = (line[None, :] == lax.iota(jnp.int32, 128)[:, None]).astype(F32)
    heads = 3 * parts
    keys = 2 * enc_rows
    saved = [
        ((2 * rows, width), BF16),
        ((parts, rows, 192), BF16),
        ((parts, 2 * rows, 384), BF16),
        ((heads, rows, 2 * rows), BF16),
        ((parts, rows, 192), BF16),
        ((parts, rows, 128), F32),
        ((rows, width), F32),
        ((rows, width), BF16),
        ((parts, rows, 192), BF16),
        ((parts, keys, 384), BF16),
        ((heads, rows, keys), BF16),
        ((parts, rows, 192), BF16),
        ((parts, rows, 128), F32),
        ((rows, width), F32),
        ((rows, width), BF16),
        ((parts, rows, width), BF16),
        ((parts, rows, width), BF16),
    ]
    n1s, q1s, kv1s, p1s, o1s, l1s, x1s, n2s, q2s, kv2s, p2s, o2s, l2s, x2s, n3s, hids, slopes = [
        pltpu.VMEM(*s) for s in saved
    ]
    result, *kept = pl.pallas_call(
        functools.partial(forward_kernel, halves),
        out_shape=[sds((rows, width), BF16)] + [sds(*s) for s in saved],
        in_specs=[smem, vmem, vmem, hbm, hbm, vmem, vmem, vmem, vmem, hbm, hbm],
        out_specs=[vmem] + [hbm] * len(saved),
        scratch_shapes=[
            pltpu.VMEM((4, parts, 4, 2, share, width), BF16),
            pltpu.VMEM((2, enc_rows, width), BF16),
            pltpu.VMEM((parts, 8, diag), F32),
            pltpu.VMEM((rows, 2 * rows), F32),
            pltpu.VMEM((3, rows, keys), F32),
            n1s, q1s, kv1s, p1s, o1s, x1s, n2s, q2s, kv2s, p2s, o2s, x2s, n3s, hids, slopes,
            l1s, l2s,
            pltpu.VMEM((rows, width), F32),
            pltpu.SemaphoreType.DMA((4, parts)),
            pltpu.SemaphoreType.DMA((2,)),
            pltpu.SemaphoreType.DMA((len(saved),)),
        ],
        compiler_params=pltpu.CompilerParams(vmem_limit_bytes=VMEM_BYTES),
        name="forward",
    )(
        length, inputs, other, encoded, enc_other, gains, table_own, table_all, onehot, packed, weights
    )

    dx, dxa, denc, small, grads = pl.pallas_call(
        backward_kernel,
        out_shape=[
            sds((rows, width), F32),
            sds((rows, width), BF16),
            sds((2, enc_rows, width), BF16),
            sds((8, diag), F32),
            sds((TICKS, 4, 2, share, width), BF16),
        ],
        in_specs=[vmem, vmem, vmem, vmem, vmem] + [hbm] * 21,
        out_specs=[vmem] * 4 + [hbm],
        scratch_shapes=[
            pltpu.VMEM((parts, 2, 4, 2, share, width), BF16),
            pltpu.VMEM((2, enc_rows, width), BF16),
            n1s, q1s, kv1s, pltpu.VMEM((2, 3, rows, 2 * rows), BF16), o1s, l1s, n2s, q2s, kv2s, pltpu.VMEM((2, 3, rows, keys), BF16), o2s, l2s, x2s, n3s,
            hids, slopes,
            pltpu.VMEM((2, 4, 2, share, width), BF16),
            pltpu.VMEM((width, rows), BF16),
            pltpu.VMEM((width, rows), BF16),
            pltpu.VMEM((width, keys), BF16),
            pltpu.VMEM((2, rows, keys), F32),
            pltpu.VMEM((2, rows, keys), BF16),
            pltpu.VMEM((384, keys), F32),
            pltpu.VMEM((rows, width), F32),
            pltpu.VMEM((rows, width), F32),
            pltpu.VMEM((keys, width), F32),
            pltpu.VMEM((heads, 8, diag), F32),
            pltpu.SemaphoreType.DMA((parts, 2)),
            pltpu.SemaphoreType.DMA((20,)),
            pltpu.SemaphoreType.DMA((2, 2)),
            pltpu.SemaphoreType.DMA((2,)),
        ],
        compiler_params=pltpu.CompilerParams(vmem_limit_bytes=VMEM_BYTES),
        name="backward",
    )(inputs, other, cotangent, gains, onehot, encoded, enc_other, packed, weights, *kept)

    summed, small, input_grad, encoder_grad = pl.pallas_call(
        scatter_kernel,
        out_shape=[
            sds((4, share, width), F32),
            sds((8, diag), F32),
            sds((rows, width), BF16),
            sds((enc_rows, width), BF16),
        ],
        in_specs=[hbm, vmem, vmem, vmem, vmem],
        out_specs=[vmem] * 4,
        scratch_shapes=[
            pltpu.VMEM((2, 4, share, width), BF16),
            pltpu.VMEM((C_RING, 4, share, width), BF16),
            pltpu.VMEM((TICKS, 2, 2, share // 2, width), BF16),
            pltpu.VMEM((TICKS, 2, share // 2, width), BF16),
            pltpu.VMEM((TICKS, share, width), BF16),
            pltpu.VMEM((2, 2, 2, share // 2, width), BF16),
            pltpu.VMEM((2, 2, 2, share // 2, width), F32),
            pltpu.VMEM((2, 2, share // 2, width), BF16),
            pltpu.VMEM((2, 2, share // 2, width), F32),
            pltpu.VMEM((2, share, width), BF16),
            pltpu.VMEM((3, 8, diag), F32),
            pltpu.VMEM((3, 8, diag), F32),
            pltpu.VMEM((parts, 8, diag), F32),
            pltpu.VMEM((rows, width), BF16),
            pltpu.VMEM((enc_rows, width), BF16),
            pltpu.SemaphoreType.DMA((2, 6, TICKS)),
            pltpu.SemaphoreType.REGULAR,
            pltpu.SemaphoreType.DMA((6,)),
            pltpu.SemaphoreType.DMA((6,)),
            pltpu.SemaphoreType.DMA((2,)),
            pltpu.SemaphoreType.DMA((2,)),
            pltpu.SemaphoreType.DMA((2,)),
        ],
        compiler_params=pltpu.CompilerParams(
            collective_id=2, has_side_effects=True, vmem_limit_bytes=VMEM_BYTES
        ),
        name="scatter",
    )(grads, small, dx, dxa, denc)
    if n_dp > 8:
        summed, small = across_groups(summed, small, n_dp)
    buckets_here = bias_table.shape[0]
    mine = lax.dynamic_slice_in_dim(small, 3 + z, 1, 0)[0]
    table_mine = jnp.stack(
        [mine[width : width + buckets_here], mine[width + 128 :][:buckets_here], mine[:buckets_here]],
        axis=1,
    )
    gs, gc = summed[0], summed[1]
    return (
        result,
        low(input_grad),
        low(encoder_grad),
        small[0, :width],
        gs[:, 384:576],
        gs[:, 0:192],
        gs[:, 192:384],
        gs[:, 576:768].T,
        table_mine,
        small[1, :width],
        gc[:, 384:576],
        gc[:, 0:192],
        gc[:, 192:384],
        gc[:, 576:768].T,
        small[2, :width],
        summed[2],
        summed[3].T,
    )


def solution(mesh):
    rows = P(("dp", "mp"), None)
    across, down = P(None, "mp"), P("mp", None)
    return jax.shard_map(
        body,
        mesh=mesh,
        in_specs=(
            rows, rows, rows, P("dp"), P(),
            P(), across, across, across, down, across,
            P(), across, across, across, down,
            P(), across, down,
        ),
        out_specs=(
            rows, rows, rows,
            P(), P("dp", "mp"), P("dp", "mp"), P("dp", "mp"), P("mp", "dp"), P(None, "mp"),
            P(), P("dp", "mp"), P("dp", "mp"), P("dp", "mp"), P("mp", "dp"),
            P(), P("dp", "mp"), P("mp", "dp"),
        ),
        check_vma=False,
    )
```

```python
import functools

import jax
import jax.numpy as jnp
from jax import lax
from jax.experimental import pallas as pl
from jax.experimental.pallas import tpu as pltpu
from jax.sharding import PartitionSpec as P

EPS = 1e-06
MASKED = -1e30
DH = 64
F32 = jnp.float32
BF16 = jnp.bfloat16
VMEM_BYTES = 62 << 20
ROOT = 0.7978845608028654
CUBE = 0.044715


def mm(a, b):
    return jnp.dot(a, b, preferred_element_type=F32)


def mm_nt(a, b):
    return lax.dot_general(a, b, (((1,), (1,)), ((), ())), preferred_element_type=F32)


def low(v):
    return v.astype(BF16)


def flip(v):
    return jnp.transpose(v.astype(F32)).astype(BF16)


def norm_rows(v, gain):
    root = lax.rsqrt(jnp.mean(v * v, axis=-1, keepdims=True) + EPS)
    unit = v * root
    return unit * gain, unit, root


def norm_back(grad, v, gain):
    _, unit, root = norm_rows(v, gain)
    scaled = grad * gain
    back = root * (scaled - unit * jnp.mean(scaled * unit, axis=-1, keepdims=True))
    return back, jnp.sum(grad * unit, axis=0, keepdims=True)


def block(w, i, j, start=0, stop=None):
    part = w[i, j, :, :, :, start:stop]
    return part.reshape(part.shape[0] * part.shape[1] * part.shape[2], part.shape[3])


def half_of_sequence(halves):
    return lax.rem(lax.axis_index("mp"), halves)


def chunks(rows, step):
    return [(r, min(step, rows - r)) for r in range(0, rows, step)]


MESH_ID = pl.DeviceIdType.MESH


def places():
    d = lax.axis_index("dp")
    z = lax.axis_index("mp")
    lo = lax.rem(d, 8)
    core = lax.rem(lo, 2)
    x = lax.rem(lax.div(lo, 2), 2)
    y = lax.div(lo, 4)
    d_core = d + 1 - 2 * core
    d_x = d + 2 - 4 * x
    d_y = d + 4 - 8 * y
    return d, z, core, x, y, d_core, d_x, d_y


def greet(z_parts):
    d, z, _, _, _, d_core, d_x, d_y = places()
    barrier = pltpu.get_barrier_semaphore()
    for who in (d_core, d_x, d_y):
        pl.semaphore_signal(barrier, inc=1, device_id=(who, z), device_id_type=MESH_ID)
    for step in range(1, z_parts):
        pl.semaphore_signal(
            barrier, inc=1, device_id=(d, lax.rem(z + step, z_parts)), device_id_type=MESH_ID
        )
    pl.semaphore_wait(barrier, 2 + z_parts)


def remote(src, dst, send, recv, who):
    return pltpu.make_async_remote_copy(
        src_ref=src, dst_ref=dst, send_sem=send, recv_sem=recv, device_id=who, device_id_type=MESH_ID
    )


class Gather:
    chunks = 8

    def __init__(self, packed, wg, z_send, z_recv, s_send, s_recv):
        self.packed, self.wg = packed, wg
        self.z_sems, self.s_sems = (z_send, z_recv), (s_send, s_recv)
        self.parts = wg.shape[1]
        self.place = places()

    def rows(self, k):
        half = self.wg.shape[4] // 2
        return k // 2, pl.ds((k % 2) * half, half)

    def z_copy(self, k, step):
        d, z, core, x, y, *_ = self.place
        yx = 2 * y + x
        g, rows = self.rows(k)
        return remote(
            self.packed.at[g, yx, core, rows],
            self.wg.at[g, self.parts - step, yx, core, rows],
            self.z_sems[0].at[k, step - 1],
            self.z_sems[1].at[k, step - 1],
            (d, lax.rem(z + step, self.parts)),
        )

    def s_copy(self, k, n):
        d, z, core, x, y, d_core, d_x, d_y = self.place
        rest = pl.ds(1, self.parts - 1)
        g, rows = self.rows(k)
        width = self.wg.shape[5]
        if n < 2:
            ref = self.wg.at[g, rest, 2 * y + x, core, rows]
            who = (d_x, d_y)[n]
        elif n == 2:
            ref = self.wg.at[g, rest, 2 * y + 1 - x, core, rows, pl.ds(0, width // 2)]
            who = d_y
        elif n == 3:
            ref = self.wg.at[g, rest, 2 * (1 - y) + x, core, rows, pl.ds(width // 2, width // 2)]
            who = d_x
        else:
            ref = self.wg.at[g, rest, :, core, rows]
            who = d_core
        return remote(ref, ref, self.s_sems[0].at[k, n], self.s_sems[1].at[k, n], (who, z))

    def z_start(self, k):
        for step in range(1, self.parts):
            self.z_copy(k, step).start()

    def tick(self, k):
        if 0 <= k - 2 < self.chunks:
            self.s_copy(k - 2, 2).wait_recv()
            self.s_copy(k - 2, 3).wait_recv()
            self.s_copy(k - 2, 4).start()
        if 0 <= k - 1 < self.chunks:
            self.s_copy(k - 1, 0).wait_recv()
            self.s_copy(k - 1, 2).start()
            self.s_copy(k - 1, 1).wait_recv()
            self.s_copy(k - 1, 3).start()
        if k < self.chunks:
            for step in range(1, self.parts):
                self.z_copy(k, step).wait_recv()
            self.s_copy(k, 0).start()
            self.s_copy(k, 1).start()
        if k + 2 < self.chunks:
            self.z_start(k + 2)

    def arrived(self, g):
        self.s_copy(2 * g, 4).wait_recv()
        self.s_copy(2 * g + 1, 4).wait_recv()

    def sent(self):
        for k in range(self.chunks):
            for step in range(1, self.parts):
                self.z_copy(k, step).wait_send()
            for n in range(5):
                self.s_copy(k, n).wait_send()


C_RING = 4
TICKS = 16


class Scatter:
    def __init__(self, bufs, sems, credit):
        (
            self.c_in, self.a_in, self.b_in, self.z_in,
            self.a_out, self.a_keep, self.b_out, self.b_keep, self.z_out, self.total,
        ) = bufs
        self.sems, self.credit = sems, credit
        self.parts = 4
        self.share = self.z_out.shape[1]
        self.place = places()

    def block(self, t):
        feed = 1 - lax.div(t, 8)
        r = feed * lax.div(t, 2) + (1 - feed) * lax.rem(t, 4)
        g = feed * (3 - lax.rem(t, 2)) + (1 - feed) * (3 - lax.div(t, 4))
        return g, r

    def copy(self, k, t, src, dst, who):
        return remote(src, dst, self.sems.at[0, k, t], self.sems.at[1, k, t], who)

    def c_copy(self, t, src):
        z, d_core = self.place[1], self.place[5]
        return self.copy(0, t, src, self.c_in.at[lax.rem(t, C_RING)], (d_core, z))

    def a_copy(self, t, q):
        _, z, *_, d_x, d_y = self.place
        src, dst = self.a_out.at[lax.rem(t, 2), q], self.a_in.at[t, q]
        return self.copy(1 + q, t, src, dst, ((d_x, d_y)[q], z))

    def b_copy(self, t, q):
        _, z, *_, d_x, d_y = self.place
        src, dst = self.b_out.at[lax.rem(t, 2), q], self.b_in.at[t, q]
        return self.copy(3 + q, t, src, dst, ((d_y, d_x)[q], z))

    def z_copy(self, t):
        d, z = self.place[:2]
        who = (d, lax.rem(z + self.block(t)[1], self.parts))
        return self.copy(5, t, self.z_out.at[lax.rem(t, 2)], self.z_in.at[t], who)

    def rows(self, q):
        return pl.ds(q * (self.share // 2), self.share // 2)

    def c_start(self, t, src):
        @pl.when(t >= C_RING)
        def _():
            pl.semaphore_wait(self.credit, 1)

        self.c_copy(t, src).start()

    def a_start(self, t, mine, src):
        _, z, _, x, y, d_core, *_ = self.place
        slot, ring = lax.rem(t, 2), lax.rem(t, C_RING)

        @pl.when(t >= 2)
        def _():
            self.a_copy(t - 2, 0).wait_send()
            self.a_copy(t - 2, 1).wait_send()

        self.c_copy(t, src).wait_recv()
        for q in range(2):
            rows = self.rows(q)
            for k in range(2):
                send = (2 * k + 1 - x, 2 * (1 - y) + k)[q]
                keep = (2 * k + x, 2 * y + k)[q]
                self.a_out[slot, q, k] = low(
                    mine[send, rows].astype(F32) + self.c_in[ring, send, rows].astype(F32)
                )
                self.a_keep[slot, q, k] = mine[keep, rows].astype(F32) + self.c_in[
                    ring, keep, rows
                ].astype(F32)
            self.a_copy(t, q).start()

        @pl.when(t < TICKS - C_RING)
        def _():
            pl.semaphore_signal(
                self.credit, inc=1, device_id=(d_core, z), device_id_type=MESH_ID
            )

    def b_start(self, t):
        _, _, _, x, y, *_ = self.place
        slot = lax.rem(t, 2)

        @pl.when(t >= 2)
        def _():
            self.b_copy(t - 2, 0).wait_send()
            self.b_copy(t - 2, 1).wait_send()

        for q in range(2):
            keep = (y, x)[q]
            send = 1 - keep
            self.a_copy(t, q).wait_recv()
            self.b_out[slot, q] = low(
                self.a_keep[slot, q, send] + self.a_in[t, q, send].astype(F32)
            )
            self.b_keep[slot, q] = self.a_keep[slot, q, keep] + self.a_in[t, q, keep].astype(F32)
            self.b_copy(t, q).start()

    def z_start(self, t):
        slot = lax.rem(t, 2)
        g, r = self.block(t)

        @pl.when((t >= 2) & (self.block(t - 2)[1] > 0))
        def _():
            self.z_copy(t - 2).wait_send()

        for q in range(2):
            self.b_copy(t, q).wait_recv()
            done = self.b_keep[slot, q] + self.b_in[t, q].astype(F32)

            @pl.when(r == 0)
            def _():
                self.total[g, self.rows(q)] = done

            @pl.when(r > 0)
            def _():
                self.z_out[slot, self.rows(q)] = low(done)

        @pl.when(r > 0)
        def _():
            self.z_copy(t).start()

    def step(self, t, mine, src):
        @pl.when((t >= 1) & (t < TICKS + 1))
        def _():
            self.a_start(t - 1, mine, src)

        @pl.when((t >= 2) & (t < TICKS + 2))
        def _():
            self.b_start(t - 2)

        @pl.when((t >= 3) & (t < TICKS + 3))
        def _():
            self.z_start(t - 3)

    def finish(self):
        def drain(t, carry):
            self.a_copy(t, 0).wait_send()
            self.a_copy(t, 1).wait_send()
            self.b_copy(t, 0).wait_send()
            self.b_copy(t, 1).wait_send()
            self.z_copy(t).wait_send()
            return carry

        lax.fori_loop(TICKS - 2, TICKS, drain, 0)

        def add(t, carry):
            g, r = self.block(t)

            @pl.when(r > 0)
            def _():
                self.z_copy(t).wait_recv()
                self.total[g] += self.z_in[t].astype(F32)

            return carry

        lax.fori_loop(0, TICKS, add, 0)


class Sum:
    def __init__(self, out, into, ring, send, recv):
        self.out, self.into, self.ring = out, into, ring
        self.send, self.recv = send, recv
        self.place = places()

    def pair(self, k):
        z, who = self.place[1], self.place[5 + k]
        return remote(
            self.out.at[k], self.into.at[k], self.send.at[k], self.recv.at[k], (who, z)
        )

    def along(self, step):
        d, z = self.place[:2]
        parts = self.ring.shape[0]
        return remote(
            self.ring.at[z], self.ring.at[z], self.send.at[2 + step], self.recv.at[2 + step],
            (d, lax.rem(z + step, parts)),
        )

    def start(self, value):
        self.out[0] = value
        self.pair(0).start()

    def turn(self, k):
        self.pair(k).wait()
        value = self.out[k] + self.into[k]
        if k < 2:
            self.out[k + 1] = value
            self.pair(k + 1).start()
            return
        self.ring[self.place[1]] = value
        for step in range(1, self.ring.shape[0]):
            self.along(step).start()

    def result(self):
        parts = self.ring.shape[0]
        z = self.place[1]
        for step in range(1, parts):
            self.along(step).wait_send()
            sender = lax.rem(z + parts - step, parts)
            remote(
                self.ring.at[sender], self.ring.at[sender],
                self.send.at[2 + step], self.recv.at[2 + step], (self.place[0], sender),
            ).wait_recv()
        value = self.ring[0]
        for k in range(1, parts):
            value = value + self.ring[k]
        return value


def forward_kernel(
    halves,
    len_ref,
    x_ref,
    enc_own,
    gains_ref,
    table_own,
    onehot_ref,
    packed,
    result_ref,
    w_hbm,
    xa_out,
    enc_out,
    n1_out,
    q1_out,
    kv1_out,
    p1_out,
    o1_out,
    l1_out,
    x1_out,
    n2_out,
    q2_out,
    kv2_out,
    p2_out,
    o2_out,
    l2_out,
    x2_out,
    n3_out,
    hid_out,
    slope_out,
    w,
    enc,
    diag,
    mask,
    s_buf,
    n1,
    q1,
    kv1,
    p1,
    o1,
    x1,
    n2,
    q2,
    kv2,
    p2,
    o2,
    x2,
    n3,
    hid,
    slope,
    l1,
    l2,
    acc,
    xa_ref,
    table_ref,
    w_sem,
    enc_sem,
    out_sem,
    z_send,
    z_recv,
    s_send,
    s_recv,
    e_send,
    e_recv,
):
    rows = x_ref.shape[0]
    parts = w.shape[1]
    half = half_of_sequence(halves)

    def fetch(g, r, src=w_hbm):
        src = packed.at[g] if src is packed else src.at[g, r]
        return pltpu.make_async_copy(src, w.at[g, r], w_sem.at[g, r])

    d, z_me = places()[:2]
    mate = z_me + 1 - 2 * half
    greet(parts)
    gather = Gather(packed, w_hbm, z_send, z_recv, s_send, s_recv)
    x_copy = remote(x_ref, xa_ref, e_send.at[0], e_recv.at[0], (d, mate))
    enc_copy = remote(enc_own, enc.at[half], e_send.at[1], e_recv.at[1], (d, mate))
    tables = [
        remote(
            table_own, table_ref.at[parts - step], e_send.at[1 + step], e_recv.at[1 + step],
            (d, lax.rem(z_me + step, parts)),
        )
        for step in range(1, parts)
    ]
    gather.z_start(0)
    for copy in tables:
        copy.start()
    x_copy.start()
    gather.z_start(1)
    enc_here = pltpu.make_async_copy(enc_own, enc.at[half], enc_sem)
    for g in range(4):
        fetch(g, 0, packed).start()
    enc_here.start()

    def take(g):
        gather.arrived(g)
        for r in range(1, parts):
            fetch(g, r).start()

    n1[rows : 2 * rows, :] = low(norm_rows(x_ref[...].astype(F32), gains_ref[0:1, :])[0])
    saves = []

    def save(src, dst):
        copy = pltpu.make_async_copy(src, dst, out_sem.at[len(saves)])
        copy.start()
        saves.append(copy)


    length = len_ref[0]
    i = lax.broadcasted_iota(jnp.int32, mask.shape, 0)
    c = lax.broadcasted_iota(jnp.int32, mask.shape, 1)
    own = c - rows
    limit = jnp.where(half > 0, length, 0)
    ok = ((own < 0) & (c < limit)) | ((own >= 0) & (own <= i) & (own + half * rows < length))
    mask[...] = jnp.where(ok, 0.0, MASKED)

    def heads(z, q, kv, p, o, l, keys, with_bias):
        outs = []
        for j in range(3):
            h = z * 3 + j
            q_h = q[z, :, DH * j : DH * (j + 1)]
            k_h = kv[z, :, DH * j : DH * (j + 1)]
            v_h = kv[z, :, DH * (3 + j) : DH * (4 + j)]
            s_buf[j % 2, :, 0:keys] = mm_nt(q_h, k_h)
            for r, n in chunks(rows, 32):
                s = s_buf[j % 2, r : r + n, 0:keys]
                if with_bias:
                    line = jnp.broadcast_to(diag[z, j : j + 1, :], (n, diag.shape[2]))
                    grid = pltpu.roll(line, r, 1, stride=1, stride_axis=0)
                    s = s + grid[:, 0:keys] + mask[r : r + n, :]
                top = jnp.max(s, axis=1, keepdims=True)
                p[h, r : r + n, :] = low(jnp.exp(s - top))
            wide = jnp.concatenate([v_h, jnp.ones_like(v_h)], axis=1)
            mixed = mm(p[h], wide)
            outs.append(low(mixed[:, 0:DH] / mixed[:, DH : 2 * DH]))
            l[z, :, 32 * j : 32 * (j + 1)] = mixed[:, DH : DH + 32]
        o[z] = jnp.concatenate(outs, axis=1)

    acc[...] = x_ref[...].astype(F32)
    gather.tick(0)
    enc_copy.start()
    gather.tick(1)
    for copy in tables:
        copy.wait()
    for r in range(parts):
        lines = table_own[...] if r == 0 else table_ref[r]
        diag[r] = jnp.dot(
            lines, onehot_ref[...], precision=lax.Precision.HIGHEST, preferred_element_type=F32
        )

    x_copy.wait()
    n1[0:rows, :] = low(norm_rows(xa_ref[...].astype(F32), gains_ref[0:1, :])[0])
    save(n1, n1_out)
    save(xa_ref, xa_out)
    gather.tick(2)
    gather.tick(3)
    take(0)

    def self_step(z, carry):
        fetch(0, z).wait()
        kv1[z] = low(mm(n1[...], block(w, 0, z, 0, 384)))
        q1[z] = low(mm(n1[rows : 2 * rows, :], block(w, 0, z, 384, 576)))
        heads(z, q1, kv1, p1, o1, l1, 2 * rows, True)
        acc[...] += mm_nt(o1[z], block(w, 0, z, 576, 768))

        @pl.when(z == 1)
        def _():
            gather.tick(4)

        return carry

    lax.fori_loop(0, parts, self_step, 0)
    for src, dst in ((q1, q1_out), (kv1, kv1_out), (p1, p1_out), (o1, o1_out), (l1, l1_out)):
        save(src, dst)
    x1[...] = acc[...]
    n2[...] = low(norm_rows(acc[...], gains_ref[1:2, :])[0])
    save(x1, x1_out)
    save(n2, n2_out)
    gather.tick(5)
    take(1)
    enc_copy.wait()
    enc_here.wait()
    save(enc, enc_out)
    keys = 2 * enc.shape[1]

    def cross_step(z, carry):
        fetch(1, z).wait()
        kv2[z] = low(mm(enc[...].reshape(keys, enc.shape[2]), block(w, 1, z, 0, 384)))
        q2[z] = low(mm(n2[...], block(w, 1, z, 384, 576)))
        heads(z, q2, kv2, p2, o2, l2, keys, False)
        acc[...] += mm_nt(o2[z], block(w, 1, z, 576, 768))

        @pl.when(z == 1)
        def _():
            gather.tick(6)

        return carry

    lax.fori_loop(0, parts, cross_step, 0)
    for src, dst in ((q2, q2_out), (kv2, kv2_out), (p2, p2_out), (o2, o2_out), (l2, l2_out)):
        save(src, dst)
    x2[...] = acc[...]
    n3[...] = low(norm_rows(acc[...], gains_ref[2:3, :])[0])
    save(x2, x2_out)
    save(n3, n3_out)
    gather.tick(7)
    take(2)

    def inner_step(z, carry):
        fetch(2, z).wait()
        for r, n in chunks(rows, 64):
            a = mm(n3[r : r + n, :], block(w, 2, z))
            sq = a * a
            t = jnp.tanh(a * (ROOT + ROOT * CUBE * sq))
            cdf = 0.5 + 0.5 * t
            hid[z, r : r + n, :] = low(a * cdf)
            slope[z, r : r + n, :] = low(
                cdf + 0.5 * a * (1.0 - t * t) * (ROOT + 3.0 * ROOT * CUBE * sq)
            )

        @pl.when(z == 1)
        def _():
            gather.tick(8)

        return carry

    lax.fori_loop(0, parts, inner_step, 0)
    save(hid, hid_out)
    save(slope, slope_out)
    gather.tick(9)
    take(3)

    def outer_step(z, carry):
        fetch(3, z).wait()
        acc[...] += mm_nt(hid[z], block(w, 3, z))
        return carry

    lax.fori_loop(0, parts, outer_step, 0)
    result_ref[...] = low(acc[...])
    for copy in saves:
        copy.wait()
    gather.sent()


def backward_kernel(
    x_ref, xa_ref, cot_ref, gains_ref, onehot_ref, enc_hbm, packed, w_hbm,
    n1_hbm, q1_hbm, kv1_hbm, p1_hbm, o1_hbm, l1_hbm, x1_hbm,
    n2_hbm, q2_hbm, kv2_hbm, p2_hbm, o2_hbm, l2_hbm, x2_hbm,
    n3_hbm, hid_hbm, slope_hbm,
    total_out, small_out, dx_out, denc_out,
    w, enc, nbuf, n2, q_in, kv_in, p_in, o_in, l_in, x_in, hid, slope,
    g_buf, rows_t, rows_t2, keys_t, dp_buf, ds_buf, dkv_t, dn, acc, enc_acc, diag_acc,
    dxa, dxa_in, denc, denc_in, small,
    c_in, a_in, b_in, z_in, a_out, a_keep, b_out, b_keep, z_out, s_out, s_in, s_ring,
    w_sem, one_sem, ring_sem,
    sems, credit, s_send, s_recv, e_send, e_recv,
):
    rows, width_all = x_ref.shape
    parts = w_hbm.shape[1]
    place = places()
    d, z_me, core = place[:3]
    half = lax.rem(z_me, 2)
    mate = z_me + 1 - 2 * half
    keys = 2 * enc.shape[1]
    own_keys = 2 * rows

    singles = [(n3_hbm, nbuf.at[0:rows]), (x2_hbm, x_in), (n2_hbm, n2), (enc_hbm, enc),
               (x1_hbm, x_in), (n1_hbm, nbuf)]

    def single(k):
        return pltpu.make_async_copy(*singles[k], one_sem.at[k])

    def streams(phase, r):
        slot = lax.rem(r, 2)
        if phase == 0:
            pairs = [(hid_hbm.at[r], hid.at[slot]), (slope_hbm.at[r], slope.at[slot])]
        else:
            q, kv, p, o, l = (
                (q2_hbm, kv2_hbm, p2_hbm, o2_hbm, l2_hbm),
                (q1_hbm, kv1_hbm, p1_hbm, o1_hbm, l1_hbm),
            )[phase - 1]
            n = (keys, own_keys)[phase - 1]
            pairs = [
                (q.at[r], q_in.at[slot]),
                (kv.at[r], kv_in.at[slot, 0:n]),
                (p.at[pl.ds(3 * r, 3)], p_in.at[slot, :, :, 0:n]),
                (o.at[r], o_in.at[slot]),
                (l.at[r], l_in.at[slot]),
            ]
        return [
            pltpu.make_async_copy(src, dst, ring_sem.at[k, slot])
            for k, (src, dst) in enumerate(pairs)
        ]

    def weight(g, r, k, src=None):
        slot = lax.rem(r, 2)
        src = w_hbm.at[g, r] if src is None else src.at[g]
        return pltpu.make_async_copy(src, w.at[slot, k], w_sem.at[slot, k])

    groups = ((3, 2), (1,), (0,))

    def prefetch(phase, r, first):
        for k, g in enumerate(groups[phase]):
            weight(g, r, k, packed if first else None).start()
        for copy in streams(phase, r):
            copy.start()

    def turn(phase, r):
        for k, g in enumerate(groups[phase]):
            weight(g, r, k).wait()
        for copy in streams(phase, r):
            copy.wait()

        @pl.when(r + 1 < parts)
        def _():
            prefetch(phase, r + 1, False)

        if phase < 2:

            @pl.when(r + 1 == parts)
            def _():
                prefetch(phase + 1, 0, True)

    prefetch(0, 0, True)
    for k in range(4):
        single(k).start()

    greet(parts)
    scatter = Scatter(
        (c_in, a_in, b_in, z_in, a_out, a_keep, b_out, b_keep, z_out, total_out), sems, credit
    )
    sums = Sum(s_out, s_in, s_ring, s_send, s_recv)
    dxa_copy = remote(dxa, dxa_in, e_send.at[0], e_recv.at[0], (d, mate))
    denc_copy = remote(denc.at[1 - half], denc_in, e_send.at[1], e_recv.at[1], (d, mate))

    def away(t):
        return g_buf.at[lax.rem(t, 2), :, 1 - core]

    def claim(t):
        @pl.when(t >= 2)
        def _():
            scatter.c_copy(t - 2, away(t)).wait_send()

    def put(t, value, start=0):
        shape = g_buf.shape[1:4] + (value.shape[1],)
        g_buf[lax.rem(t, 2), :, :, :, start : start + value.shape[1]] = value.reshape(shape)

    def release(t):
        scatter.c_start(t, away(t))
        scatter.step(t, g_buf.at[lax.rem(t + 1, 2), :, core], away(t + 1))

    rows_t[...] = flip(cot_ref[...])
    single(0).wait()
    rows_t2[...] = flip(nbuf[0:rows, :])
    acc[...] = jnp.zeros_like(acc)

    def feed_step(r, carry):
        turn(0, r)
        slot = lax.rem(r, 2)
        dh = low(mm(cot_ref[...], block(w, slot, 0)))
        claim(2 * r)
        put(2 * r, low(mm(rows_t[...], hid[slot])))
        release(2 * r)
        slope[slot] = low(dh.astype(F32) * slope[slot].astype(F32))
        claim(2 * r + 1)
        put(2 * r + 1, low(mm(rows_t2[...], slope[slot])))
        release(2 * r + 1)
        acc[...] += mm_nt(slope[slot], block(w, slot, 1))
        return carry

    lax.fori_loop(0, parts, feed_step, 0)
    single(1).wait()
    back, gain3 = norm_back(acc[...], x_in[...], gains_ref[2:3, :])
    dn[...] = cot_ref[...].astype(F32) + back
    single(4).start()
    single(5).start()
    small[...] = jnp.zeros_like(small)
    small[2:3, 0:width_all] = gain3

    def heads_back(r, do, n, with_diag):
        slot = lax.rem(r, 2)
        q, kv, o = q_in[slot], kv_in.at[slot], o_in[slot].astype(F32)
        do_all = []
        delta_all = []
        for j in range(3):
            do_h = do[:, DH * j : DH * (j + 1)]
            inv = 1.0 / l_in[slot, :, 32 * j : 32 * j + 1]
            o_h = o[:, DH * j : DH * (j + 1)]
            delta_all.append(jnp.sum(do_h * o_h * inv, axis=1, keepdims=True))
            do_all.append(do_h * inv)
        do_t = low(jnp.transpose(jnp.concatenate(do_all, axis=1)))
        q_t = flip(q)
        dq = []
        for j in range(3):
            p_h = p_in.at[slot, j]
            k_h = kv[0:n, DH * j : DH * (j + 1)]
            v_h = kv[0:n, DH * (3 + j) : DH * (4 + j)]
            dp_buf[j % 2, :, 0:n] = mm_nt(low(do_all[j]), v_h)
            total = None
            for s, m in chunks(rows, 32):
                ds = low(
                    p_h[s : s + m, 0:n].astype(F32)
                    * (dp_buf[j % 2, s : s + m, 0:n] - delta_all[j][s : s + m, :])
                )
                ds_buf[j % 2, s : s + m, 0:n] = ds
                if with_diag:
                    width = diag_acc.shape[2]
                    wide = jnp.concatenate([ds.astype(F32), jnp.zeros((m, width - n), F32)], axis=1)
                    for b in range(0, m, 8):
                        turned = pltpu.roll(wide[b : b + 8, :], (width - s - b) % width, 1)
                        total = turned if total is None else total + turned
            if with_diag:
                diag_acc[r * 3 + j] = total
            ds_h = ds_buf[j % 2, :, 0:n]
            dq.append(low(mm(ds_h, k_h)))
            dkv_t[DH * j : DH * (j + 1), 0:n] = mm(q_t[DH * j : DH * (j + 1), :], ds_h)
            dkv_t[DH * (3 + j) : DH * (4 + j), 0:n] = mm(
                do_t[DH * j : DH * (j + 1), :], p_h[:, 0:n]
            )
        return jnp.concatenate(dq, axis=1), low(jnp.transpose(dkv_t[:, 0:n]))

    def attention_step(phase, n, r):
        slot = lax.rem(r, 2)
        t = 4 + 4 * phase + r
        turn(phase, r)
        do = low(mm(low(dn[...]), block(w, slot, 0, 576, 768))).astype(F32)
        dq, dkv = heads_back(r, do, n, phase == 2)
        claim(t)
        put(t, low(mm(keys_t[:, 0:n], dkv)))
        both = [low(mm(rows_t2[...], dq)), low(mm(rows_t[...], o_in[slot]))]
        put(t, jnp.concatenate(both, axis=1), 384)
        release(t)
        acc[...] += mm_nt(dq, block(w, slot, 0, 384, 576))
        enc_acc[0:n, :] += mm_nt(dkv, block(w, slot, 0, 0, 384))

    rows_t[...] = flip(low(dn[...]))
    single(2).wait()
    single(3).wait()
    rows_t2[...] = flip(n2[...])
    keys_t[...] = flip(enc[...].reshape(keys, width_all))
    acc[...] = jnp.zeros_like(acc)
    enc_acc[...] = jnp.zeros_like(enc_acc)

    def cross_step(r, carry):
        attention_step(1, keys, r)
        return carry

    lax.fori_loop(0, parts, cross_step, 0)
    denc[...] = low(enc_acc[...]).reshape(denc.shape)
    denc_copy.start()
    single(4).wait()
    back, gain2 = norm_back(acc[...], x_in[...], gains_ref[1:2, :])
    dn[...] += back
    small[1:2, 0:width_all] = gain2

    rows_t[...] = flip(low(dn[...]))
    single(5).wait()
    rows_t2[...] = flip(nbuf[rows : 2 * rows, :])
    keys_t[:, 0:own_keys] = flip(nbuf[...])
    acc[...] = jnp.zeros_like(acc)
    enc_acc[0:own_keys, :] = jnp.zeros((own_keys, width_all), F32)

    def self_step(r, carry):
        attention_step(2, own_keys, r)
        return carry

    lax.fori_loop(0, parts, self_step, 0)
    gain = gains_ref[0:1, :]
    back, gain1a = norm_back(enc_acc[0:rows, :], xa_ref[...].astype(F32), gain)
    dxa[...] = low(back)

    @pl.when(half == 1)
    def _():
        dxa_copy.start()

    back, gain1 = norm_back(
        acc[...] + enc_acc[rows : 2 * rows, :], x_ref[...].astype(F32), gain
    )
    dn[...] += back
    small[0:1, 0:width_all] = gain1 + gain1a
    width = diag_acc.shape[2]
    lines = []
    for r in range(parts):
        for j in range(3):
            part = diag_acc[3 * r + j]
            line = part[0:1, :]
            for k in range(1, 8):
                line = line + pltpu.roll(part[k : k + 1, :], width - k, 1)
            lines.append(line)
    lines.append(jnp.zeros((16 - len(lines), width), F32))
    table = lax.dot_general(
        jnp.concatenate(lines, axis=0),
        onehot_ref[...],
        (((1,), (1,)), ((), ())),
        precision=lax.Precision.HIGHEST,
        preferred_element_type=F32,
    )
    for r in range(parts):
        at = lax.rem(z_me + r, parts)
        for p in range(parts):

            @pl.when(at == p)
            def _(r=r, p=p):
                small[3 + p : 4 + p, width_all : width_all + 128] = table[3 * r : 3 * r + 1]
                small[3 + p : 4 + p, width_all + 128 :] = table[3 * r + 1 : 3 * r + 2]
                small[3 + p : 4 + p, 0:128] = table[3 * r + 2 : 3 * r + 3]

    sums.start(small[...])

    def tail(t, carry):
        scatter.step(t, g_buf.at[lax.rem(t + 1, 2), :, core], away(t + 1))
        for k in range(3):

            @pl.when(t == TICKS + k)
            def _(k=k):
                sums.turn(k)

        return carry

    lax.fori_loop(TICKS, TICKS + 3, tail, 0)
    denc_copy.wait()
    denc_out[...] = low(denc[half].astype(F32) + denc_in[...].astype(F32))
    scatter.finish()
    small_out[...] = sums.result()

    @pl.when(half == 1)
    def _():
        dxa_copy.wait_send()
        dx_out[...] = low(dn[...])

    @pl.when(half == 0)
    def _():
        dxa_copy.wait_recv()
        dx_out[...] = low(dn[...] + dxa_in[...].astype(F32))

    for t in (TICKS - 2, TICKS - 1):
        scatter.c_copy(t, away(t)).wait_send()


def across_groups(summed, small, n_dp):
    groups = n_dp // 8
    d = lax.axis_index("dp")
    whole = lax.all_gather(summed, "dp", axis=0, tiled=False)
    share, width = summed.shape[1:]
    whole = whole.reshape(groups, 8, 4, share, width).sum(0)
    whole = jnp.transpose(whole, (1, 0, 2, 3)).reshape(4, 8 * share, width)
    rows = 8 * share // n_dp
    small = lax.all_gather(small, "dp", axis=0, tiled=False).reshape(groups, 8, *small.shape)[:, 0]
    return lax.dynamic_slice_in_dim(whole, d * rows, rows, 1), small.sum(0)


def body(
    inputs, encoded, cotangent, lengths, buckets,
    self_gain, self_query, self_key, self_value, self_output, bias_table,
    cross_gain, cross_query, cross_key, cross_value, cross_output,
    feed_gain, feed_inner, feed_output_weight,
):
    rows, width = inputs.shape
    parts = lax.axis_size("mp")
    n_dp = lax.axis_size("dp")
    halves = parts // lengths.shape[0]
    assert halves == 2 and buckets.shape[0] == 2 * rows and parts == 4
    z = lax.axis_index("mp")
    enc_rows = encoded.shape[0]
    vmem = pl.BlockSpec(memory_space=pltpu.VMEM)
    smem = pl.BlockSpec(memory_space=pltpu.SMEM)
    hbm = pl.BlockSpec(memory_space=pl.ANY)
    sds = jax.ShapeDtypeStruct

    share = width // 8
    packed = jnp.stack(
        [
            jnp.concatenate([self_key, self_value, self_query, self_output.T], axis=1),
            jnp.concatenate([cross_key, cross_value, cross_query, cross_output.T], axis=1),
            feed_inner,
            feed_output_weight.T,
        ]
    ).reshape(4, 4, 2, share, width)
    table_own = jnp.pad(bias_table.T, ((0, 8 - bias_table.shape[1]), (0, 128 - bias_table.shape[0])))
    length = lax.dynamic_slice_in_dim(lengths, lax.div(z, 2), 1)
    gains = jnp.concatenate(
        [jnp.stack([self_gain, cross_gain, feed_gain]), jnp.zeros((5, width), F32)]
    )
    diag = 1024
    line = jnp.concatenate(
        [
            buckets[0 : rows + 1][::-1],
            jnp.full((diag - 2 * rows,), -1, jnp.int32),
            buckets[rows + 1 :][::-1],
        ]
    )
    onehot = (line[None, :] == lax.iota(jnp.int32, 128)[:, None]).astype(F32)
    heads = 3 * parts
    keys = 2 * enc_rows
    saved = [
        ((2 * rows, width), BF16),
        ((parts, rows, 192), BF16),
        ((parts, 2 * rows, 384), BF16),
        ((heads, rows, 2 * rows), BF16),
        ((parts, rows, 192), BF16),
        ((parts, rows, 128), F32),
        ((rows, width), F32),
        ((rows, width), BF16),
        ((parts, rows, 192), BF16),
        ((parts, keys, 384), BF16),
        ((heads, rows, keys), BF16),
        ((parts, rows, 192), BF16),
        ((parts, rows, 128), F32),
        ((rows, width), F32),
        ((rows, width), BF16),
        ((parts, rows, width), BF16),
        ((parts, rows, width), BF16),
    ]
    n1s, q1s, kv1s, p1s, o1s, l1s, x1s, n2s, q2s, kv2s, p2s, o2s, l2s, x2s, n3s, hids, slopes = [
        pltpu.VMEM(*s) for s in saved
    ]
    result, weights, other, enc_all, *kept = pl.pallas_call(
        functools.partial(forward_kernel, halves),
        out_shape=[
            sds((rows, width), BF16),
            sds((4, parts, 4, 2, share, width), BF16),
            sds((rows, width), BF16),
            sds((2, enc_rows, width), BF16),
        ]
        + [sds(*s) for s in saved],
        in_specs=[smem, vmem, hbm, vmem, vmem, vmem, hbm],
        out_specs=[vmem] + [hbm] * (3 + len(saved)),
        scratch_shapes=[
            pltpu.VMEM((4, parts, 4, 2, share, width), BF16),
            pltpu.VMEM((2, enc_rows, width), BF16),
            pltpu.VMEM((parts, 8, diag), F32),
            pltpu.VMEM((rows, 2 * rows), F32),
            pltpu.VMEM((2, rows, keys), F32),
            n1s, q1s, kv1s, p1s, o1s, x1s, n2s, q2s, kv2s, p2s, o2s, x2s, n3s, hids, slopes,
            l1s, l2s,
            pltpu.VMEM((rows, width), F32),
            pltpu.VMEM((rows, width), BF16),
            pltpu.VMEM((parts, 8, 128), F32),
            pltpu.SemaphoreType.DMA((4, parts)),
            pltpu.SemaphoreType.DMA,
            pltpu.SemaphoreType.DMA((2 + len(saved),)),
            pltpu.SemaphoreType.DMA((8, parts - 1)),
            pltpu.SemaphoreType.DMA((8, parts - 1)),
            pltpu.SemaphoreType.DMA((8, 5)),
            pltpu.SemaphoreType.DMA((8, 5)),
            pltpu.SemaphoreType.DMA((5,)),
            pltpu.SemaphoreType.DMA((5,)),
        ],
        compiler_params=pltpu.CompilerParams(
            collective_id=1, has_side_effects=True, vmem_limit_bytes=VMEM_BYTES
        ),
        name="forward",
    )(length, inputs, encoded, gains, table_own, onehot, packed)

    half_share = share // 2
    summed, small, input_grad, encoder_grad = pl.pallas_call(
        backward_kernel,
        out_shape=[
            sds((4, share, width), F32),
            sds((8, diag), F32),
            sds((rows, width), BF16),
            sds((enc_rows, width), BF16),
        ],
        in_specs=[vmem] * 5 + [hbm] * 20,
        out_specs=[vmem] * 4,
        scratch_shapes=[
            pltpu.VMEM((2, 2, 4, 2, share, width), BF16),
            pltpu.VMEM((2, enc_rows, width), BF16),
            pltpu.VMEM((2 * rows, width), BF16),
            pltpu.VMEM((rows, width), BF16),
            pltpu.VMEM((2, rows, 192), BF16),
            pltpu.VMEM((2, keys, 384), BF16),
            pltpu.VMEM((2, 3, rows, keys), BF16),
            pltpu.VMEM((2, rows, 192), BF16),
            pltpu.VMEM((2, rows, 128), F32),
            pltpu.VMEM((rows, width), F32),
            pltpu.VMEM((2, rows, width), BF16),
            pltpu.VMEM((2, rows, width), BF16),
            pltpu.VMEM((2, 4, 2, share, width), BF16),
            pltpu.VMEM((width, rows), BF16),
            pltpu.VMEM((width, rows), BF16),
            pltpu.VMEM((width, keys), BF16),
            pltpu.VMEM((2, rows, keys), F32),
            pltpu.VMEM((2, rows, keys), BF16),
            pltpu.VMEM((384, keys), F32),
            pltpu.VMEM((rows, width), F32),
            pltpu.VMEM((rows, width), F32),
            pltpu.VMEM((keys, width), F32),
            pltpu.VMEM((heads, 8, diag), F32),
            pltpu.VMEM((rows, width), BF16),
            pltpu.VMEM((rows, width), BF16),
            pltpu.VMEM((2, enc_rows, width), BF16),
            pltpu.VMEM((enc_rows, width), BF16),
            pltpu.VMEM((8, diag), F32),
            pltpu.VMEM((C_RING, 4, share, width), BF16),
            pltpu.VMEM((TICKS, 2, 2, half_share, width), BF16),
            pltpu.VMEM((TICKS, 2, half_share, width), BF16),
            pltpu.VMEM((TICKS, share, width), BF16),
            pltpu.VMEM((2, 2, 2, half_share, width), BF16),
            pltpu.VMEM((2, 2, 2, half_share, width), F32),
            pltpu.VMEM((2, 2, half_share, width), BF16),
            pltpu.VMEM((2, 2, half_share, width), F32),
            pltpu.VMEM((2, share, width), BF16),
            pltpu.VMEM((3, 8, diag), F32),
            pltpu.VMEM((3, 8, diag), F32),
            pltpu.VMEM((parts, 8, diag), F32),
            pltpu.SemaphoreType.DMA((2, 2)),
            pltpu.SemaphoreType.DMA((6,)),
            pltpu.SemaphoreType.DMA((5, 2)),
            pltpu.SemaphoreType.DMA((2, 6, TICKS)),
            pltpu.SemaphoreType.REGULAR,
            pltpu.SemaphoreType.DMA((6,)),
            pltpu.SemaphoreType.DMA((6,)),
            pltpu.SemaphoreType.DMA((2,)),
            pltpu.SemaphoreType.DMA((2,)),
        ],
        compiler_params=pltpu.CompilerParams(
            collective_id=2, has_side_effects=True, vmem_limit_bytes=VMEM_BYTES
        ),
        name="backward",
    )(inputs, other, cotangent, gains, onehot, enc_all, packed, weights, *kept)
    if n_dp > 8:
        summed, small = across_groups(summed, small, n_dp)
    buckets_here = bias_table.shape[0]
    mine = lax.dynamic_slice_in_dim(small, 3 + z, 1, 0)[0]
    table_mine = jnp.stack(
        [mine[width : width + buckets_here], mine[width + 128 :][:buckets_here], mine[:buckets_here]],
        axis=1,
    )
    gs, gc = summed[0], summed[1]
    return (
        result,
        low(input_grad),
        low(encoder_grad),
        small[0, :width],
        gs[:, 384:576],
        gs[:, 0:192],
        gs[:, 192:384],
        gs[:, 576:768].T,
        table_mine,
        small[1, :width],
        gc[:, 384:576],
        gc[:, 0:192],
        gc[:, 192:384],
        gc[:, 576:768].T,
        small[2, :width],
        summed[2],
        summed[3].T,
    )


def solution(mesh):
    rows = P(("dp", "mp"), None)
    across, down = P(None, "mp"), P("mp", None)
    return jax.shard_map(
        body,
        mesh=mesh,
        in_specs=(
            rows, rows, rows, P("dp"), P(),
            P(), across, across, across, down, across,
            P(), across, across, across, down,
            P(), across, down,
        ),
        out_specs=(
            rows, rows, rows,
            P(), P("dp", "mp"), P("dp", "mp"), P("dp", "mp"), P("mp", "dp"), P(None, "mp"),
            P(), P("dp", "mp"), P("dp", "mp"), P("dp", "mp"), P("mp", "dp"),
            P(), P("dp", "mp"), P("mp", "dp"),
        ),
        check_vma=False,
    )
```

```python
import functools

import jax
import jax.numpy as jnp
from jax import lax
from jax.experimental import pallas as pl
from jax.experimental.pallas import tpu as pltpu
from jax.sharding import PartitionSpec as P

EPS = 1e-06
MASKED = -1e30
DH = 64
F32 = jnp.float32
BF16 = jnp.bfloat16
VMEM_BYTES = 62 << 20
ROOT = 0.7978845608028654
CUBE = 0.044715


def mm(a, b):
    return jnp.dot(a, b, preferred_element_type=F32)


def mm_nt(a, b):
    return lax.dot_general(a, b, (((1,), (1,)), ((), ())), preferred_element_type=F32)


def line_of(ref):
    return ref[...].reshape(1, ref.shape[0])


def low(v):
    return v.astype(BF16)


def flip(v):
    return jnp.transpose(v.astype(F32)).astype(BF16)


def norm_rows(v, gain):
    root = lax.rsqrt(jnp.mean(v * v, axis=-1, keepdims=True) + EPS)
    unit = v * root
    return unit * gain, unit, root


def norm_back(grad, v, gain):
    _, unit, root = norm_rows(v, gain)
    scaled = grad * gain
    back = root * (scaled - unit * jnp.mean(scaled * unit, axis=-1, keepdims=True))
    return back, jnp.sum(grad * unit, axis=0, keepdims=True)


def block(w, i, j, start=0, stop=None):
    part = w[i, j]
    part = part.reshape(part.shape[0] * part.shape[1] * part.shape[2], part.shape[3])
    return part[start:stop]


def half_of_sequence(halves):
    return lax.rem(lax.axis_index("mp"), halves)


def chunks(rows, step):
    return [(r, min(step, rows - r)) for r in range(0, rows, step)]


MESH_ID = pl.DeviceIdType.MESH


def places():
    d = lax.axis_index("dp")
    z = lax.axis_index("mp")
    lo = lax.rem(d, 8)
    core = lax.rem(lo, 2)
    x = lax.rem(lax.div(lo, 2), 2)
    y = lax.div(lo, 4)
    d_core = d + 1 - 2 * core
    d_x = d + 2 - 4 * x
    d_y = d + 4 - 8 * y
    return d, z, core, x, y, d_core, d_x, d_y


def peer(k):
    d = lax.axis_index("dp")
    lo = lax.rem(d, 8)
    return d - lo + lax.rem(lo + k, 8)


def greet(z_parts, everyone):
    d, z, _, _, _, d_core, d_x, d_y = places()
    barrier = pltpu.get_barrier_semaphore()
    near = [peer(k) for k in range(1, 8)] if everyone else [d_core, d_x, d_y]
    for who in near:
        pl.semaphore_signal(barrier, inc=1, device_id=(who, z), device_id_type=MESH_ID)
    for step in range(1, z_parts):
        pl.semaphore_signal(
            barrier, inc=1, device_id=(d, lax.rem(z + step, z_parts)), device_id_type=MESH_ID
        )
    return lambda: pl.semaphore_wait(barrier, len(near) + z_parts - 1)


def remote(src, dst, send, recv, who):
    return pltpu.make_async_remote_copy(
        src_ref=src, dst_ref=dst, send_sem=send, recv_sem=recv, device_id=who, device_id_type=MESH_ID
    )


class Gather:
    parts_of_group = 3
    chunks = 12
    ahead = 6

    def __init__(self, mine, wg, z_send, z_recv, s_send, s_recv):
        self.mine, self.wg = mine, wg
        self.z_sems, self.s_sems = (z_send, z_recv), (s_send, s_recv)
        self.parts = wg.shape[1]
        self.place = places()

    def rows(self, k):
        some = self.wg.shape[4] // self.parts_of_group
        return k // self.parts_of_group, pl.ds((k % self.parts_of_group) * some, some)

    def z_copy(self, k, step):
        d, z, core, x, y, *_ = self.place
        yx = 2 * y + x
        g, rows = self.rows(k)
        return remote(
            self.mine.at[g, 0, yx, core, rows],
            self.wg.at[g, self.parts - step, yx, core, rows],
            self.z_sems[0].at[k, step - 1],
            self.z_sems[1].at[k, step - 1],
            (d, lax.rem(z + step, self.parts)),
        )

    def s_copy(self, k, n):
        d, z, core, x, y, d_core, d_x, d_y = self.place
        rest = pl.ds(1, self.parts - 1)
        g, rows = self.rows(k)
        width = self.wg.shape[5]
        if n < 2:
            ref = self.wg.at[g, rest, 2 * y + x, core, rows]
            who = (d_x, d_y)[n]
        elif n == 2:
            ref = self.wg.at[g, rest, 2 * y + 1 - x, core, rows, pl.ds(0, width // 2)]
            who = d_y
        elif n == 3:
            ref = self.wg.at[g, rest, 2 * (1 - y) + x, core, rows, pl.ds(width // 2, width // 2)]
            who = d_x
        else:
            ref = self.wg.at[g, rest, :, core, rows]
            who = d_core
        return remote(ref, ref, self.s_sems[0].at[k, n], self.s_sems[1].at[k, n], (who, z))

    def z_start(self, k):
        for step in range(1, self.parts):
            self.z_copy(k, step).start()

    def tick(self, k):
        if k < self.chunks:
            for step in range(1, self.parts):
                self.z_copy(k, step).wait_recv()
            self.s_copy(k, 0).start()
            self.s_copy(k, 1).start()
            if k + self.ahead < self.chunks:
                self.z_start(k + self.ahead)
        if 0 <= k - 1 < self.chunks:
            self.s_copy(k - 1, 0).wait_recv()
            self.s_copy(k - 1, 2).start()
            self.s_copy(k - 1, 1).wait_recv()
            self.s_copy(k - 1, 3).start()
        if 0 <= k - 2 < self.chunks:
            self.s_copy(k - 2, 2).wait_recv()
            self.s_copy(k - 2, 3).wait_recv()
            self.s_copy(k - 2, 4).start()

    def arrived(self, g):
        for k in range(self.parts_of_group * g, self.parts_of_group * (g + 1)):
            self.s_copy(k, 4).wait_recv()

    def sent(self):
        for k in range(self.chunks):
            for step in range(1, self.parts):
                self.z_copy(k, step).wait_send()
            for n in range(5):
                self.s_copy(k, n).wait_send()


C_RING = 4
KEEP = 4
Z_RING = 6
TICKS = 16


class Scatter:
    def __init__(self, bufs, sems, credit):
        (
            self.c_in, self.a_in, self.b_in, self.z_in,
            self.a_out, self.a_keep, self.b_out, self.b_keep, self.z_out, self.total,
        ) = bufs
        self.sems, self.credit = sems, credit
        self.parts = 4
        self.share = self.z_out.shape[1]
        self.place = places()

    def block(self, t):
        if t < 6:
            return 3 - t % 2, 1 + t // 2
        if t < 14:
            return 1 - (t - 6) // 4, (t - 5) % 4
        return 17 - t, 0

    def copy(self, k, t, src, dst, who):
        return remote(src, dst, self.sems.at[0, k, t], self.sems.at[1, k, t], who)

    def c_copy(self, t, src):
        z, d_core = self.place[1], self.place[5]
        return self.copy(0, t, src, self.c_in.at[t % C_RING], (d_core, z))

    def a_copy(self, t, q):
        _, z, *_, d_x, d_y = self.place
        src, dst = self.a_out.at[t % 2, q], self.a_in.at[t, q]
        return self.copy(1 + q, t, src, dst, ((d_x, d_y)[q], z))

    def b_copy(self, t, q):
        _, z, *_, d_x, d_y = self.place
        src, dst = self.b_out.at[t % 2, q], self.b_in.at[t, q]
        return self.copy(3 + q, t, src, dst, ((d_y, d_x)[q], z))

    def z_copy(self, t):
        d, z = self.place[:2]
        who = (d, lax.rem(z + self.block(t)[1], self.parts))
        return self.copy(5, t, self.z_out.at[t % Z_RING], self.z_in.at[t], who)

    def rows(self, q):
        return pl.ds(q * (self.share // 2), self.share // 2)

    def c_start(self, t, src):
        if t >= C_RING:
            pl.semaphore_wait(self.credit, 1)
        self.c_copy(t, src).start()

    def a_start(self, t, mine, src):
        _, z, _, x, y, d_core, *_ = self.place
        slot, ring, held = t % 2, t % C_RING, t % KEEP
        if t >= 2:
            self.a_copy(t - 2, 0).wait_send()
            self.a_copy(t - 2, 1).wait_send()
        self.c_copy(t, src).wait_recv()
        for q in range(2):
            rows = self.rows(q)
            for k in range(2):
                send = (2 * k + 1 - x, 2 * (1 - y) + k)[q]
                self.a_out[slot, q, k] = low(
                    mine[send, rows].astype(F32) + self.c_in[ring, send, rows].astype(F32)
                )
            self.a_copy(t, q).start()
        for q in range(2):
            rows = self.rows(q)
            for k in range(2):
                keep = (2 * k + x, 2 * y + k)[q]
                self.a_keep[held, q, k] = low(
                    mine[keep, rows].astype(F32) + self.c_in[ring, keep, rows].astype(F32)
                )
        if t < TICKS - C_RING:
            pl.semaphore_signal(
                self.credit, inc=1, device_id=(d_core, z), device_id_type=MESH_ID
            )

    def b_start(self, t):
        _, _, _, x, y, *_ = self.place
        slot, held = t % 2, t % KEEP
        if t >= 2:
            self.b_copy(t - 2, 0).wait_send()
            self.b_copy(t - 2, 1).wait_send()
        for q in range(2):
            keep = (y, x)[q]
            send = 1 - keep
            self.a_copy(t, q).wait_recv()
            self.b_out[slot, q] = low(
                self.a_keep[held, q, send].astype(F32) + self.a_in[t, q, send].astype(F32)
            )
            self.b_copy(t, q).start()
            self.b_keep[held, q] = self.a_keep[held, q, keep].astype(F32) + self.a_in[
                t, q, keep
            ].astype(F32)

    def z_start(self, t):
        slot, held = t % Z_RING, t % KEEP
        g, r = self.block(t)
        if t >= Z_RING and self.block(t - Z_RING)[1] > 0:
            self.z_copy(t - Z_RING).wait_send()
        for q in range(2):
            self.b_copy(t, q).wait_recv()
            done = self.b_keep[held, q] + self.b_in[t, q].astype(F32)
            if r == 0:
                self.total[g, self.rows(q)] = done
            else:
                self.z_out[slot, self.rows(q)] = low(done)
        if r > 0:
            self.z_copy(t).start()

    def finish(self):
        for t in range(TICKS - 2, TICKS):
            for q in range(2):
                self.a_copy(t, q).wait_send()
                self.b_copy(t, q).wait_send()
        for t in range(TICKS):
            g, r = self.block(t)
            if r > 0:
                if t >= TICKS - Z_RING:
                    self.z_copy(t).wait_send()
                self.z_copy(t).wait_recv()
                self.total[g] += self.z_in[t].astype(F32)


class Sum:
    def __init__(self, near, far, send, recv):
        self.near, self.far = near, far
        self.send, self.recv = send, recv
        self.place = places()
        self.lo = lax.rem(self.place[0], 8)

    def near_copy(self, k):
        ref = self.near.at[self.lo]
        return remote(
            ref, ref, self.send.at[k - 1], self.recv.at[k - 1], (peer(k), self.place[1])
        )

    def far_copy(self, k):
        d, z = self.place[:2]
        ref = self.far.at[z]
        who = (d, lax.rem(z + k, self.far.shape[0]))
        return remote(ref, ref, self.send.at[6 + k], self.recv.at[6 + k], who)

    def start(self, value):
        self.near[self.lo] = value
        for k in range(1, 8):
            self.near_copy(k).start()

    def turn(self):
        for k in range(1, 8):
            self.near_copy(k).wait_send()
            sender = lax.rem(self.lo + 8 - k, 8)
            ref = self.near.at[sender]
            remote(
                ref, ref, self.send.at[k - 1], self.recv.at[k - 1], (peer(8 - k), self.place[1])
            ).wait_recv()
        value = self.near[0]
        for k in range(1, 8):
            value = value + self.near[k]
        self.far[self.place[1]] = value
        for k in range(1, self.far.shape[0]):
            self.far_copy(k).start()

    def result(self):
        d, z = self.place[:2]
        parts = self.far.shape[0]
        for k in range(1, parts):
            self.far_copy(k).wait_send()
            sender = lax.rem(z + parts - k, parts)
            ref = self.far.at[sender]
            remote(
                ref, ref, self.send.at[6 + k], self.recv.at[6 + k], (d, sender)
            ).wait_recv()
        value = self.far[0]
        for k in range(1, parts):
            value = value + self.far[k]
        return value


def forward_kernel(
    halves,
    len_ref, x_ref, enc_own, gain1, gain2, gain3, buckets_ref, table_in,
    sk, sv, sq, so, ck, cv, cq, co, fi, fo,
    result_ref, w_hbm, xa_out, enc_out, onehot_out,
    n1_out, q1_out, kv1_out, p1_out, o1_out, l1_out, x1_out,
    n2_out, q2_out, kv2_out, p2_out, o2_out, l2_out, x2_out,
    n3_out, hid_out, slope_out,
    w, enc, diag, mask, s_buf,
    n1, q1, kv1, p_buf, o1, x1, n2, q2, kv2, o2, x2, n3, hid, slope, l1, l2,
    acc, xa, table_own, table_far,
    w_sem, in_sem, own_sem, out_sem, p_sem,
    z_send, z_recv, s_send, s_recv, e_send, e_recv,
):
    rows, width = x_ref.shape
    parts = w.shape[1]
    half = half_of_sequence(halves)
    d, z_me = places()[:2]
    mate = z_me + 1 - 2 * half
    entered = greet(parts, False)

    def fetch(g, r):
        return pltpu.make_async_copy(w_hbm.at[g, r], w.at[g, r], w_sem.at[g, r])

    enc_here = pltpu.make_async_copy(enc_own, enc.at[half], in_sem.at[4])

    def own(g):
        if g == 2:
            return [pltpu.make_async_copy(fi, w.at[2, 0], in_sem.at[2])]
        if g == 3:
            return [pltpu.make_async_copy(fo, w.at[3, 0], in_sem.at[3])]
        refs = ((sk, sv, sq, so), (ck, cv, cq, co))[g]
        return [
            pltpu.make_async_copy(ref, w.at[g, 0, k], own_sem.at[g, k])
            for k, ref in enumerate(refs)
        ]

    for g in range(4):
        for copy in own(g):
            copy.start()
    enc_here.start()

    saves = []

    def saving(k):
        src, dst = saves[k]()
        return pltpu.make_async_copy(src, dst, out_sem.at[k])

    def save(src, dst):
        saves.append((lambda: (src, dst)) if not callable(src) else lambda: (src(), dst()))
        saving(len(saves) - 1).start()

    def pack(g):
        for copy in own(g):
            copy.wait()
        save(lambda: w.at[g, 0], lambda: w_hbm.at[g, 0])

    pack(0)
    entered()
    gather = Gather(w, w_hbm, z_send, z_recv, s_send, s_recv)
    x_copy = remote(x_ref, xa, e_send.at[0], e_recv.at[0], (d, mate))
    enc_copy = remote(enc_own, enc.at[half], e_send.at[1], e_recv.at[1], (d, mate))
    tables = [
        remote(
            table_own, table_far.at[parts - step], e_send.at[1 + step], e_recv.at[1 + step],
            (d, lax.rem(z_me + step, parts)),
        )
        for step in range(1, parts)
    ]
    gather.z_start(0)
    gather.z_start(1)

    @pl.when(half == 0)
    def _():
        x_copy.start()

    gather.z_start(2)
    table_own[...] = jnp.zeros_like(table_own)
    table_own[0 : table_in.shape[0], 0 : table_in.shape[1]] = table_in[...]
    for copy in tables:
        copy.start()
    pack(1)
    pack(2)
    pack(3)
    for k in range(3, gather.ahead):
        gather.z_start(k)

    n1[rows : 2 * rows, :] = low(norm_rows(x_ref[...].astype(F32), line_of(gain1))[0])
    gather.tick(0)

    slots = buckets_ref.shape[0]
    span = onehot_out.shape[1]
    here = jnp.concatenate(
        [line_of(buckets_ref), jnp.full((1, span - slots), -1, jnp.int32)], axis=1
    )
    kinds = onehot_out.shape[0]
    which = lax.broadcasted_iota(jnp.int32, (kinds, span), 0) == here
    plain = jnp.where(which, 1.0, 0.0).astype(BF16)
    for start in range(0, span, 128):
        offset = lax.broadcasted_iota(jnp.int32, (span, 128), 0)
        column = lax.broadcasted_iota(jnp.int32, (span, 128), 1) + start
        turn = (offset + column == rows) | (offset + column == rows + span)
        onehot_out[:, start : start + 128] = mm(plain, jnp.where(turn, 1.0, 0.0).astype(BF16))

    length = len_ref[lax.div(z_me, halves)]
    i = lax.broadcasted_iota(jnp.int32, mask.shape, 0)
    c = lax.broadcasted_iota(jnp.int32, mask.shape, 1)
    own = c - rows
    limit = jnp.where(half > 0, length, 0)
    ok = ((own < 0) & (c < limit)) | ((own >= 0) & (own <= i) & (own + half * rows < length))
    mask[...] = jnp.where(ok, 0.0, MASKED)
    gather.tick(1)
    enc_copy.start()
    for copy in tables:
        copy.wait()
    for r in range(parts):
        table = table_own[...] if r == 0 else table_far[r]
        diag[r] = jnp.dot(
            table[:, 0 : onehot_out.shape[0]],
            onehot_out[...],
            precision=lax.Precision.HIGHEST,
            preferred_element_type=F32,
        )

    @pl.when(half == 0)
    def _():
        x_copy.wait_send()
        xa[...] = x_ref[...]

    @pl.when(half == 1)
    def _():
        x_copy.wait_recv()

    n1[0:rows, :] = low(norm_rows(xa[...].astype(F32), line_of(gain1))[0])
    save(n1, n1_out)
    save(xa, xa_out)

    def take(g):
        gather.arrived(g)
        for r in range(1, parts):
            fetch(g, r).start()

    def ready(g, r):
        @pl.when(r > 0)
        def _():
            fetch(g, r).wait()

    def after(r, **hooks):
        for name, hook in hooks.items():
            pl.when(r == int(name[1:]))(hook)

    p_outs = (p1_out, p2_out)
    p_keys = (2 * rows, 2 * enc.shape[1])

    def p_save(phase, r):
        slot = lax.rem(r, 2)
        return pltpu.make_async_copy(
            p_buf.at[slot, :, :, 0 : p_keys[phase]],
            p_outs[phase].at[pl.ds(3 * r, 3)],
            p_sem.at[phase, slot],
        )

    def heads(phase, r, q, kv, o, l):
        keys = p_keys[phase]
        slot = lax.rem(r, 2)

        @pl.when(r >= 2)
        def _():
            p_save(phase, r - 2).wait()

        if phase == 1:

            @pl.when(r < 2)
            def _():
                p_save(0, r + 2).wait()

        outs = []
        for j in range(3):
            q_h = q[r, :, DH * j : DH * (j + 1)]
            k_h = kv[r, :, DH * j : DH * (j + 1)]
            v_h = kv[r, :, DH * (3 + j) : DH * (4 + j)]
            s_buf[j % 2, :, 0:keys] = mm_nt(q_h, k_h)
            for a, n in chunks(rows, 32):
                s = s_buf[j % 2, a : a + n, 0:keys]
                if phase == 0:
                    line = jnp.broadcast_to(diag[r, j : j + 1, :], (n, diag.shape[2]))
                    grid = pltpu.roll(line, a, 1, stride=1, stride_axis=0)
                    s = s + grid[:, 0:keys] + mask[a : a + n, :]
                top = jnp.max(s, axis=1, keepdims=True)
                p_buf[slot, j, a : a + n, 0:keys] = low(jnp.exp(s - top))
            wide = jnp.concatenate([v_h, jnp.ones_like(v_h)], axis=1)
            mixed = mm(p_buf[slot, j, :, 0:keys], wide)
            outs.append(low(mixed[:, 0:DH] / mixed[:, DH : 2 * DH]))
            l[r, :, 32 * j : 32 * (j + 1)] = mixed[:, DH : DH + 32]
        o[r] = jnp.concatenate(outs, axis=1)
        p_save(phase, r).start()

    acc[...] = x_ref[...].astype(F32)

    def self_step(r, carry):
        ready(0, r)
        kv1[r] = low(mm_nt(n1[...], block(w, 0, r, 0, 384)))
        q1[r] = low(mm_nt(n1[rows : 2 * rows, :], block(w, 0, r, 384, 576)))
        heads(0, r, q1, kv1, o1, l1)
        acc[...] += mm(o1[r], block(w, 0, r, 576, 768))

        def first():
            for k in (2, 3, 4):
                gather.tick(k)
            take(0)

        after(r, r0=first, r1=lambda: gather.tick(5), r2=lambda: gather.tick(6), r3=lambda: gather.tick(7))
        return carry

    lax.fori_loop(0, parts, self_step, 0)
    for src, dst in ((q1, q1_out), (kv1, kv1_out), (o1, o1_out), (l1, l1_out)):
        save(src, dst)
    x1[...] = acc[...]
    n2[...] = low(norm_rows(acc[...], line_of(gain2))[0])
    save(x1, x1_out)
    save(n2, n2_out)
    enc_copy.wait()
    enc_here.wait()
    save(enc, enc_out)
    keys = 2 * enc.shape[1]

    def cross_step(r, carry):
        ready(1, r)
        kv2[r] = low(mm_nt(enc[...].reshape(keys, width), block(w, 1, r, 0, 384)))
        q2[r] = low(mm_nt(n2[...], block(w, 1, r, 384, 576)))
        heads(1, r, q2, kv2, o2, l2)
        acc[...] += mm(o2[r], block(w, 1, r, 576, 768))

        def first():
            gather.tick(8)
            take(1)

        after(r, r0=first, r1=lambda: gather.tick(9), r2=lambda: gather.tick(10), r3=lambda: gather.tick(11))
        return carry

    lax.fori_loop(0, parts, cross_step, 0)
    for src, dst in ((q2, q2_out), (kv2, kv2_out), (o2, o2_out), (l2, l2_out)):
        save(src, dst)
    x2[...] = acc[...]
    n3[...] = low(norm_rows(acc[...], line_of(gain3))[0])
    save(x2, x2_out)
    save(n3, n3_out)

    def inner_step(r, carry):
        ready(2, r)
        for a, n in chunks(rows, 64):
            v = mm(n3[a : a + n, :], block(w, 2, r))
            sq = v * v
            t = jnp.tanh(v * (ROOT + ROOT * CUBE * sq))
            cdf = 0.5 + 0.5 * t
            hid[r, a : a + n, :] = low(v * cdf)
            slope[r, a : a + n, :] = low(
                cdf + 0.5 * v * (1.0 - t * t) * (ROOT + 3.0 * ROOT * CUBE * sq)
            )
        after(r, r0=lambda: take(2), r1=lambda: gather.tick(12), r3=lambda: gather.tick(13))
        return carry

    lax.fori_loop(0, parts, inner_step, 0)
    save(hid, hid_out)
    save(slope, slope_out)

    def outer_step(r, carry):
        ready(3, r)
        acc[...] += mm(hid[r], block(w, 3, r))
        after(r, r0=lambda: take(3))
        return carry

    lax.fori_loop(0, parts, outer_step, 0)
    result_ref[...] = low(acc[...])
    for k in range(len(saves)):
        saving(k).wait()
    for r in (parts - 2, parts - 1):
        p_save(1, r).wait()
    gather.sent()


def backward_kernel(
    x_ref, xa_ref, cot_ref, gain1, gain2, gain3, onehot_ref, enc_hbm, w_hbm,
    n1_hbm, q1_hbm, kv1_hbm, p1_hbm, o1_hbm, l1_hbm, x1_hbm,
    n2_hbm, q2_hbm, kv2_hbm, p2_hbm, o2_hbm, l2_hbm, x2_hbm,
    n3_hbm, hid_hbm, slope_hbm,
    total_out, small_out, dx_out, denc_out, g_hbm,
    w, enc, nbuf, n2, q_in, kv_in, p_in, o_in, l_in, x_in, hid, slope,
    g_buf, l_buf, rows_t, rows_t2, keys_t, dp_buf, ds_buf, dkv_t, dn, acc, enc_acc, diag_acc,
    dxa, dxa_in, denc, denc_in, small,
    c_in, a_in, b_in, z_in, a_out, a_keep, b_out, b_keep, z_out, s_near, s_far,
    w_sem, one_sem, ring_sem, store_sem, load_sem,
    sems, credit, s_send, s_recv, e_send, e_recv,
):
    rows, width_all = x_ref.shape
    parts = w_hbm.shape[1]
    place = places()
    d, z_me, core = place[:3]
    half = lax.rem(z_me, 2)
    mate = z_me + 1 - 2 * half
    keys = 2 * enc.shape[1]
    own_keys = 2 * rows

    singles = [(n3_hbm, nbuf.at[0:rows]), (x2_hbm, x_in), (n2_hbm, n2), (enc_hbm, enc),
               (x1_hbm, x_in), (n1_hbm, nbuf)]

    def single(k):
        return pltpu.make_async_copy(*singles[k], one_sem.at[k])

    def which(i):
        return lax.rem(i + 1, parts)

    def streams(phase, i):
        slot, r = lax.rem(i, 2), which(i)
        if phase == 0:
            pairs = [(hid_hbm.at[r], hid.at[slot]), (slope_hbm.at[r], slope.at[slot])]
        else:
            q, kv, p, o, l = (
                (q2_hbm, kv2_hbm, p2_hbm, o2_hbm, l2_hbm),
                (q1_hbm, kv1_hbm, p1_hbm, o1_hbm, l1_hbm),
            )[phase - 1]
            n = (keys, own_keys)[phase - 1]
            pairs = [
                (q.at[r], q_in.at[slot]),
                (kv.at[r], kv_in.at[slot, 0:n]),
                (p.at[pl.ds(3 * r, 3)], p_in.at[slot, :, :, 0:n]),
                (o.at[r], o_in.at[slot]),
                (l.at[r], l_in.at[slot]),
            ]
        return [
            pltpu.make_async_copy(src, dst, ring_sem.at[k, slot])
            for k, (src, dst) in enumerate(pairs)
        ]

    def weight(g, i, k):
        slot = lax.rem(i, 2)
        return pltpu.make_async_copy(w_hbm.at[g, which(i)], w.at[slot, k], w_sem.at[slot, k])

    groups = ((3, 2), (1,), (0,))

    def prefetch(phase, r):
        for k, g in enumerate(groups[phase]):
            weight(g, r, k).start()
        for copy in streams(phase, r):
            copy.start()

    def turn(phase, r):
        for k, g in enumerate(groups[phase]):
            weight(g, r, k).wait()
        for copy in streams(phase, r):
            copy.wait()

        @pl.when(r + 1 < parts)
        def _():
            prefetch(phase, r + 1)

        if phase < 2:

            @pl.when(r + 1 == parts)
            def _():
                prefetch(phase + 1, 0)

    entered = greet(parts, True)
    prefetch(0, 0)
    for k in range(4):
        single(k).start()

    scatter = Scatter(
        (c_in, a_in, b_in, z_in, a_out, a_keep, b_out, b_keep, z_out, total_out), sems, credit
    )
    sums = Sum(s_near, s_far, s_send, s_recv)
    dxa_copy = remote(dxa, dxa_in, e_send.at[0], e_recv.at[0], (d, mate))
    denc_copy = remote(denc.at[1 - half], denc_in, e_send.at[1], e_recv.at[1], (d, mate))

    def put(t, value, start=0):
        shape = g_buf.shape[1:4] + (value.shape[1],)
        g_buf[lax.rem(t, 2), :, :, :, start : start + value.shape[1]] = value.reshape(shape)

    def store(t):
        slot = lax.rem(t, 2)
        return pltpu.make_async_copy(g_buf.at[slot], g_hbm.at[t], store_sem.at[slot])

    def away(t):
        return g_hbm.at[t, :, 1 - core]

    def load(t):
        slot = t % 2
        return pltpu.make_async_copy(g_hbm.at[t, :, core], l_buf.at[slot], load_sem.at[slot])

    def leave(t):
        if t < TICKS:
            scatter.c_start(t, away(t))
            load(t).start()
        if t >= 1:
            load(t - 1).wait()
            scatter.a_start(t - 1, l_buf.at[(t - 1) % 2], away(t - 1))

    def tick(t):
        leave(t)
        if t >= 3:
            scatter.b_start(t - 3)
        if t >= 5:
            scatter.z_start(t - 5)

    b, z = scatter.b_start, scatter.z_start

    def at(i, step, *moves):
        @pl.when(i == step)
        def _():
            for move, t in moves:
                move(t)

    def keep_sum(g, value):
        part = width_all // 2
        small[2 * g : 2 * g + 1, :] = value[:, 0:part]
        small[2 * g + 1 : 2 * g + 2, :] = value[:, part:]

    rows_t[...] = flip(cot_ref[...])
    single(0).wait()
    rows_t2[...] = flip(nbuf[0:rows, :])
    acc[...] = jnp.zeros_like(acc)

    def feed_step(i, carry):
        turn(0, i)
        slot = lax.rem(i, 2)
        t = 2 * i + 8 * lax.div(i, 3)
        put(t, low(mm(rows_t[...], hid[slot])))
        store(t).start()
        dh = low(mm_nt(cot_ref[...], block(w, slot, 0)))
        slope[slot] = low(dh.astype(F32) * slope[slot].astype(F32))
        store(t).wait()

        @pl.when(i == 0)
        def _():
            entered()
            tick(0)

        put(t + 1, low(mm(rows_t2[...], slope[slot])))
        store(t + 1).start()
        acc[...] += mm_nt(slope[slot], block(w, slot, 1))
        store(t + 1).wait()
        at(i, 1, (tick, 1))
        at(i, 2, (tick, 2))
        at(i, 3, (tick, 3))
        return carry

    lax.fori_loop(0, parts, feed_step, 0)
    single(1).wait()
    back, sum3 = norm_back(acc[...], x_in[...], line_of(gain3))
    dn[...] = cot_ref[...].astype(F32) + back
    single(4).start()
    single(5).start()
    small[...] = jnp.zeros_like(small)
    keep_sum(2, sum3)

    def heads_back(r, do, n, with_diag, between):
        slot = lax.rem(r, 2)
        q, kv, o = q_in[slot], kv_in.at[slot], o_in[slot].astype(F32)
        do_all = []
        delta_all = []
        for j in range(3):
            do_h = do[:, DH * j : DH * (j + 1)]
            inv = 1.0 / l_in[slot, :, 32 * j : 32 * j + 1]
            o_h = o[:, DH * j : DH * (j + 1)]
            delta_all.append(jnp.sum(do_h * o_h * inv, axis=1, keepdims=True))
            do_all.append(do_h * inv)
        do_t = low(jnp.transpose(jnp.concatenate(do_all, axis=1)))
        q_t = flip(q)
        dq = []
        for j in range(3):
            p_h = p_in.at[slot, j]
            k_h = kv[0:n, DH * j : DH * (j + 1)]
            v_h = kv[0:n, DH * (3 + j) : DH * (4 + j)]
            dp_buf[j % 2, :, 0:n] = mm_nt(low(do_all[j]), v_h)
            total = None
            for s, m in chunks(rows, 32):
                ds = low(
                    p_h[s : s + m, 0:n].astype(F32)
                    * (dp_buf[j % 2, s : s + m, 0:n] - delta_all[j][s : s + m, :])
                )
                ds_buf[j % 2, s : s + m, 0:n] = ds
                if with_diag:
                    width = diag_acc.shape[2]
                    wide = jnp.concatenate([ds.astype(F32), jnp.zeros((m, width - n), F32)], axis=1)
                    for b in range(0, m, 8):
                        turned = pltpu.roll(wide[b : b + 8, :], (width - s - b) % width, 1)
                        total = turned if total is None else total + turned
            if with_diag:
                diag_acc[which(r) * 3 + j] = total
            ds_h = ds_buf[j % 2, :, 0:n]
            dq.append(low(mm(ds_h, k_h)))
            dkv_t[DH * j : DH * (j + 1), 0:n] = mm(q_t[DH * j : DH * (j + 1), :], ds_h)
            dkv_t[DH * (3 + j) : DH * (4 + j), 0:n] = mm(
                do_t[DH * j : DH * (j + 1), :], p_h[:, 0:n]
            )
            if j == 1:
                between()
        return jnp.concatenate(dq, axis=1), low(jnp.transpose(dkv_t[:, 0:n]))

    def attention_step(phase, n, r, middle):
        slot = lax.rem(r, 2)
        t = 2 + 4 * phase + r
        turn(phase, r)
        do = low(mm_nt(low(dn[...]), block(w, slot, 0, 576, 768))).astype(F32)
        dq, dkv = heads_back(r, do, n, phase == 2, lambda: middle(r))
        put(t, low(mm(keys_t[:, 0:n], dkv)))
        both = [low(mm(rows_t2[...], dq)), low(mm(rows_t[...], o_in[slot]))]
        put(t, jnp.concatenate(both, axis=1), 384)
        store(t).start()
        acc[...] += mm(dq, block(w, slot, 0, 384, 576))
        enc_acc[0:n, :] += mm(dkv, block(w, slot, 0, 0, 384))
        store(t).wait()

    rows_t[...] = flip(low(dn[...]))
    single(2).wait()
    single(3).wait()
    rows_t2[...] = flip(n2[...])
    keys_t[...] = flip(enc[...].reshape(keys, width_all))
    acc[...] = jnp.zeros_like(acc)
    enc_acc[...] = jnp.zeros_like(enc_acc)

    def cross_step(r, carry):
        def middle(r):
            at(r, 0, (tick, 4))
            at(r, 3, (tick, 8))

        attention_step(1, keys, r, middle)
        at(r, 0, (tick, 5))
        at(r, 1, (tick, 6))
        at(r, 2, (tick, 7))
        at(r, 3, (tick, 9))
        return carry

    lax.fori_loop(0, parts, cross_step, 0)
    denc[...] = low(enc_acc[...]).reshape(denc.shape)
    denc_copy.start()
    single(4).wait()
    back, sum2 = norm_back(acc[...], x_in[...], line_of(gain2))
    dn[...] += back
    keep_sum(1, sum2)

    rows_t[...] = flip(low(dn[...]))
    single(5).wait()
    rows_t2[...] = flip(nbuf[rows : 2 * rows, :])
    keys_t[:, 0:own_keys] = flip(nbuf[...])
    acc[...] = jnp.zeros_like(acc)
    enc_acc[0:own_keys, :] = jnp.zeros((own_keys, width_all), F32)

    def self_step(r, carry):
        def middle(r):
            at(r, 1, (b, 8), (z, 6))
            at(r, 2, (z, 8))

        attention_step(2, own_keys, r, middle)
        at(r, 0, (tick, 10))
        at(r, 1, (leave, 11), (b, 9), (z, 7))
        at(r, 2, (leave, 12), (b, 10), (z, 9))
        at(r, 3, (leave, 13), (b, 11), (z, 10))
        return carry

    lax.fori_loop(0, parts, self_step, 0)
    gain = line_of(gain1)
    back, sum1a = norm_back(enc_acc[0:rows, :], xa_ref[...].astype(F32), gain)
    dxa[...] = low(back)

    @pl.when(half == 1)
    def _():
        dxa_copy.start()

    leave(14)
    b(12)
    z(11)
    back, sum1 = norm_back(
        acc[...] + enc_acc[rows : 2 * rows, :], x_ref[...].astype(F32), gain
    )
    dn[...] += back
    keep_sum(0, sum1 + sum1a)
    width = diag_acc.shape[2]
    lines = []
    for r in range(parts):
        for j in range(3):
            part = diag_acc[3 * r + j]
            line = part[0:1, :]
            for k in range(1, 8):
                line = line + pltpu.roll(part[k : k + 1, :], width - k, 1)
            lines.append(line)
    lines.append(jnp.zeros((16 - len(lines), width), F32))
    table = lax.dot_general(
        jnp.concatenate(lines, axis=0),
        onehot_ref[...],
        (((1,), (1,)), ((), ())),
        precision=lax.Precision.HIGHEST,
        preferred_element_type=F32,
    )
    kinds = onehot_ref.shape[0]
    for r in range(parts):
        at = lax.rem(z_me + r, parts)
        for p in range(parts):

            @pl.when(at == p)
            def _(r=r, p=p):
                for j in range(3):
                    lane = kinds * (3 * p + j)
                    small[6:7, lane : lane + kinds] = table[3 * r + j : 3 * r + j + 1]

    leave(15)
    b(13)
    z(12)
    sums.start(small[...])
    leave(16)
    b(14)
    z(13)
    sums.turn()
    b(15)
    z(14)
    z(15)
    denc_copy.wait()
    denc_out[...] = low(denc[half].astype(F32) + denc_in[...].astype(F32))
    scatter.finish()
    small_out[...] = sums.result()

    @pl.when(half == 1)
    def _():
        dxa_copy.wait_send()
        dx_out[...] = low(dn[...])

    @pl.when(half == 0)
    def _():
        dxa_copy.wait_recv()
        dx_out[...] = low(dn[...] + dxa_in[...].astype(F32))

    for t in range(TICKS):
        scatter.c_copy(t, away(t)).wait_send()


def finish_kernel(
    result_in, dx, denc, total, small,
    result, input_grad, encoder_grad,
    g_gain1, gsq, gsk, gsv, gso, g_gain2, gcq, gck, gcv, gco, g_gain3, gfi, gfo, lines,
):
    result[...] = result_in[...]
    input_grad[...] = dx[...]
    encoder_grad[...] = denc[...]
    width = result.shape[1]
    for g, (k, v, q, o) in enumerate(((gsk, gsv, gsq, gso), (gck, gcv, gcq, gco))):
        k[...] = total[g, :, 0:192]
        v[...] = total[g, :, 192:384]
        q[...] = total[g, :, 384:576]
        o[...] = jnp.transpose(total[g, :, 576:768])
    gfi[...] = total[2]
    gfo[...] = total[3]
    for row, gain in enumerate((g_gain1, g_gain2, g_gain3)):
        part = small[2 * row : 2 * row + 2, :]
        gain[...] = jnp.concatenate([part[0:1], part[1:2]], axis=1).reshape(width)
    z = lax.axis_index("mp")
    for p in range(4):

        @pl.when(z == p)
        def _(p=p):
            kinds = lines.shape[1]
            for j in range(3):
                lane = kinds * (3 * p + j)
                lines[j : j + 1, :] = small[6:7, lane : lane + kinds]


def across(value, axis, n_dp):
    groups = n_dp // 8
    whole = lax.all_gather(value, "dp", axis=0, tiled=False)
    whole = whole.reshape(groups, 8, *value.shape).sum(0)
    whole = jnp.concatenate([whole[k] for k in range(8)], axis=axis)
    share = whole.shape[axis] // n_dp
    return lax.dynamic_slice_in_dim(whole, lax.axis_index("dp") * share, share, axis)


def across_small(value, n_dp):
    whole = lax.all_gather(value, "dp", axis=0, tiled=False)
    return whole.reshape(n_dp // 8, 8, *value.shape)[:, 0].sum(0)


def body(
    inputs, encoded, cotangent, lengths, buckets,
    self_gain, self_query, self_key, self_value, self_output, bias_table,
    cross_gain, cross_query, cross_key, cross_value, cross_output,
    feed_gain, feed_inner, feed_output_weight,
):
    rows, width = inputs.shape
    parts = lax.axis_size("mp")
    n_dp = lax.axis_size("dp")
    halves = parts // lengths.shape[0]
    assert halves == 2 and buckets.shape[0] == 2 * rows and parts == 4
    z = lax.axis_index("mp")
    enc_rows = encoded.shape[0]
    vmem = pl.BlockSpec(memory_space=pltpu.VMEM)
    smem = pl.BlockSpec(memory_space=pltpu.SMEM)
    hbm = pl.BlockSpec(memory_space=pl.ANY)
    sds = jax.ShapeDtypeStruct

    share = width // 8
    diag = 1024
    heads = 3 * parts
    keys = 2 * enc_rows
    gains = [self_gain, cross_gain, feed_gain]
    split = lambda v: v.reshape(2, share, width)
    whole = lambda v: v.reshape(4, 2, share, width)
    kinds = bias_table.shape[0]
    saved = [
        ((2 * rows, width), BF16),
        ((parts, rows, 192), BF16),
        ((parts, 2 * rows, 384), BF16),
        ((heads, rows, 2 * rows), BF16),
        ((parts, rows, 192), BF16),
        ((parts, rows, 128), F32),
        ((rows, width), F32),
        ((rows, width), BF16),
        ((parts, rows, 192), BF16),
        ((parts, keys, 384), BF16),
        ((heads, rows, keys), BF16),
        ((parts, rows, 192), BF16),
        ((parts, rows, 128), F32),
        ((rows, width), F32),
        ((rows, width), BF16),
        ((parts, rows, width), BF16),
        ((parts, rows, width), BF16),
    ]
    n1s, q1s, kv1s, p1s, o1s, l1s, x1s, n2s, q2s, kv2s, p2s, o2s, l2s, x2s, n3s, hids, slopes = [
        pltpu.VMEM(*s) for s in saved
    ]
    result, weights, other, enc_all, onehot, *kept = pl.pallas_call(
        functools.partial(forward_kernel, halves),
        out_shape=[
            sds((rows, width), BF16),
            sds((4, parts, 4, 2, share, width), BF16),
            sds((rows, width), BF16),
            sds((2, enc_rows, width), BF16),
            sds((kinds, diag), F32),
        ]
        + [sds(*s) for s in saved],
        in_specs=[smem, vmem, hbm] + [vmem] * 5 + [hbm] * 10,
        out_specs=[vmem, hbm, hbm, hbm, vmem] + [hbm] * len(saved),
        scratch_shapes=[
            pltpu.VMEM((4, parts, 4, 2, share, width), BF16),
            pltpu.VMEM((2, enc_rows, width), BF16),
            pltpu.VMEM((parts, 8, diag), F32),
            pltpu.VMEM((rows, 2 * rows), F32),
            pltpu.VMEM((2, rows, keys), F32),
            n1s, q1s, kv1s, pltpu.VMEM((2, 3, rows, keys), BF16), o1s, x1s,
            n2s, q2s, kv2s, o2s, x2s, n3s, hids, slopes,
            l1s, l2s,
            pltpu.VMEM((rows, width), F32),
            pltpu.VMEM((rows, width), BF16),
            pltpu.VMEM((8, 128), F32),
            pltpu.VMEM((parts, 8, 128), F32),
            pltpu.SemaphoreType.DMA((4, parts)),
            pltpu.SemaphoreType.DMA((5,)),
            pltpu.SemaphoreType.DMA((2, 4)),
            pltpu.SemaphoreType.DMA((6 + len(saved),)),
            pltpu.SemaphoreType.DMA((2, 2)),
            pltpu.SemaphoreType.DMA((Gather.chunks, parts - 1)),
            pltpu.SemaphoreType.DMA((Gather.chunks, parts - 1)),
            pltpu.SemaphoreType.DMA((Gather.chunks, 5)),
            pltpu.SemaphoreType.DMA((Gather.chunks, 5)),
            pltpu.SemaphoreType.DMA((5,)),
            pltpu.SemaphoreType.DMA((5,)),
        ],
        compiler_params=pltpu.CompilerParams(
            collective_id=1, has_side_effects=True, vmem_limit_bytes=VMEM_BYTES
        ),
        name="forward",
    )(
        lengths, inputs, encoded, *gains, buckets, bias_table.T,
        split(self_key.T), split(self_value.T), split(self_query.T), split(self_output),
        split(cross_key.T), split(cross_value.T), split(cross_query.T), split(cross_output),
        whole(feed_inner), whole(feed_output_weight),
    )

    half_share = share // 2
    summed, small, input_grad, encoder_grad, _ = pl.pallas_call(
        backward_kernel,
        out_shape=[
            sds((4, share, width), F32),
            sds((8, width // 2), F32),
            sds((rows, width), BF16),
            sds((enc_rows, width), BF16),
            sds((TICKS, 4, 2, share, width), BF16),
        ],
        in_specs=[vmem] * 7 + [hbm] * 19,
        out_specs=[vmem] * 4 + [hbm],
        scratch_shapes=[
            pltpu.VMEM((2, 2, 4, 2, share, width), BF16),
            pltpu.VMEM((2, enc_rows, width), BF16),
            pltpu.VMEM((2 * rows, width), BF16),
            pltpu.VMEM((rows, width), BF16),
            pltpu.VMEM((2, rows, 192), BF16),
            pltpu.VMEM((2, keys, 384), BF16),
            pltpu.VMEM((2, 3, rows, keys), BF16),
            pltpu.VMEM((2, rows, 192), BF16),
            pltpu.VMEM((2, rows, 128), F32),
            pltpu.VMEM((rows, width), F32),
            pltpu.VMEM((2, rows, width), BF16),
            pltpu.VMEM((2, rows, width), BF16),
            pltpu.VMEM((2, 4, 2, share, width), BF16),
            pltpu.VMEM((2, 4, share, width), BF16),
            pltpu.VMEM((width, rows), BF16),
            pltpu.VMEM((width, rows), BF16),
            pltpu.VMEM((width, keys), BF16),
            pltpu.VMEM((2, rows, keys), F32),
            pltpu.VMEM((2, rows, keys), BF16),
            pltpu.VMEM((384, keys), F32),
            pltpu.VMEM((rows, width), F32),
            pltpu.VMEM((rows, width), F32),
            pltpu.VMEM((keys, width), F32),
            pltpu.VMEM((heads, 8, diag), F32),
            pltpu.VMEM((rows, width), BF16),
            pltpu.VMEM((rows, width), BF16),
            pltpu.VMEM((2, enc_rows, width), BF16),
            pltpu.VMEM((enc_rows, width), BF16),
            pltpu.VMEM((8, width // 2), F32),
            pltpu.VMEM((C_RING, 4, share, width), BF16),
            pltpu.VMEM((TICKS, 2, 2, half_share, width), BF16),
            pltpu.VMEM((TICKS, 2, half_share, width), BF16),
            pltpu.VMEM((TICKS, share, width), BF16),
            pltpu.VMEM((2, 2, 2, half_share, width), BF16),
            pltpu.VMEM((KEEP, 2, 2, half_share, width), BF16),
            pltpu.VMEM((2, 2, half_share, width), BF16),
            pltpu.VMEM((KEEP, 2, half_share, width), F32),
            pltpu.VMEM((Z_RING, share, width), BF16),
            pltpu.VMEM((8, 8, width // 2), F32),
            pltpu.VMEM((parts, 8, width // 2), F32),
            pltpu.SemaphoreType.DMA((2, 2)),
            pltpu.SemaphoreType.DMA((6,)),
            pltpu.SemaphoreType.DMA((5, 2)),
            pltpu.SemaphoreType.DMA((2,)),
            pltpu.SemaphoreType.DMA((2,)),
            pltpu.SemaphoreType.DMA((2, 6, TICKS)),
            pltpu.SemaphoreType.REGULAR,
            pltpu.SemaphoreType.DMA((10,)),
            pltpu.SemaphoreType.DMA((10,)),
            pltpu.SemaphoreType.DMA((2,)),
            pltpu.SemaphoreType.DMA((2,)),
        ],
        compiler_params=pltpu.CompilerParams(
            collective_id=2, has_side_effects=True, vmem_limit_bytes=VMEM_BYTES
        ),
        name="backward",
    )(inputs, other, cotangent, *gains, onehot, enc_all, weights, *kept)

    f32 = lambda *shape: sds(shape, F32)
    outs = pl.pallas_call(
        finish_kernel,
        out_shape=[
            sds((rows, width), BF16), sds((rows, width), BF16), sds((enc_rows, width), BF16),
            f32(width), f32(share, 192), f32(share, 192), f32(share, 192), f32(192, share),
            f32(width), f32(share, 192), f32(share, 192), f32(share, 192), f32(192, share),
            f32(width), f32(share, width), f32(share, width), f32(3, kinds),
        ],
        in_specs=[vmem] * 5,
        out_specs=[vmem] * 17,
        name="finish",
    )(result, input_grad, encoder_grad, summed, small)
    result, input_grad, encoder_grad, *grads, lines = outs
    if n_dp > 8:
        axes = (None, 0, 0, 0, 1, None, 0, 0, 0, 1, None, 0, 0)
        grads = [
            across_small(value, n_dp) if axis is None else across(value, axis, n_dp)
            for value, axis in zip(grads, axes)
        ]
        lines = across_small(lines, n_dp)
    return (result, input_grad, encoder_grad, *grads[0:5], lines.T, *grads[5:-1], grads[-1].T)


def solution(mesh):
    rows = P(("dp", "mp"), None)
    across, down = P(None, "mp"), P("mp", None)
    return jax.shard_map(
        body,
        mesh=mesh,
        in_specs=(
            rows, rows, rows, P("dp"), P(),
            P(), across, across, across, down, across,
            P(), across, across, across, down,
            P(), across, down,
        ),
        out_specs=(
            rows, rows, rows,
            P(), P("dp", "mp"), P("dp", "mp"), P("dp", "mp"), P("mp", "dp"), P(None, "mp"),
            P(), P("dp", "mp"), P("dp", "mp"), P("dp", "mp"), P("mp", "dp"),
            P(), P("dp", "mp"), P("mp", "dp"),
        ),
        check_vma=False,
    )
```

```python
import functools

import jax
import jax.numpy as jnp
from jax import lax
from jax.experimental import pallas as pl
from jax.experimental.pallas import tpu as pltpu
from jax.sharding import PartitionSpec as P

EPS = 1e-06
MASKED = -1e30
DH = 64
F32 = jnp.float32
BF16 = jnp.bfloat16
VMEM_BYTES = 62 << 20
ROOT = 0.7978845608028654
CUBE = 0.044715


def mm(a, b):
    return jnp.dot(a, b, preferred_element_type=F32)


def mm_nt(a, b):
    return lax.dot_general(a, b, (((1,), (1,)), ((), ())), preferred_element_type=F32)


def line_of(ref):
    return ref[...].reshape(1, ref.shape[0])


def low(v):
    return v.astype(BF16)


def flip(v):
    return jnp.transpose(v.astype(F32)).astype(BF16)


def norm_rows(v, gain):
    root = lax.rsqrt(jnp.mean(v * v, axis=-1, keepdims=True) + EPS)
    unit = v * root
    return unit * gain, unit, root


def norm_back(grad, v, gain):
    _, unit, root = norm_rows(v, gain)
    scaled = grad * gain
    back = root * (scaled - unit * jnp.mean(scaled * unit, axis=-1, keepdims=True))
    return back, jnp.sum(grad * unit, axis=0, keepdims=True)


def block(w, i, j, start=0, stop=None):
    part = w[i, j]
    part = part.reshape(part.shape[0] * part.shape[1] * part.shape[2], part.shape[3])
    return part[start:stop]


def half_of_sequence(halves):
    return lax.rem(lax.axis_index("mp"), halves)


def chunks(rows, step):
    return [(r, min(step, rows - r)) for r in range(0, rows, step)]


MESH_ID = pl.DeviceIdType.MESH


def places():
    d = lax.axis_index("dp")
    z = lax.axis_index("mp")
    lo = lax.rem(d, 8)
    core = lax.rem(lo, 2)
    x = lax.rem(lax.div(lo, 2), 2)
    y = lax.div(lo, 4)
    d_core = d + 1 - 2 * core
    d_x = d + 2 - 4 * x
    d_y = d + 4 - 8 * y
    return d, z, core, x, y, d_core, d_x, d_y


def peer(k):
    d = lax.axis_index("dp")
    lo = lax.rem(d, 8)
    return d - lo + lax.rem(lo + k, 8)


def greet(z_parts, everyone):
    d, z, _, _, _, d_core, d_x, d_y = places()
    barrier = pltpu.get_barrier_semaphore()
    near = [peer(k) for k in range(1, 8)] if everyone else [d_core, d_x, d_y]
    for who in near:
        pl.semaphore_signal(barrier, inc=1, device_id=(who, z), device_id_type=MESH_ID)
    for step in range(1, z_parts):
        pl.semaphore_signal(
            barrier, inc=1, device_id=(d, lax.rem(z + step, z_parts)), device_id_type=MESH_ID
        )
    return lambda: pl.semaphore_wait(barrier, len(near) + z_parts - 1)


def remote(src, dst, send, recv, who):
    return pltpu.make_async_remote_copy(
        src_ref=src, dst_ref=dst, send_sem=send, recv_sem=recv, device_id=who, device_id_type=MESH_ID
    )


class Gather:
    parts_of_group = 3
    chunks = 12
    ahead = 6

    def __init__(self, mine, wg, z_send, z_recv, s_send, s_recv):
        self.mine, self.wg = mine, wg
        self.z_sems, self.s_sems = (z_send, z_recv), (s_send, s_recv)
        self.parts = wg.shape[1]
        self.place = places()

    def rows(self, k):
        some = self.wg.shape[4] // self.parts_of_group
        return k // self.parts_of_group, pl.ds((k % self.parts_of_group) * some, some)

    def z_copy(self, k, step, part=0):
        d, z, core, x, y, *_ = self.place
        yx = 2 * y + x
        g, rows = self.rows(k)
        mine = self.mine[g]
        src = mine[part].at[core, rows] if isinstance(mine, tuple) else mine.at[yx, core, rows]
        return remote(
            src,
            self.wg.at[g, self.parts - step, yx, core, rows],
            self.z_sems[0].at[k, step - 1],
            self.z_sems[1].at[k, step - 1],
            (d, lax.rem(z + step, self.parts)),
        )

    def s_copy(self, k, n):
        d, z, core, x, y, d_core, d_x, d_y = self.place
        rest = pl.ds(1, self.parts - 1)
        g, rows = self.rows(k)
        width = self.wg.shape[5]
        if n < 2:
            ref = self.wg.at[g, rest, 2 * y + x, core, rows]
            who = (d_x, d_y)[n]
        elif n == 2:
            ref = self.wg.at[g, rest, 2 * y + 1 - x, core, rows, pl.ds(0, width // 2)]
            who = d_y
        elif n == 3:
            ref = self.wg.at[g, rest, 2 * (1 - y) + x, core, rows, pl.ds(width // 2, width // 2)]
            who = d_x
        else:
            ref = self.wg.at[g, rest, :, core, rows]
            who = d_core
        return remote(ref, ref, self.s_sems[0].at[k, n], self.s_sems[1].at[k, n], (who, z))

    def z_start(self, k):
        _, _, _, x, y, *_ = self.place
        if isinstance(self.mine[self.rows(k)[0]], tuple):
            for part in range(4):

                @pl.when(2 * y + x == part)
                def _(part=part):
                    for step in range(1, self.parts):
                        self.z_copy(k, step, part).start()

        else:
            for step in range(1, self.parts):
                self.z_copy(k, step).start()

    def tick(self, k):
        if k < self.chunks:
            for step in range(1, self.parts):
                self.z_copy(k, step).wait_recv()
            self.s_copy(k, 0).start()
            self.s_copy(k, 1).start()
            if k + self.ahead < self.chunks:
                self.z_start(k + self.ahead)
        if 0 <= k - 1 < self.chunks:
            self.s_copy(k - 1, 0).wait_recv()
            self.s_copy(k - 1, 2).start()
            self.s_copy(k - 1, 1).wait_recv()
            self.s_copy(k - 1, 3).start()
        if 0 <= k - 2 < self.chunks:
            self.s_copy(k - 2, 2).wait_recv()
            self.s_copy(k - 2, 3).wait_recv()
            self.s_copy(k - 2, 4).start()

    def arrived(self, g):
        for k in range(self.parts_of_group * g, self.parts_of_group * (g + 1)):
            self.s_copy(k, 4).wait_recv()

    def sent(self):
        for k in range(self.chunks):
            for step in range(1, self.parts):
                self.z_copy(k, step).wait_send()
            for n in range(5):
                self.s_copy(k, n).wait_send()


C_RING = 4
KEEP = 4
A_RING = 6
B_RING = 6
Z_RING = 6
TICKS = 16


class Scatter:
    def __init__(self, bufs, sems, credit):
        (
            self.c_in, self.a_in, self.b_in, self.z_in,
            self.a_out, self.a_keep, self.b_out, self.b_keep, self.z_out, self.total,
        ) = bufs
        self.sems, self.credit = sems, credit
        self.parts = 4
        self.share = self.z_out.shape[1]
        self.place = places()

    def block(self, t):
        if t < 8:
            return 3 - t // 4, t % 4
        return 3 - t // 4, (t + 1) % 4

    def copy(self, k, t, src, dst, who):
        return remote(src, dst, self.sems.at[0, k, t], self.sems.at[1, k, t], who)

    def c_copy(self, t, src):
        z, d_core = self.place[1], self.place[5]
        return self.copy(0, t, src, self.c_in.at[t % C_RING], (d_core, z))

    def a_copy(self, t, q):
        _, z, *_, d_x, d_y = self.place
        src, dst = self.a_out.at[t % 2, q], self.a_in.at[t % A_RING, q]
        return self.copy(1 + q, t, src, dst, ((d_x, d_y)[q], z))

    def b_copy(self, t, q):
        _, z, *_, d_x, d_y = self.place
        src, dst = self.b_out.at[t % 2, q], self.b_in.at[t % B_RING, q]
        return self.copy(3 + q, t, src, dst, ((d_y, d_x)[q], z))

    def z_copy(self, t):
        d, z = self.place[:2]
        who = (d, lax.rem(z + self.block(t)[1], self.parts))
        return self.copy(5, t, self.z_out.at[t % Z_RING], self.z_in.at[t], who)

    def rows(self, q):
        return pl.ds(q * (self.share // 2), self.share // 2)

    def c_start(self, t, src):
        if t >= C_RING:
            pl.semaphore_wait(self.credit.at[0], 1)
        self.c_copy(t, src).start()

    def a_start(self, t, mine, src):
        _, _, _, x, y, d_core, *_ = self.place
        slot, ring, held = t % 2, t % C_RING, t % KEEP
        if t >= 2:
            self.a_copy(t - 2, 0).wait_send()
            self.a_copy(t - 2, 1).wait_send()
        self.c_copy(t, src).wait_recv()
        for q in range(2):
            rows = self.rows(q)
            for k in range(2):
                send = (2 * k + 1 - x, 2 * (1 - y) + k)[q]
                self.a_out[slot, q, k] = mine[send, rows] + self.c_in[ring, send, rows]
            if t >= A_RING:
                pl.semaphore_wait(self.credit.at[1 + q], 1)
            self.a_copy(t, q).start()
        for q in range(2):
            rows = self.rows(q)
            for k in range(2):
                keep = (2 * k + x, 2 * y + k)[q]
                self.a_keep[held, q, k] = mine[keep, rows] + self.c_in[ring, keep, rows]
        if t < TICKS - C_RING:
            self.free(0, d_core)

    def free(self, k, who):
        pl.semaphore_signal(
            self.credit.at[k], inc=1, device_id=(who, self.place[1]), device_id_type=MESH_ID
        )

    def b_start(self, t):
        _, _, _, x, y, _, d_x, d_y = self.place
        slot, held, ring = t % 2, t % KEEP, t % A_RING
        if t >= 2:
            self.b_copy(t - 2, 0).wait_send()
            self.b_copy(t - 2, 1).wait_send()
        for q in range(2):
            keep = (y, x)[q]
            send = 1 - keep
            self.a_copy(t, q).wait_recv()
            self.b_out[slot, q] = self.a_keep[held, q, send] + self.a_in[ring, q, send]
            if t >= B_RING:
                pl.semaphore_wait(self.credit.at[3 + q], 1)
            self.b_copy(t, q).start()
            self.b_keep[held, q] = self.a_keep[held, q, keep].astype(F32) + self.a_in[
                ring, q, keep
            ].astype(F32)
            if t < TICKS - A_RING:
                self.free(1 + q, (d_x, d_y)[q])

    def z_start(self, t):
        slot, held = t % Z_RING, t % KEEP
        g, r = self.block(t)
        if t >= Z_RING and self.block(t - Z_RING)[1] > 0:
            self.z_copy(t - Z_RING).wait_send()
        for q in range(2):
            self.b_copy(t, q).wait_recv()
            done = self.b_keep[held, q] + self.b_in[t % B_RING, q].astype(F32)
            if r == 0:
                self.total[g, self.rows(q)] = done
            else:
                self.z_out[slot, self.rows(q)] = low(done)
            if t < TICKS - B_RING:
                self.free(3 + q, self.place[7 - q])
        if r > 0:
            self.z_copy(t).start()

    def finish(self):
        for t in range(TICKS - 2, TICKS):
            for q in range(2):
                self.a_copy(t, q).wait_send()
                self.b_copy(t, q).wait_send()
        for t in range(TICKS):
            g, r = self.block(t)
            if r > 0:
                if t >= TICKS - Z_RING:
                    self.z_copy(t).wait_send()
                self.z_copy(t).wait_recv()
                self.total[g] += self.z_in[t].astype(F32)


class Sum:
    def __init__(self, near, far, send, recv):
        self.near, self.far = near, far
        self.send, self.recv = send, recv
        self.place = places()
        self.lo = lax.rem(self.place[0], 8)

    def near_copy(self, k):
        ref = self.near.at[self.lo]
        return remote(
            ref, ref, self.send.at[k - 1], self.recv.at[k - 1], (peer(k), self.place[1])
        )

    def far_copy(self, k):
        d, z = self.place[:2]
        ref = self.far.at[z]
        who = (d, lax.rem(z + k, self.far.shape[0]))
        return remote(ref, ref, self.send.at[6 + k], self.recv.at[6 + k], who)

    def start(self, value):
        self.near[self.lo] = value
        for k in range(1, 8):
            self.near_copy(k).start()

    def turn(self):
        for k in range(1, 8):
            self.near_copy(k).wait_send()
            sender = lax.rem(self.lo + 8 - k, 8)
            ref = self.near.at[sender]
            remote(
                ref, ref, self.send.at[k - 1], self.recv.at[k - 1], (peer(8 - k), self.place[1])
            ).wait_recv()
        value = self.near[0]
        for k in range(1, 8):
            value = value + self.near[k]
        self.far[self.place[1]] = value
        for k in range(1, self.far.shape[0]):
            self.far_copy(k).start()

    def result(self):
        d, z = self.place[:2]
        parts = self.far.shape[0]
        for k in range(1, parts):
            self.far_copy(k).wait_send()
            sender = lax.rem(z + parts - k, parts)
            ref = self.far.at[sender]
            remote(
                ref, ref, self.send.at[6 + k], self.recv.at[6 + k], (d, sender)
            ).wait_recv()
        value = self.far[0]
        for k in range(1, parts):
            value = value + self.far[k]
        return value


def layer_kernel(
    halves,
    len_ref, x_ref, cot_ref, enc_own, gain1, gain2, gain3, buckets_ref, table_in,
    sk, sv, sq, so, ck, cv, cq, co, fi, fo,
    result_ref, total_out, small_out, dx_out, denc_out,
    w_hbm, g_hbm, q1_hbm, kv1_hbm, p1_hbm, o1_hbm, l1_hbm, q2_hbm, kv2_hbm, p2_hbm, o2_hbm, l2_hbm,
    w, enc, diag, mask, onehot, spread, xa, table_own, table_far,
    nbuf, n2, n3, q_in, kv_in, p_in, o_in, l_in, x1, x2, hid, slope, acc, dn,
    g_buf, l_buf, rows_t, rows_t2, keys_t, dp_buf, ds_buf, dkv_t, enc_acc, diag_acc,
    dxa_in, denc_in, small,
    c_in, a_in, b_in, z_in, a_out, a_keep, b_out, b_keep, z_out, s_near, s_far,
    w_sem, own_sem, in_sem, ring_sem, keep_sem, store_sem, load_sem, out_sem,
    z_send, z_recv, s_send, s_recv, e_send, e_recv,
    sems, credit, n_send, n_recv,
):
    rows, width_all = x_ref.shape
    width = width_all
    parts = w_hbm.shape[1]
    place = places()
    d, z_me, core = place[:3]
    half = half_of_sequence(halves)
    mate = z_me + 1 - 2 * half
    keys = 2 * enc.shape[1]
    own_keys = 2 * rows
    all_keys = (own_keys, keys)
    entered = greet(parts, True)

    mine = ((sk, sv, sq, so), (ck, cv, cq, co), fi, fo)

    def own_copies(g, k):
        if g >= 2:
            return [pltpu.make_async_copy(mine[g], w.at[0, k], own_sem.at[k, 0])]
        return [
            pltpu.make_async_copy(ref, w.at[0, k, part], own_sem.at[k, part])
            for part, ref in enumerate(mine[g])
        ]

    def own_start(g, k):
        for copy in own_copies(g, k):
            copy.start()

    def far_copy(g, r, slot, k):
        return pltpu.make_async_copy(w_hbm.at[g, r], w.at[slot, k], w_sem.at[slot, k])

    def own_in_slot_one(g, k):
        if g >= 2:
            return [pltpu.make_async_copy(mine[g], w.at[1, k], own_sem.at[k, 0])]
        return [
            pltpu.make_async_copy(ref, w.at[1, k, part], own_sem.at[k, part])
            for part, ref in enumerate(mine[g])
        ]

    def w_wait(g, r, k):
        @pl.when(r == 0)
        def _():
            for copy in own_copies(g, k):
                copy.wait()

        @pl.when(r > 0)
        def _():
            far_copy(g, r, lax.rem(r, 2), k).wait()

    def w_next(g, r, k):
        @pl.when((r > 0) & (r + 1 < parts))
        def _():
            far_copy(g, r + 1, lax.rem(r + 1, 2), k).start()

    def which(i):
        return lax.rem(i + 1, parts)

    kept = (
        (q1_hbm, kv1_hbm, p1_hbm, o1_hbm, l1_hbm),
        (q2_hbm, kv2_hbm, p2_hbm, o2_hbm, l2_hbm),
    )

    def ring(phase, r, slot):
        n = all_keys[phase]
        q, kv, p, o, l = kept[phase]
        return [
            (q.at[r], q_in.at[slot]),
            (kv.at[r], kv_in.at[slot, 0:n]),
            (p.at[pl.ds(3 * r, 3)], p_in.at[slot, :, :, 0:n]),
            (o.at[r], o_in.at[slot]),
            (l.at[r], l_in.at[slot]),
        ]

    def keeps(phase, r):
        slot = lax.rem(r, 2)
        return [
            pltpu.make_async_copy(dst, src, keep_sem.at[k, slot])
            for k, (src, dst) in enumerate(ring(phase, r, slot))
        ]

    def keep_wait(phase, r):
        for copy in keeps(phase, r):
            copy.wait()

    def streams(phase, i):
        slot = lax.rem(i, 2)
        return [
            pltpu.make_async_copy(src, dst, ring_sem.at[k, slot])
            for k, (src, dst) in enumerate(ring(phase, which(i), slot))
        ]

    def back_prefetch(phase, i):
        @pl.when(i < parts - 1)
        def _():
            far_copy(phase, which(i), lax.rem(i, 2), 0).start()

        @pl.when(i == parts - 1)
        def _():
            for copy in own_in_slot_one(phase, 0):
                copy.start()

        for copy in streams(phase, i):
            copy.start()

    def back_wait(phase, i):
        @pl.when(i < parts - 1)
        def _():
            far_copy(phase, which(i), lax.rem(i, 2), 0).wait()

        @pl.when(i == parts - 1)
        def _():
            for copy in own_in_slot_one(phase, 0):
                copy.wait()

        for copy in streams(phase, i):
            copy.wait()

    enc_here = pltpu.make_async_copy(enc_own, enc.at[half], in_sem)
    own_start(0, 0)
    enc_here.start()
    entered()

    gather = Gather(mine, w_hbm, z_send, z_recv, s_send, s_recv)
    scatter = Scatter(
        (c_in, a_in, b_in, z_in, a_out, a_keep, b_out, b_keep, z_out, total_out), sems, credit
    )
    sums = Sum(s_near, s_far, n_send, n_recv)
    x_copy = remote(x_ref, xa, e_send.at[0], e_recv.at[0], (d, mate))
    enc_copy = remote(enc_own, enc.at[half], e_send.at[1], e_recv.at[1], (d, mate))
    dxa_copy = remote(n2, dxa_in, e_send.at[2], e_recv.at[2], (d, mate))
    denc_copy = remote(enc.at[1 - half], denc_in, e_send.at[3], e_recv.at[3], (d, mate))
    tables = [
        remote(
            table_own, table_far.at[parts - step], e_send.at[3 + step], e_recv.at[3 + step],
            (d, lax.rem(z_me + step, parts)),
        )
        for step in range(1, parts)
    ]

    def put(t, value, start=0):
        shape = g_buf.shape[1:4] + (value.shape[1],)
        g_buf[lax.rem(t, 2), :, :, :, start : start + value.shape[1]] = value.reshape(shape)

    def store(t):
        slot = lax.rem(t, 2)
        return pltpu.make_async_copy(g_buf.at[slot], g_hbm.at[t], store_sem.at[slot])

    def away(t):
        return g_hbm.at[t, :, 1 - core]

    def load(t):
        slot = t % 2
        return pltpu.make_async_copy(g_hbm.at[t, :, core], l_buf.at[slot], load_sem.at[slot])

    def leave(t):
        if t < TICKS:
            scatter.c_start(t, away(t))
            load(t).start()
        if t >= 1:
            load(t - 1).wait()
            scatter.a_start(t - 1, l_buf.at[(t - 1) % 2], away(t - 1))

    b, z, tick = scatter.b_start, scatter.z_start, gather.tick

    def at(i, step, *moves):
        @pl.when(i == step)
        def _():
            for move, *args in moves:
                move(*args)

    gather.z_start(0)
    gather.z_start(1)

    @pl.when(half == 0)
    def _():
        x_copy.start()

    gather.z_start(2)
    table_own[...] = jnp.zeros_like(table_own)
    table_own[0 : table_in.shape[0], 0 : table_in.shape[1]] = table_in[...]
    for copy in tables:
        copy.start()
    for k in range(3, gather.ahead):
        gather.z_start(k)

    nbuf[rows : 2 * rows, :] = low(norm_rows(x_ref[...].astype(F32), line_of(gain1))[0])
    tick(0)

    slots = buckets_ref.shape[0]
    span = onehot.shape[1]
    here = jnp.concatenate(
        [line_of(buckets_ref), jnp.full((1, span - slots), -1, jnp.int32)], axis=1
    )
    kinds = onehot.shape[0]
    hit = lax.broadcasted_iota(jnp.int32, (kinds, span), 0) == here
    plain = jnp.where(hit, 1.0, 0.0).astype(BF16)
    for start in range(0, span, 128):
        offset = lax.broadcasted_iota(jnp.int32, (span, 128), 0)
        column = lax.broadcasted_iota(jnp.int32, (span, 128), 1) + start
        turn = (offset + column == rows) | (offset + column == rows + span)
        onehot[:, start : start + 128] = mm(plain, jnp.where(turn, 1.0, 0.0).astype(BF16))

    turns = [onehot[...]] + [pltpu.roll(onehot[...], k, 1) for k in range(1, 8)]
    spread[...] = jnp.transpose(jnp.concatenate(turns, axis=0))

    length = len_ref[lax.div(z_me, halves)]
    i = lax.broadcasted_iota(jnp.int32, mask.shape, 0)
    c = lax.broadcasted_iota(jnp.int32, mask.shape, 1)
    own = c - rows
    limit = jnp.where(half > 0, length, 0)
    ok = ((own < 0) & (c < limit)) | ((own >= 0) & (own <= i) & (own + half * rows < length))
    mask[...] = jnp.where(ok, 0.0, MASKED)
    tick(1)
    enc_copy.start()
    for copy in tables:
        copy.wait()
    for r in range(parts):
        table = table_own[...] if r == 0 else table_far[r]
        diag[r] = jnp.dot(
            table[:, 0 : onehot.shape[0]],
            onehot[...],
            precision=lax.Precision.HIGHEST,
            preferred_element_type=F32,
        )

    @pl.when(half == 0)
    def _():
        x_copy.wait_send()
        xa[...] = x_ref[...]

    @pl.when(half == 1)
    def _():
        x_copy.wait_recv()

    nbuf[0:rows, :] = low(norm_rows(xa[...].astype(F32), line_of(gain1))[0])

    def heads(phase, r):
        n = all_keys[phase]
        slot = lax.rem(r, 2)
        outs = []
        for j in range(3):
            q_h = q_in[slot, :, DH * j : DH * (j + 1)]
            k_h = kv_in[slot, 0:n, DH * j : DH * (j + 1)]
            v_h = kv_in[slot, 0:n, DH * (3 + j) : DH * (4 + j)]
            dp_buf[j % 2, :, 0:n] = mm_nt(q_h, k_h)
            for a, m in chunks(rows, 32):
                s = dp_buf[j % 2, a : a + m, 0:n]
                if phase == 0:
                    line = jnp.broadcast_to(diag[r, j : j + 1, :], (m, diag.shape[2]))
                    grid = pltpu.roll(line, a, 1, stride=1, stride_axis=0)
                    s = s + grid[:, 0:n] + mask[a : a + m, :]
                top = jnp.max(s, axis=1, keepdims=True)
                p_in[slot, j, a : a + m, 0:n] = low(jnp.exp(s - top))
            wide = jnp.concatenate([v_h, jnp.ones_like(v_h)], axis=1)
            mixed = mm(p_in[slot, j, :, 0:n], wide)
            outs.append(low(mixed[:, 0:DH] / mixed[:, DH : 2 * DH]))
            l_in[slot, :, 32 * j : 32 * (j + 1)] = mixed[:, DH : DH + 32]
        o_in[slot] = jnp.concatenate(outs, axis=1)

    def attention(phase, r, key_rows, query_rows):
        slot = lax.rem(r, 2)
        w_wait(phase, r, 0)
        w_next(phase, r, 0)

        @pl.when(r >= 2)
        def _():
            keep_wait(phase, r - 2)

        if phase == 1:

            @pl.when(r < 2)
            def _():
                keep_wait(0, r + 2)

        kv_in[slot, 0 : all_keys[phase]] = low(mm_nt(key_rows, block(w, slot, 0, 0, 384)))
        q_in[slot] = low(mm_nt(query_rows, block(w, slot, 0, 384, 576)))
        heads(phase, r)
        acc[...] += mm(o_in[slot], block(w, slot, 0, 576, 768))
        for copy in keeps(phase, r):
            copy.start()

    def take(g, k):
        gather.arrived(g)
        far_copy(g, 1, 1, k).start()

    acc[...] = x_ref[...].astype(F32)

    def self_step(r, carry):
        attention(0, r, nbuf[...], nbuf[rows : 2 * rows, :])
        at(r, 0, (tick, 2), (tick, 3), (tick, 4), (take, 0, 0))
        at(r, 1, (tick, 5))
        at(r, 2, (tick, 6), (own_start, 1, 0))
        at(r, 3, (tick, 7))
        return carry

    lax.fori_loop(0, parts, self_step, 0)
    x1[...] = acc[...]
    n2[...] = low(norm_rows(acc[...], line_of(gain2))[0])

    enc_copy.wait()
    enc_here.wait()

    def cross_step(r, carry):
        attention(1, r, enc[...].reshape(keys, width), n2[...])
        at(r, 0, (tick, 8), (take, 1, 0))
        at(r, 1, (tick, 9))
        at(r, 2, (tick, 10), (own_start, 2, 0))
        at(r, 3, (tick, 11))
        return carry

    lax.fori_loop(0, parts, cross_step, 0)
    x2[...] = acc[...]
    n3[...] = low(norm_rows(acc[...], line_of(gain3))[0])

    own_start(3, 1)
    rows_t[...] = flip(cot_ref[...])

    def inner_step(r, carry):
        slot = lax.rem(r, 2)
        w_wait(2, r, 0)
        w_next(2, r, 0)
        for a, n in chunks(rows, 64):
            v = mm(n3[a : a + n, :], block(w, slot, 0))
            sq = v * v
            t = jnp.tanh(v * (ROOT + ROOT * CUBE * sq))
            cdf = 0.5 + 0.5 * t
            hid[r, a : a + n, :] = low(v * cdf)
            slope[r, a : a + n, :] = low(
                cdf + 0.5 * v * (1.0 - t * t) * (ROOT + 3.0 * ROOT * CUBE * sq)
            )
        put(r, low(mm(rows_t[...], hid[r])))
        store(r).start()
        at(r, 0, (take, 2, 0))
        at(r, 1, (tick, 12))
        at(r, 2, (own_start, 2, 0))
        at(r, 3, (tick, 13))
        store(r).wait()
        at(r, 2, (leave, 0))
        at(r, 3, (leave, 1))
        return carry

    lax.fori_loop(0, parts, inner_step, 0)
    for r in (parts - 2, parts - 1):
        keep_wait(1, r)
    rows_t2[...] = flip(n3[...])
    dn[...] = jnp.zeros_like(dn)
    leave(2)

    def outer_step(r, carry):
        slot = lax.rem(r, 2)
        w_wait(3, r, 1)
        w_next(3, r, 1)
        w_wait(2, r, 0)

        @pl.when(r + 1 < parts)
        def _():
            far_copy(2, r + 1, lax.rem(r + 1, 2), 0).start()

        @pl.when(r + 1 == parts)
        def _():
            back_prefetch(1, jnp.int32(0))

        dh = low(mm_nt(cot_ref[...], block(w, slot, 1)))
        slope[r] = low(dh.astype(F32) * slope[r].astype(F32))
        put(4 + r, low(mm(rows_t2[...], slope[r])))
        store(4 + r).start()
        dn[...] += mm_nt(slope[r], block(w, slot, 0))
        store(4 + r).wait()
        at(r, 0, (leave, 3), (b, 0), (take, 3, 1))
        at(r, 1, (leave, 4), (b, 1), (z, 0))
        at(r, 2, (leave, 5), (b, 2), (z, 1))
        return carry

    lax.fori_loop(0, parts, outer_step, 0)
    def keep_sum(g, value):
        part = width_all // 2
        small[2 * g : 2 * g + 1, :] = value[:, 0:part]
        small[2 * g + 1 : 2 * g + 2, :] = value[:, part:]

    small[...] = jnp.zeros_like(small)
    back, sum3 = norm_back(dn[...], x2[...], line_of(gain3))
    dn[...] = cot_ref[...].astype(F32) + back
    keep_sum(2, sum3)
    leave(6)
    b(3)
    z(2)

    def heads_back(r, do, n, with_diag, between):
        slot = lax.rem(r, 2)
        q, kv, o = q_in[slot], kv_in.at[slot], o_in[slot].astype(F32)
        do_all = []
        delta_all = []
        for j in range(3):
            do_h = do[:, DH * j : DH * (j + 1)]
            inv = 1.0 / l_in[slot, :, 32 * j : 32 * j + 1]
            o_h = o[:, DH * j : DH * (j + 1)]
            delta_all.append(jnp.sum(do_h * o_h * inv, axis=1, keepdims=True))
            do_all.append(do_h * inv)
        do_t = low(jnp.transpose(jnp.concatenate(do_all, axis=1)))
        q_t = flip(q)
        dq = []
        for j in range(3):
            p_h = p_in.at[slot, j]
            k_h = kv[0:n, DH * j : DH * (j + 1)]
            v_h = kv[0:n, DH * (3 + j) : DH * (4 + j)]
            dp_buf[j % 2, :, 0:n] = mm_nt(low(do_all[j]), v_h)
            total = None
            for s, m in chunks(rows, 32):
                ds = low(
                    p_h[s : s + m, 0:n].astype(F32)
                    * (dp_buf[j % 2, s : s + m, 0:n] - delta_all[j][s : s + m, :])
                )
                ds_buf[j % 2, s : s + m, 0:n] = ds
                if with_diag:
                    width = diag_acc.shape[2]
                    wide = jnp.concatenate([ds.astype(F32), jnp.zeros((m, width - n), F32)], axis=1)
                    for b in range(0, m, 8):
                        turned = pltpu.roll(wide[b : b + 8, :], (width - s - b) % width, 1)
                        total = turned if total is None else total + turned
            if with_diag:
                diag_acc[which(r) * 3 + j] = total
            ds_h = ds_buf[j % 2, :, 0:n]
            dq.append(low(mm(ds_h, k_h)))
            dkv_t[DH * j : DH * (j + 1), 0:n] = mm(q_t[DH * j : DH * (j + 1), :], ds_h)
            dkv_t[DH * (3 + j) : DH * (4 + j), 0:n] = mm(
                do_t[DH * j : DH * (j + 1), :], p_h[:, 0:n]
            )
            if j == 1:
                between()
        return jnp.concatenate(dq, axis=1), low(jnp.transpose(dkv_t[:, 0:n]))

    def attention_step(phase, i, middle):
        slot = lax.rem(i, 2)
        n = all_keys[phase]
        t = 12 - 4 * phase + i
        back_wait(phase, i)

        @pl.when(i + 1 < parts)
        def _():
            back_prefetch(phase, i + 1)

        if phase == 1:

            @pl.when(i + 1 == parts)
            def _():
                back_prefetch(0, jnp.int32(0))

        do = low(mm_nt(low(dn[...]), block(w, slot, 0, 576, 768))).astype(F32)
        dq, dkv = heads_back(i, do, n, phase == 0, lambda: middle(i))
        put(t, low(mm(keys_t[:, 0:n], dkv)))
        both = [low(mm(rows_t2[...], dq)), low(mm(rows_t[...], o_in[slot]))]
        put(t, jnp.concatenate(both, axis=1), 384)
        store(t).start()
        acc[...] += mm(dq, block(w, slot, 0, 384, 576))
        enc_acc[0:n, :] += mm(dkv, block(w, slot, 0, 0, 384))
        store(t).wait()

    rows_t[...] = flip(low(dn[...]))
    rows_t2[...] = flip(n2[...])
    keys_t[...] = flip(enc[...].reshape(keys, width_all))
    acc[...] = jnp.zeros_like(acc)
    enc_acc[...] = jnp.zeros_like(enc_acc)

    def cross_back_step(i, carry):
        def middle(i):
            at(i, 0, (leave, 7), (b, 4), (z, 3))
            at(i, 1, (leave, 8), (b, 6), (z, 5))
            at(i, 2, (b, 7), (z, 6))
            at(i, 3, (leave, 10), (b, 8), (z, 7))

        attention_step(1, i, middle)
        at(i, 0, (b, 5), (z, 4))
        at(i, 1, (leave, 9))
        at(i, 3, (leave, 11))
        return carry

    lax.fori_loop(0, parts, cross_back_step, 0)
    enc[...] = low(enc_acc[...]).reshape(enc.shape)
    denc_copy.start()
    back, sum2 = norm_back(acc[...], x1[...], line_of(gain2))
    dn[...] += back
    keep_sum(1, sum2)
    b(9)
    z(8)

    own_start(3, 1)
    far_copy(3, 1, 1, 1).start()
    rows_t[...] = flip(low(dn[...]))
    rows_t2[...] = flip(nbuf[rows : 2 * rows, :])
    keys_t[:, 0:own_keys] = flip(nbuf[...])
    acc[...] = jnp.zeros_like(acc)
    enc_acc[0:own_keys, :] = jnp.zeros((own_keys, width_all), F32)

    def self_back_step(i, carry):
        def middle(i):
            at(i, 0, (b, 10), (z, 9))
            at(i, 1, (z, 10))
            at(i, 2, (z, 11))

        attention_step(0, i, middle)
        at(i, 0, (leave, 12))
        at(i, 1, (leave, 13), (b, 11))
        at(i, 2, (leave, 14), (b, 12))
        at(i, 3, (leave, 15), (b, 13), (z, 12))
        return carry

    lax.fori_loop(0, parts, self_back_step, 0)
    for r in (2, 3):
        far_copy(3, r, r - 2, 0).start()
    gain = line_of(gain1)
    back, sum1a = norm_back(enc_acc[0:rows, :], xa[...].astype(F32), gain)
    n2[...] = low(back)

    @pl.when(half == 1)
    def _():
        dxa_copy.start()

    leave(16)
    back, sum1 = norm_back(
        acc[...] + enc_acc[rows : 2 * rows, :], x_ref[...].astype(F32), gain
    )
    dn[...] += back
    keep_sum(0, sum1 + sum1a)
    count = 8 * diag_acc.shape[0]
    turned = jnp.dot(
        diag_acc[...].reshape(count, diag_acc.shape[2]),
        spread[...],
        precision=lax.Precision.HIGHEST,
        preferred_element_type=F32,
    )
    kinds = onehot.shape[0]
    row = lax.rem(lax.broadcasted_iota(jnp.int32, turned.shape, 0), 8)
    place_of = lax.div(lax.broadcasted_iota(jnp.int32, turned.shape, 1), kinds)
    turned = jnp.where(row == place_of, turned, 0.0)
    turned = jnp.sum(turned.reshape(count // 8, 8, turned.shape[1]), axis=1)
    table = turned[:, 0:kinds]
    for k in range(1, 8):
        table = table + turned[:, kinds * k : kinds * (k + 1)]
    for r in range(parts):
        at = lax.rem(z_me + r, parts)
        for p in range(parts):

            @pl.when(at == p)
            def _(r=r, p=p):
                for j in range(3):
                    lane = kinds * (3 * p + j)
                    small[6:7, lane : lane + kinds] = table[3 * r + j : 3 * r + j + 1]

    sums.start(small[...])
    for copy in own_copies(3, 1):
        copy.wait()
    x2[...] += mm(hid[0], block(w, 0, 1))
    b(14)
    z(13)
    far_copy(3, 1, 1, 1).wait()
    x2[...] += mm(hid[1], block(w, 1, 1))
    sums.turn()
    b(15)
    z(14)
    for r in (2, 3):
        far_copy(3, r, r - 2, 0).wait()
        x2[...] += mm(hid[r], block(w, r - 2, 0))
    result_ref[...] = low(x2[...])
    denc_copy.wait()
    enc[half] = low(enc[half].astype(F32) + denc_in[...].astype(F32))
    denc_done = pltpu.make_async_copy(enc.at[half], denc_out, out_sem.at[0])
    denc_done.start()
    z(15)

    @pl.when(half == 1)
    def _():
        dxa_copy.wait_send()
        n3[...] = low(dn[...])

    @pl.when(half == 0)
    def _():
        dxa_copy.wait_recv()
        n3[...] = low(dn[...] + dxa_in[...].astype(F32))

    dx_done = pltpu.make_async_copy(n3, dx_out, out_sem.at[1])
    dx_done.start()
    scatter.finish()
    small_out[...] = sums.result()
    for t in range(TICKS):
        scatter.c_copy(t, away(t)).wait_send()
    gather.sent()
    denc_done.wait()
    dx_done.wait()


def finish_kernel(
    result_in, dx, denc, total, small,
    result, input_grad, encoder_grad,
    g_gain1, gsq, gsk, gsv, gso, g_gain2, gcq, gck, gcv, gco, g_gain3, gfi, gfo, lines,
):
    result[...] = result_in[...]
    input_grad[...] = dx[...]
    encoder_grad[...] = denc[...]
    width = result.shape[1]
    for g, (k, v, q, o) in enumerate(((gsk, gsv, gsq, gso), (gck, gcv, gcq, gco))):
        k[...] = total[g, :, 0:192]
        v[...] = total[g, :, 192:384]
        q[...] = total[g, :, 384:576]
        o[...] = jnp.transpose(total[g, :, 576:768])
    gfi[...] = total[2]
    gfo[...] = total[3]
    for row, gain in enumerate((g_gain1, g_gain2, g_gain3)):
        part = small[2 * row : 2 * row + 2, :]
        gain[...] = jnp.concatenate([part[0:1], part[1:2]], axis=1).reshape(width)
    z = lax.axis_index("mp")
    for p in range(4):

        @pl.when(z == p)
        def _(p=p):
            kinds = lines.shape[1]
            for j in range(3):
                lane = kinds * (3 * p + j)
                lines[j : j + 1, :] = small[6:7, lane : lane + kinds]


def across(value, axis, n_dp):
    groups = n_dp // 8
    whole = lax.all_gather(value, "dp", axis=0, tiled=False)
    whole = whole.reshape(groups, 8, *value.shape).sum(0)
    whole = jnp.concatenate([whole[k] for k in range(8)], axis=axis)
    share = whole.shape[axis] // n_dp
    return lax.dynamic_slice_in_dim(whole, lax.axis_index("dp") * share, share, axis)


def across_small(value, n_dp):
    whole = lax.all_gather(value, "dp", axis=0, tiled=False)
    return whole.reshape(n_dp // 8, 8, *value.shape)[:, 0].sum(0)


def body(
    inputs, encoded, cotangent, lengths, buckets,
    self_gain, self_query, self_key, self_value, self_output, bias_table,
    cross_gain, cross_query, cross_key, cross_value, cross_output,
    feed_gain, feed_inner, feed_output_weight,
):
    rows, width = inputs.shape
    parts = lax.axis_size("mp")
    n_dp = lax.axis_size("dp")
    halves = parts // lengths.shape[0]
    assert halves == 2 and buckets.shape[0] == 2 * rows and parts == 4
    z = lax.axis_index("mp")
    enc_rows = encoded.shape[0]
    vmem = pl.BlockSpec(memory_space=pltpu.VMEM)
    smem = pl.BlockSpec(memory_space=pltpu.SMEM)
    hbm = pl.BlockSpec(memory_space=pl.ANY)
    sds = jax.ShapeDtypeStruct

    share = width // 8
    diag = 1024
    heads = 3 * parts
    keys = 2 * enc_rows
    gains = [self_gain, cross_gain, feed_gain]
    split = lambda v: v.reshape(2, share, width)
    whole = lambda v: v.reshape(4, 2, share, width)
    kinds = bias_table.shape[0]
    kept = [
        kind
        for n in (2 * rows, keys)
        for kind in (
            sds((parts, rows, 192), BF16),
            sds((parts, n, 384), BF16),
            sds((heads, rows, n), BF16),
            sds((parts, rows, 192), BF16),
            sds((parts, rows, 128), F32),
        )
    ]
    half_share = share // 2
    bf, ff = (lambda *shape: pltpu.VMEM(shape, BF16)), (lambda *shape: pltpu.VMEM(shape, F32))
    dma = lambda *shape: pltpu.SemaphoreType.DMA(shape)
    result, summed, small, input_grad, encoder_grad, *_ = pl.pallas_call(
        functools.partial(layer_kernel, halves),
        out_shape=[
            sds((rows, width), BF16),
            sds((4, share, width), F32),
            sds((8, width // 2), F32),
            sds((rows, width), BF16),
            sds((enc_rows, width), BF16),
            sds((4, parts, 4, 2, share, width), BF16),
            sds((TICKS, 4, 2, share, width), BF16),
            *kept,
        ],
        in_specs=[smem, vmem, vmem, hbm] + [vmem] * 5 + [hbm] * 10,
        out_specs=[vmem] * 3 + [hbm] * (4 + len(kept)),
        scratch_shapes=[
            bf(2, 2, 4, 2, share, width), bf(2, enc_rows, width), ff(parts, 8, diag),
            ff(rows, 2 * rows), ff(kinds, diag), ff(diag, 8 * kinds), bf(rows, width), ff(8, 128), ff(parts, 8, 128),
            bf(2 * rows, width), bf(rows, width), bf(rows, width),
            bf(2, rows, 192), bf(2, keys, 384), bf(2, 3, rows, keys), bf(2, rows, 192),
            ff(2, rows, 128), ff(rows, width), ff(rows, width),
            bf(parts, rows, width), bf(parts, rows, width), ff(rows, width), ff(rows, width),
            bf(2, 4, 2, share, width), bf(2, 4, share, width),
            bf(width, rows), bf(width, rows), bf(width, keys),
            ff(2, rows, keys), bf(2, rows, keys), ff(384, keys), ff(keys, width),
            ff(heads, 8, diag),
            bf(rows, width), bf(enc_rows, width), ff(8, width // 2),
            bf(C_RING, 4, share, width), bf(A_RING, 2, 2, half_share, width),
            bf(B_RING, 2, half_share, width), bf(TICKS, share, width),
            bf(2, 2, 2, half_share, width), bf(KEEP, 2, 2, half_share, width),
            bf(2, 2, half_share, width), ff(KEEP, 2, half_share, width),
            bf(Z_RING, share, width), ff(8, 8, width // 2), ff(parts, 8, width // 2),
            dma(2, 2), dma(2, 4), pltpu.SemaphoreType.DMA, dma(5, 2), dma(5, 2), dma(2), dma(2),
            dma(2),
            dma(Gather.chunks, parts - 1), dma(Gather.chunks, parts - 1),
            dma(Gather.chunks, 5), dma(Gather.chunks, 5), dma(7), dma(7),
            dma(2, 6, TICKS), pltpu.SemaphoreType.REGULAR((5,)), dma(10), dma(10),
        ],
        compiler_params=pltpu.CompilerParams(
            collective_id=1, has_side_effects=True, vmem_limit_bytes=VMEM_BYTES
        ),
        name="layer",
    )(
        lengths, inputs, cotangent, encoded, *gains, buckets, bias_table.T,
        split(self_key.T), split(self_value.T), split(self_query.T), split(self_output),
        split(cross_key.T), split(cross_value.T), split(cross_query.T), split(cross_output),
        whole(feed_inner), whole(feed_output_weight),
    )

    f32 = lambda *shape: sds(shape, F32)
    outs = pl.pallas_call(
        finish_kernel,
        out_shape=[
            sds((rows, width), BF16), sds((rows, width), BF16), sds((enc_rows, width), BF16),
            f32(width), f32(share, 192), f32(share, 192), f32(share, 192), f32(192, share),
            f32(width), f32(share, 192), f32(share, 192), f32(share, 192), f32(192, share),
            f32(width), f32(share, width), f32(share, width), f32(3, kinds),
        ],
        in_specs=[vmem] * 5,
        out_specs=[vmem] * 17,
        name="finish",
    )(result, input_grad, encoder_grad, summed, small)
    result, input_grad, encoder_grad, *grads, lines = outs
    if n_dp > 8:
        axes = (None, 0, 0, 0, 1, None, 0, 0, 0, 1, None, 0, 0)
        grads = [
            across_small(value, n_dp) if axis is None else across(value, axis, n_dp)
            for value, axis in zip(grads, axes)
        ]
        lines = across_small(lines, n_dp)
    return (result, input_grad, encoder_grad, *grads[0:5], lines.T, *grads[5:-1], grads[-1].T)


def solution(mesh):
    rows = P(("dp", "mp"), None)
    across, down = P(None, "mp"), P("mp", None)
    return jax.shard_map(
        body,
        mesh=mesh,
        in_specs=(
            rows, rows, rows, P("dp"), P(),
            P(), across, across, across, down, across,
            P(), across, across, across, down,
            P(), across, down,
        ),
        out_specs=(
            rows, rows, rows,
            P(), P("dp", "mp"), P("dp", "mp"), P("dp", "mp"), P("mp", "dp"), P(None, "mp"),
            P(), P("dp", "mp"), P("dp", "mp"), P("dp", "mp"), P("mp", "dp"),
            P(), P("dp", "mp"), P("mp", "dp"),
        ),
        check_vma=False,
    )
```

```python
import functools

import jax
import jax.numpy as jnp
from jax import lax
from jax.experimental import pallas as pl
from jax.experimental.pallas import tpu as pltpu
from jax.sharding import PartitionSpec as P

EPS = 1e-06
MASKED = -1e30
DH = 64
F32 = jnp.float32
BF16 = jnp.bfloat16
VMEM_BYTES = 62 << 20
ROOT = 0.7978845608028654
CUBE = 0.044715


def mm(a, b):
    return jnp.dot(a, b, preferred_element_type=F32)


def mm_nt(a, b):
    return lax.dot_general(a, b, (((1,), (1,)), ((), ())), preferred_element_type=F32)


def line_of(ref):
    return ref[...].reshape(1, ref.shape[0])


def low(v):
    return v.astype(BF16)


def flip(v):
    return jnp.transpose(v.astype(F32)).astype(BF16)


def norm_rows(v, gain):
    root = lax.rsqrt(jnp.mean(v * v, axis=-1, keepdims=True) + EPS)
    unit = v * root
    return unit * gain, unit, root


def norm_back(grad, v, gain):
    _, unit, root = norm_rows(v, gain)
    scaled = grad * gain
    back = root * (scaled - unit * jnp.mean(scaled * unit, axis=-1, keepdims=True))
    return back, jnp.sum(grad * unit, axis=0, keepdims=True)


def block(w, i, j, start=0, stop=None):
    part = w[i, j]
    part = part.reshape(part.shape[0] * part.shape[1] * part.shape[2], part.shape[3])
    return part[start:stop]


def half_of_sequence(halves):
    return lax.rem(lax.axis_index("mp"), halves)


def chunks(rows, step):
    return [(r, min(step, rows - r)) for r in range(0, rows, step)]


MESH_ID = pl.DeviceIdType.MESH


def places():
    d = lax.axis_index("dp")
    z = lax.axis_index("mp")
    lo = lax.rem(d, 8)
    core = lax.rem(lo, 2)
    x = lax.rem(lax.div(lo, 2), 2)
    y = lax.div(lo, 4)
    d_core = d + 1 - 2 * core
    d_x = d + 2 - 4 * x
    d_y = d + 4 - 8 * y
    return d, z, core, x, y, d_core, d_x, d_y


def peer(k):
    d = lax.axis_index("dp")
    lo = lax.rem(d, 8)
    return d - lo + lax.rem(lo + k, 8)


def greet(z_parts, everyone):
    d, z, _, _, _, d_core, d_x, d_y = places()
    barrier = pltpu.get_barrier_semaphore()
    near = [peer(k) for k in range(1, 8)] if everyone else [d_core, d_x, d_y]
    for who in near:
        pl.semaphore_signal(barrier, inc=1, device_id=(who, z), device_id_type=MESH_ID)
    for step in range(1, z_parts):
        pl.semaphore_signal(
            barrier, inc=1, device_id=(d, lax.rem(z + step, z_parts)), device_id_type=MESH_ID
        )
    return lambda: pl.semaphore_wait(barrier, len(near) + z_parts - 1)


def remote(src, dst, send, recv, who):
    return pltpu.make_async_remote_copy(
        src_ref=src, dst_ref=dst, send_sem=send, recv_sem=recv, device_id=who, device_id_type=MESH_ID
    )


class Gather:
    parts_of_group = 3
    chunks = 12
    ahead = 6

    def __init__(self, mine, wg, z_send, z_recv, s_send, s_recv):
        self.mine, self.wg = mine, wg
        self.z_sems, self.s_sems = (z_send, z_recv), (s_send, s_recv)
        self.parts = wg.shape[1]
        self.place = places()

    def rows(self, k):
        some = self.wg.shape[4] // self.parts_of_group
        return k // self.parts_of_group, pl.ds((k % self.parts_of_group) * some, some)

    def z_copy(self, k, step, part=0):
        d, z, core, x, y, *_ = self.place
        yx = 2 * y + x
        g, rows = self.rows(k)
        mine = self.mine[g]
        src = mine[part].at[core, rows] if isinstance(mine, tuple) else mine.at[yx, core, rows]
        return remote(
            src,
            self.wg.at[g, self.parts - step, yx, core, rows],
            self.z_sems[0].at[k, step - 1],
            self.z_sems[1].at[k, step - 1],
            (d, lax.rem(z + step, self.parts)),
        )

    def s_copy(self, k, n):
        d, z, core, x, y, d_core, d_x, d_y = self.place
        rest = pl.ds(1, self.parts - 1)
        g, rows = self.rows(k)
        width = self.wg.shape[5]
        if n < 2:
            ref = self.wg.at[g, rest, 2 * y + x, core, rows]
            who = (d_x, d_y)[n]
        elif n == 2:
            ref = self.wg.at[g, rest, 2 * y + 1 - x, core, rows, pl.ds(0, width // 2)]
            who = d_y
        elif n == 3:
            ref = self.wg.at[g, rest, 2 * (1 - y) + x, core, rows, pl.ds(width // 2, width // 2)]
            who = d_x
        else:
            ref = self.wg.at[g, rest, :, core, rows]
            who = d_core
        return remote(ref, ref, self.s_sems[0].at[k, n], self.s_sems[1].at[k, n], (who, z))

    def z_start(self, k):
        _, _, _, x, y, *_ = self.place
        if isinstance(self.mine[self.rows(k)[0]], tuple):
            for part in range(4):

                @pl.when(2 * y + x == part)
                def _(part=part):
                    for step in range(1, self.parts):
                        self.z_copy(k, step, part).start()

        else:
            for step in range(1, self.parts):
                self.z_copy(k, step).start()

    def tick(self, k):
        if k < self.chunks:
            for step in range(1, self.parts):
                self.z_copy(k, step).wait_recv()
            self.s_copy(k, 0).start()
            self.s_copy(k, 1).start()
            if k + self.ahead < self.chunks:
                self.z_start(k + self.ahead)
        if 0 <= k - 1 < self.chunks:
            self.s_copy(k - 1, 0).wait_recv()
            self.s_copy(k - 1, 2).start()
            self.s_copy(k - 1, 1).wait_recv()
            self.s_copy(k - 1, 3).start()
        if 0 <= k - 2 < self.chunks:
            self.s_copy(k - 2, 2).wait_recv()
            self.s_copy(k - 2, 3).wait_recv()
            self.s_copy(k - 2, 4).start()

    def arrived(self, g):
        for k in range(self.parts_of_group * g, self.parts_of_group * (g + 1)):
            self.s_copy(k, 4).wait_recv()

    def sent(self):
        for k in range(self.chunks):
            for step in range(1, self.parts):
                self.z_copy(k, step).wait_send()
            for n in range(5):
                self.s_copy(k, n).wait_send()


C_RING = 4
KEEP = 4
OUT_RING = 4
A_RING = 6
B_RING = 6
Z_RING = 6
TICKS = 16


class Scatter:
    def __init__(self, bufs, sems, credit):
        (
            self.c_in, self.a_in, self.b_in, self.z_in,
            self.a_out, self.a_keep, self.b_out, self.b_keep, self.z_out, self.total,
        ) = bufs
        self.sems, self.credit = sems, credit
        self.parts = 4
        self.share = self.z_out.shape[1]
        self.place = places()

    def block(self, t):
        if t < 8:
            return 3 - t // 4, t % 4
        return 3 - t // 4, (t + 1) % 4

    def copy(self, k, t, src, dst, who):
        return remote(src, dst, self.sems.at[0, k, t], self.sems.at[1, k, t], who)

    def c_copy(self, t, src):
        z, d_core = self.place[1], self.place[5]
        return self.copy(0, t, src, self.c_in.at[t % C_RING], (d_core, z))

    def a_copy(self, t, q):
        _, z, *_, d_x, d_y = self.place
        src, dst = self.a_out.at[t % OUT_RING, q], self.a_in.at[t % A_RING, q]
        return self.copy(1 + q, t, src, dst, ((d_x, d_y)[q], z))

    def b_copy(self, t, q):
        _, z, *_, d_x, d_y = self.place
        src, dst = self.b_out.at[t % OUT_RING, q], self.b_in.at[t % B_RING, q]
        return self.copy(3 + q, t, src, dst, ((d_y, d_x)[q], z))

    def z_copy(self, t):
        d, z = self.place[:2]
        who = (d, lax.rem(z + self.block(t)[1], self.parts))
        return self.copy(5, t, self.z_out.at[t % Z_RING], self.z_in.at[t], who)

    def rows(self, q):
        return pl.ds(q * (self.share // 2), self.share // 2)

    def c_start(self, t, src):
        if t >= C_RING:
            pl.semaphore_wait(self.credit.at[0], 1)
        self.c_copy(t, src).start()

    def a_start(self, t, mine, src):
        _, _, _, x, y, d_core, *_ = self.place
        slot, ring, held = t % OUT_RING, t % C_RING, t % KEEP
        if t >= OUT_RING:
            self.a_copy(t - OUT_RING, 0).wait_send()
            self.a_copy(t - OUT_RING, 1).wait_send()
        self.c_copy(t, src).wait_recv()
        for q in range(2):
            rows = self.rows(q)
            for k in range(2):
                send = (2 * k + 1 - x, 2 * (1 - y) + k)[q]
                self.a_out[slot, q, k] = mine[send, rows] + self.c_in[ring, send, rows]
            if t >= A_RING:
                pl.semaphore_wait(self.credit.at[1 + q], 1)
            self.a_copy(t, q).start()
        for q in range(2):
            rows = self.rows(q)
            for k in range(2):
                keep = (2 * k + x, 2 * y + k)[q]
                self.a_keep[held, q, k] = mine[keep, rows] + self.c_in[ring, keep, rows]
        if t < TICKS - C_RING:
            self.free(0, d_core)

    def free(self, k, who):
        pl.semaphore_signal(
            self.credit.at[k], inc=1, device_id=(who, self.place[1]), device_id_type=MESH_ID
        )

    def b_start(self, t):
        _, _, _, x, y, _, d_x, d_y = self.place
        slot, held, ring = t % OUT_RING, t % KEEP, t % A_RING
        if t >= OUT_RING:
            self.b_copy(t - OUT_RING, 0).wait_send()
            self.b_copy(t - OUT_RING, 1).wait_send()
        for q in range(2):
            keep = (y, x)[q]
            send = 1 - keep
            self.a_copy(t, q).wait_recv()
            self.b_out[slot, q] = self.a_keep[held, q, send] + self.a_in[ring, q, send]
            if t >= B_RING:
                pl.semaphore_wait(self.credit.at[3 + q], 1)
            self.b_copy(t, q).start()
            self.b_keep[held, q] = self.a_keep[held, q, keep].astype(F32) + self.a_in[
                ring, q, keep
            ].astype(F32)
            if t < TICKS - A_RING:
                self.free(1 + q, (d_x, d_y)[q])

    def z_start(self, t):
        slot, held = t % Z_RING, t % KEEP
        g, r = self.block(t)
        if t >= Z_RING and self.block(t - Z_RING)[1] > 0:
            self.z_copy(t - Z_RING).wait_send()
        for q in range(2):
            self.b_copy(t, q).wait_recv()
            done = self.b_keep[held, q] + self.b_in[t % B_RING, q].astype(F32)
            if r == 0:
                self.total[g, self.rows(q)] = done
            else:
                self.z_out[slot, self.rows(q)] = low(done)
            if t < TICKS - B_RING:
                self.free(3 + q, self.place[7 - q])
        if r > 0:
            self.z_copy(t).start()

    def finish(self):
        for t in range(TICKS - OUT_RING, TICKS):
            for q in range(2):
                self.a_copy(t, q).wait_send()
                self.b_copy(t, q).wait_send()
        for t in range(TICKS):
            g, r = self.block(t)
            if r > 0:
                if t >= TICKS - Z_RING:
                    self.z_copy(t).wait_send()
                self.z_copy(t).wait_recv()
                self.total[g] += self.z_in[t].astype(F32)


class Sum:
    def __init__(self, near, far, send, recv):
        self.near, self.far = near, far
        self.send, self.recv = send, recv
        self.place = places()
        self.lo = lax.rem(self.place[0], 8)

    def near_copy(self, k):
        ref = self.near.at[self.lo]
        return remote(
            ref, ref, self.send.at[k - 1], self.recv.at[k - 1], (peer(k), self.place[1])
        )

    def far_copy(self, k):
        d, z = self.place[:2]
        ref = self.far.at[z]
        who = (d, lax.rem(z + k, self.far.shape[0]))
        return remote(ref, ref, self.send.at[6 + k], self.recv.at[6 + k], who)

    def start(self, value):
        self.near[self.lo] = value
        for k in range(1, 8):
            self.near_copy(k).start()

    def turn(self):
        for k in range(1, 8):
            self.near_copy(k).wait_send()
            sender = lax.rem(self.lo + 8 - k, 8)
            ref = self.near.at[sender]
            remote(
                ref, ref, self.send.at[k - 1], self.recv.at[k - 1], (peer(8 - k), self.place[1])
            ).wait_recv()
        value = self.near[0]
        for k in range(1, 8):
            value = value + self.near[k]
        self.far[self.place[1]] = value
        for k in range(1, self.far.shape[0]):
            self.far_copy(k).start()

    def result(self):
        d, z = self.place[:2]
        parts = self.far.shape[0]
        for k in range(1, parts):
            self.far_copy(k).wait_send()
            sender = lax.rem(z + parts - k, parts)
            ref = self.far.at[sender]
            remote(
                ref, ref, self.send.at[6 + k], self.recv.at[6 + k], (d, sender)
            ).wait_recv()
        value = self.far[0]
        for k in range(1, parts):
            value = value + self.far[k]
        return value


def layer_kernel(
    halves,
    len_ref, x_ref, cot_ref, enc_own, gain1, gain2, gain3, buckets_ref, table_in,
    sk, sv, sq, so, ck, cv, cq, co, fi, fo,
    result_ref, total_out, small_out, dx_out, denc_out,
    w_hbm, g_hbm, q1_hbm, kv1_hbm, p1_hbm, o1_hbm, l1_hbm, q2_hbm, kv2_hbm, p2_hbm, o2_hbm, l2_hbm,
    w, enc, diag, mask, onehot, spread, xa, table_own, table_far,
    nbuf, n2, n3, q_in, kv_in, p_in, o_in, l_in, x1, x2, hid, slope, acc, dn,
    g_buf, l_buf, rows_t, rows_t2, keys_t, dp_buf, ds_buf, dkv_t, enc_acc, diag_acc,
    dxa_in, denc_in, small,
    c_in, a_in, b_in, z_in, a_out, a_keep, b_out, b_keep, z_out, s_near, s_far,
    w_sem, own_sem, in_sem, ring_sem, keep_sem, store_sem, load_sem, out_sem,
    z_send, z_recv, s_send, s_recv, e_send, e_recv,
    sems, credit, n_send, n_recv,
):
    rows, width_all = x_ref.shape
    width = width_all
    parts = w_hbm.shape[1]
    place = places()
    d, z_me, core = place[:3]
    half = half_of_sequence(halves)
    mate = z_me + 1 - 2 * half
    keys = 2 * enc.shape[1]
    own_keys = 2 * rows
    all_keys = (own_keys, keys)
    entered = greet(parts, True)

    mine = ((sk, sv, sq, so), (ck, cv, cq, co), fi, fo)

    def own_copies(g, k):
        if g >= 2:
            return [pltpu.make_async_copy(mine[g], w.at[0, k], own_sem.at[k, 0])]
        return [
            pltpu.make_async_copy(ref, w.at[0, k, part], own_sem.at[k, part])
            for part, ref in enumerate(mine[g])
        ]

    def own_start(g, k):
        for copy in own_copies(g, k):
            copy.start()

    def far_copy(g, r, slot, k):
        return pltpu.make_async_copy(w_hbm.at[g, r], w.at[slot, k], w_sem.at[slot, k])

    def own_in_slot_one(g, k):
        if g >= 2:
            return [pltpu.make_async_copy(mine[g], w.at[1, k], own_sem.at[k, 0])]
        return [
            pltpu.make_async_copy(ref, w.at[1, k, part], own_sem.at[k, part])
            for part, ref in enumerate(mine[g])
        ]

    def w_wait(g, r, k):
        @pl.when(r == 0)
        def _():
            for copy in own_copies(g, k):
                copy.wait()

        @pl.when(r > 0)
        def _():
            far_copy(g, r, lax.rem(r, 2), k).wait()

    def w_next(g, r, k):
        @pl.when((r > 0) & (r + 1 < parts))
        def _():
            far_copy(g, r + 1, lax.rem(r + 1, 2), k).start()

    def which(i):
        return lax.rem(i + 1, parts)

    kept = (
        (q1_hbm, kv1_hbm, p1_hbm, o1_hbm, l1_hbm),
        (q2_hbm, kv2_hbm, p2_hbm, o2_hbm, l2_hbm),
    )

    def ring(phase, r, slot):
        n = all_keys[phase]
        q, kv, p, o, l = kept[phase]
        return [
            (q.at[r], q_in.at[slot]),
            (kv.at[r], kv_in.at[slot, 0:n]),
            (p.at[pl.ds(3 * r, 3)], p_in.at[slot, :, :, 0:n]),
            (o.at[r], o_in.at[slot]),
            (l.at[r], l_in.at[slot]),
        ]

    def keeps(phase, r):
        slot = lax.rem(r, 2)
        return [
            pltpu.make_async_copy(dst, src, keep_sem.at[k, slot])
            for k, (src, dst) in enumerate(ring(phase, r, slot))
        ]

    def keep_wait(phase, r):
        for copy in keeps(phase, r):
            copy.wait()

    def streams(phase, i):
        slot = lax.rem(i, 2)
        return [
            pltpu.make_async_copy(src, dst, ring_sem.at[k, slot])
            for k, (src, dst) in enumerate(ring(phase, which(i), slot))
        ]

    def back_prefetch(phase, i):
        @pl.when(i < parts - 1)
        def _():
            far_copy(phase, which(i), lax.rem(i, 2), 0).start()

        @pl.when(i == parts - 1)
        def _():
            for copy in own_in_slot_one(phase, 0):
                copy.start()

        for copy in streams(phase, i):
            copy.start()

    def back_wait(phase, i):
        @pl.when(i < parts - 1)
        def _():
            far_copy(phase, which(i), lax.rem(i, 2), 0).wait()

        @pl.when(i == parts - 1)
        def _():
            for copy in own_in_slot_one(phase, 0):
                copy.wait()

        for copy in streams(phase, i):
            copy.wait()

    enc_here = pltpu.make_async_copy(enc_own, enc.at[half], in_sem)
    own_start(0, 0)
    enc_here.start()
    entered()

    gather = Gather(mine, w_hbm, z_send, z_recv, s_send, s_recv)
    scatter = Scatter(
        (c_in, a_in, b_in, z_in, a_out, a_keep, b_out, b_keep, z_out, total_out), sems, credit
    )
    sums = Sum(s_near, s_far, n_send, n_recv)
    x_copy = remote(x_ref, xa, e_send.at[0], e_recv.at[0], (d, mate))
    enc_copy = remote(enc_own, enc.at[half], e_send.at[1], e_recv.at[1], (d, mate))
    dxa_copy = remote(n2, dxa_in, e_send.at[2], e_recv.at[2], (d, mate))
    denc_copy = remote(enc.at[1 - half], denc_in, e_send.at[3], e_recv.at[3], (d, mate))
    tables = [
        remote(
            table_own, table_far.at[parts - step], e_send.at[3 + step], e_recv.at[3 + step],
            (d, lax.rem(z_me + step, parts)),
        )
        for step in range(1, parts)
    ]

    def put(t, value, start=0):
        shape = g_buf.shape[1:4] + (value.shape[1],)
        g_buf[lax.rem(t, 2), :, :, :, start : start + value.shape[1]] = value.reshape(shape)

    def store(t):
        slot = lax.rem(t, 2)
        return pltpu.make_async_copy(g_buf.at[slot], g_hbm.at[t], store_sem.at[slot])

    def away(t):
        return g_hbm.at[t, :, 1 - core]

    def load(t):
        slot = t % 2
        return pltpu.make_async_copy(g_hbm.at[t, :, core], l_buf.at[slot], load_sem.at[slot])

    def c(t):
        scatter.c_start(t, away(t))
        load(t).start()

    def a(t):
        load(t).wait()
        scatter.a_start(t, l_buf.at[t % 2], away(t))

    def leave(t):
        c(t)
        if t >= 1:
            a(t - 1)

    b, z, tick = scatter.b_start, scatter.z_start, gather.tick

    def at(i, step, *moves):
        @pl.when(i == step)
        def _():
            for move, *args in moves:
                move(*args)

    gather.z_start(0)
    table_own[...] = jnp.zeros_like(table_own)
    table_own[0 : table_in.shape[0], 0 : table_in.shape[1]] = table_in[...]
    for copy in tables:
        copy.start()
    gather.z_start(1)

    @pl.when(half == 0)
    def _():
        x_copy.start()

    gather.z_start(2)
    for k in range(3, gather.ahead):
        gather.z_start(k)

    nbuf[rows : 2 * rows, :] = low(norm_rows(x_ref[...].astype(F32), line_of(gain1))[0])
    tick(0)

    slots = buckets_ref.shape[0]
    span = onehot.shape[1]
    here = jnp.concatenate(
        [line_of(buckets_ref), jnp.full((1, span - slots), -1, jnp.int32)], axis=1
    )
    kinds = onehot.shape[0]
    hit = lax.broadcasted_iota(jnp.int32, (kinds, span), 0) == here
    plain = jnp.where(hit, 1.0, 0.0).astype(BF16)
    for start in range(0, span, 128):
        offset = lax.broadcasted_iota(jnp.int32, (span, 128), 0)
        column = lax.broadcasted_iota(jnp.int32, (span, 128), 1) + start
        turn = (offset + column == rows) | (offset + column == rows + span)
        onehot[:, start : start + 128] = mm(plain, jnp.where(turn, 1.0, 0.0).astype(BF16))

    length = len_ref[lax.div(z_me, halves)]
    i = lax.broadcasted_iota(jnp.int32, mask.shape, 0)
    column = lax.broadcasted_iota(jnp.int32, mask.shape, 1)
    own = column - rows
    limit = jnp.where(half > 0, length, 0)
    ok = ((own < 0) & (column < limit)) | ((own >= 0) & (own <= i) & (own + half * rows < length))
    mask[...] = jnp.where(ok, 0.0, MASKED)
    tick(1)
    enc_copy.start()
    for copy in tables:
        copy.wait()
    for r in range(parts):
        table = table_own[...] if r == 0 else table_far[r]
        diag[r] = jnp.dot(
            table[:, 0 : onehot.shape[0]],
            onehot[...],
            precision=lax.Precision.HIGHEST,
            preferred_element_type=F32,
        )

    @pl.when(half == 0)
    def _():
        x_copy.wait_send()
        xa[...] = x_ref[...]

    @pl.when(half == 1)
    def _():
        x_copy.wait_recv()

    nbuf[0:rows, :] = low(norm_rows(xa[...].astype(F32), line_of(gain1))[0])

    def heads(phase, r):
        n = all_keys[phase]
        slot = lax.rem(r, 2)
        outs = []
        for j in range(3):
            q_h = q_in[slot, :, DH * j : DH * (j + 1)]
            k_h = kv_in[slot, 0:n, DH * j : DH * (j + 1)]
            v_h = kv_in[slot, 0:n, DH * (3 + j) : DH * (4 + j)]
            dp_buf[j % 2, :, 0:n] = mm_nt(q_h, k_h)
            for a, m in chunks(rows, 32):
                s = dp_buf[j % 2, a : a + m, 0:n]
                if phase == 0:
                    line = jnp.broadcast_to(diag[r, j : j + 1, :], (m, diag.shape[2]))
                    grid = pltpu.roll(line, a, 1, stride=1, stride_axis=0)
                    s = s + grid[:, 0:n] + mask[a : a + m, :]
                top = jnp.max(s, axis=1, keepdims=True)
                p_in[slot, j, a : a + m, 0:n] = low(jnp.exp(s - top))
            wide = jnp.concatenate([v_h, jnp.ones_like(v_h)], axis=1)
            mixed = mm(p_in[slot, j, :, 0:n], wide)
            outs.append(low(mixed[:, 0:DH] / mixed[:, DH : 2 * DH]))
            l_in[slot, :, 32 * j : 32 * (j + 1)] = mixed[:, DH : DH + 32]
        o_in[slot] = jnp.concatenate(outs, axis=1)

    def attention(phase, r, key_rows, query_rows):
        slot = lax.rem(r, 2)
        w_wait(phase, r, 0)
        w_next(phase, r, 0)

        @pl.when(r >= 2)
        def _():
            keep_wait(phase, r - 2)

        if phase == 1:

            @pl.when(r < 2)
            def _():
                keep_wait(0, r + 2)

        kv_in[slot, 0 : all_keys[phase]] = low(mm_nt(key_rows, block(w, slot, 0, 0, 384)))
        q_in[slot] = low(mm_nt(query_rows, block(w, slot, 0, 384, 576)))
        heads(phase, r)
        acc[...] += mm(o_in[slot], block(w, slot, 0, 576, 768))
        for copy in keeps(phase, r):
            copy.start()

    def take(g, k):
        gather.arrived(g)
        far_copy(g, 1, 1, k).start()

    acc[...] = x_ref[...].astype(F32)

    def self_step(r, carry):
        attention(0, r, nbuf[...], nbuf[rows : 2 * rows, :])
        at(r, 0, (tick, 2), (tick, 3), (tick, 4), (take, 0, 0))
        at(r, 1, (tick, 5))
        at(r, 2, (tick, 6), (own_start, 1, 0))
        at(r, 3, (tick, 7))
        return carry

    lax.fori_loop(0, parts, self_step, 0)
    x1[...] = acc[...]
    n2[...] = low(norm_rows(acc[...], line_of(gain2))[0])

    turns = [onehot[...]] + [pltpu.roll(onehot[...], k, 1) for k in range(1, 8)]
    spread[...] = jnp.transpose(jnp.concatenate(turns, axis=0))

    enc_copy.wait()
    enc_here.wait()

    def cross_step(r, carry):
        attention(1, r, enc[...].reshape(keys, width), n2[...])
        at(r, 0, (tick, 8), (take, 1, 0))
        at(r, 1, (tick, 9))
        at(r, 2, (tick, 10), (own_start, 2, 0))
        at(r, 3, (tick, 11))
        return carry

    lax.fori_loop(0, parts, cross_step, 0)
    x2[...] = acc[...]
    n3[...] = low(norm_rows(acc[...], line_of(gain3))[0])

    own_start(3, 1)
    rows_t[...] = flip(cot_ref[...])

    def inner_step(r, carry):
        slot = lax.rem(r, 2)
        w_wait(2, r, 0)
        w_next(2, r, 0)
        for a, n in chunks(rows, 64):
            v = mm(n3[a : a + n, :], block(w, slot, 0))
            sq = v * v
            t = jnp.tanh(v * (ROOT + ROOT * CUBE * sq))
            cdf = 0.5 + 0.5 * t
            hid[r, a : a + n, :] = low(v * cdf)
            slope[r, a : a + n, :] = low(
                cdf + 0.5 * v * (1.0 - t * t) * (ROOT + 3.0 * ROOT * CUBE * sq)
            )
        put(r, low(mm(rows_t[...], hid[r])))
        store(r).start()
        at(r, 0, (take, 2, 0))
        at(r, 1, (tick, 12))
        at(r, 2, (own_start, 2, 0))
        at(r, 3, (tick, 13))
        store(r).wait()
        at(r, 2, (leave, 0))
        at(r, 3, (leave, 1))
        return carry

    lax.fori_loop(0, parts, inner_step, 0)
    for r in (parts - 2, parts - 1):
        keep_wait(1, r)
    rows_t2[...] = flip(n3[...])
    dn[...] = jnp.zeros_like(dn)
    leave(2)

    def outer_step(r, carry):
        slot = lax.rem(r, 2)
        w_wait(3, r, 1)
        w_next(3, r, 1)
        w_wait(2, r, 0)

        @pl.when(r + 1 < parts)
        def _():
            far_copy(2, r + 1, lax.rem(r + 1, 2), 0).start()

        @pl.when(r + 1 == parts)
        def _():
            back_prefetch(1, jnp.int32(0))

        dh = low(mm_nt(cot_ref[...], block(w, slot, 1)))
        slope[r] = low(dh.astype(F32) * slope[r].astype(F32))
        put(4 + r, low(mm(rows_t2[...], slope[r])))
        store(4 + r).start()
        dn[...] += mm_nt(slope[r], block(w, slot, 0))
        store(4 + r).wait()
        at(r, 0, (leave, 3), (b, 0), (take, 3, 1))
        at(r, 1, (leave, 4), (b, 1), (z, 0))
        at(r, 2, (leave, 5), (b, 2), (z, 1))
        return carry

    lax.fori_loop(0, parts, outer_step, 0)
    def keep_sum(g, value):
        part = width_all // 2
        small[2 * g : 2 * g + 1, :] = value[:, 0:part]
        small[2 * g + 1 : 2 * g + 2, :] = value[:, part:]

    small[...] = jnp.zeros_like(small)
    back, sum3 = norm_back(dn[...], x2[...], line_of(gain3))
    dn[...] = cot_ref[...].astype(F32) + back
    keep_sum(2, sum3)
    leave(6)
    b(3)
    z(2)

    def heads_back(r, do, n, with_diag, between):
        slot = lax.rem(r, 2)
        q, kv, o = q_in[slot], kv_in.at[slot], o_in[slot].astype(F32)
        do_all = []
        delta_all = []
        for j in range(3):
            do_h = do[:, DH * j : DH * (j + 1)]
            inv = 1.0 / l_in[slot, :, 32 * j : 32 * j + 1]
            o_h = o[:, DH * j : DH * (j + 1)]
            delta_all.append(jnp.sum(do_h * o_h * inv, axis=1, keepdims=True))
            do_all.append(do_h * inv)
        do_t = low(jnp.transpose(jnp.concatenate(do_all, axis=1)))
        q_t = flip(q)
        dq = []
        for j in range(3):
            p_h = p_in.at[slot, j]
            k_h = kv[0:n, DH * j : DH * (j + 1)]
            v_h = kv[0:n, DH * (3 + j) : DH * (4 + j)]
            dp_buf[j % 2, :, 0:n] = mm_nt(low(do_all[j]), v_h)
            total = None
            for s, m in chunks(rows, 32):
                ds = low(
                    p_h[s : s + m, 0:n].astype(F32)
                    * (dp_buf[j % 2, s : s + m, 0:n] - delta_all[j][s : s + m, :])
                )
                ds_buf[j % 2, s : s + m, 0:n] = ds
                if with_diag:
                    width = diag_acc.shape[2]
                    wide = jnp.concatenate([ds.astype(F32), jnp.zeros((m, width - n), F32)], axis=1)
                    for b in range(0, m, 8):
                        turned = pltpu.roll(wide[b : b + 8, :], (width - s - b) % width, 1)
                        total = turned if total is None else total + turned
            if with_diag:
                diag_acc[which(r) * 3 + j] = total
            ds_h = ds_buf[j % 2, :, 0:n]
            dq.append(low(mm(ds_h, k_h)))
            dkv_t[DH * j : DH * (j + 1), 0:n] = mm(q_t[DH * j : DH * (j + 1), :], ds_h)
            dkv_t[DH * (3 + j) : DH * (4 + j), 0:n] = mm(
                do_t[DH * j : DH * (j + 1), :], p_h[:, 0:n]
            )
            if j == 1:
                between()
        return jnp.concatenate(dq, axis=1), low(jnp.transpose(dkv_t[:, 0:n]))

    def attention_step(phase, i, middle):
        slot = lax.rem(i, 2)
        n = all_keys[phase]
        t = 12 - 4 * phase + i
        back_wait(phase, i)

        @pl.when(i + 1 < parts)
        def _():
            back_prefetch(phase, i + 1)

        if phase == 1:

            @pl.when(i + 1 == parts)
            def _():
                back_prefetch(0, jnp.int32(0))

        do = low(mm_nt(low(dn[...]), block(w, slot, 0, 576, 768))).astype(F32)
        dq, dkv = heads_back(i, do, n, phase == 0, lambda: middle(i))
        put(t, low(mm(keys_t[:, 0:n], dkv)))
        both = [low(mm(rows_t2[...], dq)), low(mm(rows_t[...], o_in[slot]))]
        put(t, jnp.concatenate(both, axis=1), 384)
        store(t).start()
        acc[...] += mm(dq, block(w, slot, 0, 384, 576))
        enc_acc[0:n, :] += mm(dkv, block(w, slot, 0, 0, 384))
        store(t).wait()

    rows_t[...] = flip(low(dn[...]))
    rows_t2[...] = flip(n2[...])
    keys_t[...] = flip(enc[...].reshape(keys, width_all))
    acc[...] = jnp.zeros_like(acc)
    enc_acc[...] = jnp.zeros_like(enc_acc)

    def cross_back_step(i, carry):
        def middle(i):
            at(i, 0, (leave, 7), (b, 4), (z, 3))
            at(i, 1, (leave, 8), (b, 6), (z, 5))
            at(i, 2, (b, 7), (z, 6))
            at(i, 3, (leave, 10), (b, 8), (z, 7))

        attention_step(1, i, middle)
        at(i, 0, (b, 5), (z, 4))
        at(i, 1, (leave, 9))
        at(i, 3, (leave, 11))
        return carry

    lax.fori_loop(0, parts, cross_back_step, 0)
    enc[...] = low(enc_acc[...]).reshape(enc.shape)
    denc_copy.start()
    back, sum2 = norm_back(acc[...], x1[...], line_of(gain2))
    dn[...] += back
    keep_sum(1, sum2)
    b(9)
    z(8)

    own_start(3, 1)
    far_copy(3, 1, 1, 1).start()
    rows_t[...] = flip(low(dn[...]))
    rows_t2[...] = flip(nbuf[rows : 2 * rows, :])
    keys_t[:, 0:own_keys] = flip(nbuf[...])
    acc[...] = jnp.zeros_like(acc)
    enc_acc[0:own_keys, :] = jnp.zeros((own_keys, width_all), F32)

    def self_back_step(i, carry):
        def middle(i):
            at(i, 0, (a, 11), (b, 10), (z, 9))
            at(i, 1, (a, 12), (b, 11), (z, 10))
            at(i, 2, (a, 13), (b, 12), (z, 11))
            at(i, 3, (a, 14), (b, 13), (z, 12))

        attention_step(0, i, middle)
        at(i, 0, (c, 12))
        at(i, 1, (c, 13))
        at(i, 2, (c, 14))
        at(i, 3, (c, 15))
        return carry

    lax.fori_loop(0, parts, self_back_step, 0)
    for r in (2, 3):
        far_copy(3, r, r - 2, 0).start()
    gain = line_of(gain1)
    back, sum1a = norm_back(enc_acc[0:rows, :], xa[...].astype(F32), gain)
    n2[...] = low(back)

    @pl.when(half == 1)
    def _():
        dxa_copy.start()

    a(15)
    b(14)
    z(13)
    back, sum1 = norm_back(
        acc[...] + enc_acc[rows : 2 * rows, :], x_ref[...].astype(F32), gain
    )
    dn[...] += back
    keep_sum(0, sum1 + sum1a)
    count = 8 * diag_acc.shape[0]
    turned = jnp.dot(
        diag_acc[...].reshape(count, diag_acc.shape[2]),
        spread[...],
        precision=lax.Precision.HIGHEST,
        preferred_element_type=F32,
    )
    kinds = onehot.shape[0]
    row = lax.rem(lax.broadcasted_iota(jnp.int32, turned.shape, 0), 8)
    place_of = lax.div(lax.broadcasted_iota(jnp.int32, turned.shape, 1), kinds)
    turned = jnp.where(row == place_of, turned, 0.0)
    turned = jnp.sum(turned.reshape(count // 8, 8, turned.shape[1]), axis=1)
    table = turned[:, 0:kinds]
    for k in range(1, 8):
        table = table + turned[:, kinds * k : kinds * (k + 1)]
    for r in range(parts):
        at = lax.rem(z_me + r, parts)
        for p in range(parts):

            @pl.when(at == p)
            def _(r=r, p=p):
                for j in range(3):
                    lane = kinds * (3 * p + j)
                    small[6:7, lane : lane + kinds] = table[3 * r + j : 3 * r + j + 1]

    sums.start(small[...])
    for copy in own_copies(3, 1):
        copy.wait()
    x2[...] += mm(hid[0], block(w, 0, 1))
    far_copy(3, 1, 1, 1).wait()
    x2[...] += mm(hid[1], block(w, 1, 1))
    sums.turn()
    b(15)
    z(14)
    for r in (2, 3):
        far_copy(3, r, r - 2, 0).wait()
        x2[...] += mm(hid[r], block(w, r - 2, 0))
    result_ref[...] = low(x2[...])
    denc_copy.wait()
    enc[half] = low(enc[half].astype(F32) + denc_in[...].astype(F32))
    denc_done = pltpu.make_async_copy(enc.at[half], denc_out, out_sem.at[0])
    denc_done.start()
    z(15)

    @pl.when(half == 1)
    def _():
        dxa_copy.wait_send()
        n3[...] = low(dn[...])

    @pl.when(half == 0)
    def _():
        dxa_copy.wait_recv()
        n3[...] = low(dn[...] + dxa_in[...].astype(F32))

    dx_done = pltpu.make_async_copy(n3, dx_out, out_sem.at[1])
    dx_done.start()
    scatter.finish()
    small_out[...] = sums.result()
    for t in range(TICKS):
        scatter.c_copy(t, away(t)).wait_send()
    gather.sent()
    denc_done.wait()
    dx_done.wait()


def finish_kernel(
    result_in, dx, denc, total, small,
    result, input_grad, encoder_grad,
    g_gain1, gsq, gsk, gsv, gso, g_gain2, gcq, gck, gcv, gco, g_gain3, gfi, gfo, lines,
):
    result[...] = result_in[...]
    input_grad[...] = dx[...]
    encoder_grad[...] = denc[...]
    width = result.shape[1]
    for g, (k, v, q, o) in enumerate(((gsk, gsv, gsq, gso), (gck, gcv, gcq, gco))):
        k[...] = total[g, :, 0:192]
        v[...] = total[g, :, 192:384]
        q[...] = total[g, :, 384:576]
        o[...] = jnp.transpose(total[g, :, 576:768])
    gfi[...] = total[2]
    gfo[...] = total[3]
    for row, gain in enumerate((g_gain1, g_gain2, g_gain3)):
        part = small[2 * row : 2 * row + 2, :]
        gain[...] = jnp.concatenate([part[0:1], part[1:2]], axis=1).reshape(width)
    z = lax.axis_index("mp")
    for p in range(4):

        @pl.when(z == p)
        def _(p=p):
            kinds = lines.shape[1]
            for j in range(3):
                lane = kinds * (3 * p + j)
                lines[j : j + 1, :] = small[6:7, lane : lane + kinds]


def across(value, axis, n_dp):
    groups = n_dp // 8
    whole = lax.all_gather(value, "dp", axis=0, tiled=False)
    whole = whole.reshape(groups, 8, *value.shape).sum(0)
    whole = jnp.concatenate([whole[k] for k in range(8)], axis=axis)
    share = whole.shape[axis] // n_dp
    return lax.dynamic_slice_in_dim(whole, lax.axis_index("dp") * share, share, axis)


def across_small(value, n_dp):
    whole = lax.all_gather(value, "dp", axis=0, tiled=False)
    return whole.reshape(n_dp // 8, 8, *value.shape)[:, 0].sum(0)


def body(
    inputs, encoded, cotangent, lengths, buckets,
    self_gain, self_query, self_key, self_value, self_output, bias_table,
    cross_gain, cross_query, cross_key, cross_value, cross_output,
    feed_gain, feed_inner, feed_output_weight,
):
    rows, width = inputs.shape
    parts = lax.axis_size("mp")
    n_dp = lax.axis_size("dp")
    halves = parts // lengths.shape[0]
    assert halves == 2 and buckets.shape[0] == 2 * rows and parts == 4
    z = lax.axis_index("mp")
    enc_rows = encoded.shape[0]
    vmem = pl.BlockSpec(memory_space=pltpu.VMEM)
    smem = pl.BlockSpec(memory_space=pltpu.SMEM)
    hbm = pl.BlockSpec(memory_space=pl.ANY)
    sds = jax.ShapeDtypeStruct

    share = width // 8
    diag = 1024
    heads = 3 * parts
    keys = 2 * enc_rows
    gains = [self_gain, cross_gain, feed_gain]
    split = lambda v: v.reshape(2, share, width)
    whole = lambda v: v.reshape(4, 2, share, width)
    kinds = bias_table.shape[0]
    kept = [
        kind
        for n in (2 * rows, keys)
        for kind in (
            sds((parts, rows, 192), BF16),
            sds((parts, n, 384), BF16),
            sds((heads, rows, n), BF16),
            sds((parts, rows, 192), BF16),
            sds((parts, rows, 128), F32),
        )
    ]
    half_share = share // 2
    bf, ff = (lambda *shape: pltpu.VMEM(shape, BF16)), (lambda *shape: pltpu.VMEM(shape, F32))
    dma = lambda *shape: pltpu.SemaphoreType.DMA(shape)
    result, summed, small, input_grad, encoder_grad, *_ = pl.pallas_call(
        functools.partial(layer_kernel, halves),
        out_shape=[
            sds((rows, width), BF16),
            sds((4, share, width), F32),
            sds((8, width // 2), F32),
            sds((rows, width), BF16),
            sds((enc_rows, width), BF16),
            sds((4, parts, 4, 2, share, width), BF16),
            sds((TICKS, 4, 2, share, width), BF16),
            *kept,
        ],
        in_specs=[smem, vmem, vmem, hbm] + [vmem] * 5 + [hbm] * 10,
        out_specs=[vmem] * 3 + [hbm] * (4 + len(kept)),
        scratch_shapes=[
            bf(2, 2, 4, 2, share, width), bf(2, enc_rows, width), ff(parts, 8, diag),
            ff(rows, 2 * rows), ff(kinds, diag), ff(diag, 8 * kinds), bf(rows, width), ff(8, 128), ff(parts, 8, 128),
            bf(2 * rows, width), bf(rows, width), bf(rows, width),
            bf(2, rows, 192), bf(2, keys, 384), bf(2, 3, rows, keys), bf(2, rows, 192),
            ff(2, rows, 128), ff(rows, width), ff(rows, width),
            bf(parts, rows, width), bf(parts, rows, width), ff(rows, width), ff(rows, width),
            bf(2, 4, 2, share, width), bf(2, 4, share, width),
            bf(width, rows), bf(width, rows), bf(width, keys),
            ff(2, rows, keys), bf(2, rows, keys), ff(384, keys), ff(keys, width),
            ff(heads, 8, diag),
            bf(rows, width), bf(enc_rows, width), ff(8, width // 2),
            bf(C_RING, 4, share, width), bf(A_RING, 2, 2, half_share, width),
            bf(B_RING, 2, half_share, width), bf(TICKS, share, width),
            bf(OUT_RING, 2, 2, half_share, width), bf(KEEP, 2, 2, half_share, width),
            bf(OUT_RING, 2, half_share, width), ff(KEEP, 2, half_share, width),
            bf(Z_RING, share, width), ff(8, 8, width // 2), ff(parts, 8, width // 2),
            dma(2, 2), dma(2, 4), pltpu.SemaphoreType.DMA, dma(5, 2), dma(5, 2), dma(2), dma(2),
            dma(2),
            dma(Gather.chunks, parts - 1), dma(Gather.chunks, parts - 1),
            dma(Gather.chunks, 5), dma(Gather.chunks, 5), dma(7), dma(7),
            dma(2, 6, TICKS), pltpu.SemaphoreType.REGULAR((5,)), dma(10), dma(10),
        ],
        compiler_params=pltpu.CompilerParams(
            collective_id=1, has_side_effects=True, vmem_limit_bytes=VMEM_BYTES
        ),
        name="layer",
    )(
        lengths, inputs, cotangent, encoded, *gains, buckets, bias_table.T,
        split(self_key.T), split(self_value.T), split(self_query.T), split(self_output),
        split(cross_key.T), split(cross_value.T), split(cross_query.T), split(cross_output),
        whole(feed_inner), whole(feed_output_weight),
    )

    f32 = lambda *shape: sds(shape, F32)
    outs = pl.pallas_call(
        finish_kernel,
        out_shape=[
            sds((rows, width), BF16), sds((rows, width), BF16), sds((enc_rows, width), BF16),
            f32(width), f32(share, 192), f32(share, 192), f32(share, 192), f32(192, share),
            f32(width), f32(share, 192), f32(share, 192), f32(share, 192), f32(192, share),
            f32(width), f32(share, width), f32(share, width), f32(3, kinds),
        ],
        in_specs=[vmem] * 5,
        out_specs=[vmem] * 17,
        name="finish",
    )(result, input_grad, encoder_grad, summed, small)
    result, input_grad, encoder_grad, *grads, lines = outs
    if n_dp > 8:
        axes = (None, 0, 0, 0, 1, None, 0, 0, 0, 1, None, 0, 0)
        grads = [
            across_small(value, n_dp) if axis is None else across(value, axis, n_dp)
            for value, axis in zip(grads, axes)
        ]
        lines = across_small(lines, n_dp)
    return (result, input_grad, encoder_grad, *grads[0:5], lines.T, *grads[5:-1], grads[-1].T)


def solution(mesh):
    rows = P(("dp", "mp"), None)
    across, down = P(None, "mp"), P("mp", None)
    return jax.shard_map(
        body,
        mesh=mesh,
        in_specs=(
            rows, rows, rows, P("dp"), P(),
            P(), across, across, across, down, across,
            P(), across, across, across, down,
            P(), across, down,
        ),
        out_specs=(
            rows, rows, rows,
            P(), P("dp", "mp"), P("dp", "mp"), P("dp", "mp"), P("mp", "dp"), P(None, "mp"),
            P(), P("dp", "mp"), P("dp", "mp"), P("dp", "mp"), P("mp", "dp"),
            P(), P("dp", "mp"), P("mp", "dp"),
        ),
        check_vma=False,
    )
```

```python
import functools

import jax
import jax.numpy as jnp
from jax import lax
from jax.experimental import pallas as pl
from jax.experimental.pallas import tpu as pltpu
from jax.sharding import PartitionSpec as P

EPS = 1e-06
MASKED = -1e30
DH = 64
F32 = jnp.float32
BF16 = jnp.bfloat16
VMEM_BYTES = 62 << 20
ROOT = 0.7978845608028654
CUBE = 0.044715


def mm(a, b):
    return jnp.dot(a, b, preferred_element_type=F32)


def mm_nt(a, b):
    return lax.dot_general(a, b, (((1,), (1,)), ((), ())), preferred_element_type=F32)


def line_of(ref):
    return ref[...].reshape(1, ref.shape[0])


def low(v):
    return v.astype(BF16)


def flip(v):
    return jnp.transpose(v.astype(F32)).astype(BF16)


def norm_rows(v, gain):
    root = lax.rsqrt(jnp.mean(v * v, axis=-1, keepdims=True) + EPS)
    unit = v * root
    return unit * gain, unit, root


def norm_back(grad, v, gain):
    _, unit, root = norm_rows(v, gain)
    scaled = grad * gain
    back = root * (scaled - unit * jnp.mean(scaled * unit, axis=-1, keepdims=True))
    return back, jnp.sum(grad * unit, axis=0, keepdims=True)


def block(w, i, j, start=0, stop=None):
    part = w[i, j]
    part = part.reshape(part.shape[0] * part.shape[1] * part.shape[2], part.shape[3])
    return part[start:stop]


def half_of_sequence(halves):
    return lax.rem(lax.axis_index("mp"), halves)


def chunks(rows, step):
    return [(r, min(step, rows - r)) for r in range(0, rows, step)]


MESH_ID = pl.DeviceIdType.MESH


def places():
    d = lax.axis_index("dp")
    z = lax.axis_index("mp")
    lo = lax.rem(d, 8)
    core = lax.rem(lo, 2)
    x = lax.rem(lax.div(lo, 2), 2)
    y = lax.div(lo, 4)
    d_core = d + 1 - 2 * core
    d_x = d + 2 - 4 * x
    d_y = d + 4 - 8 * y
    return d, z, core, x, y, d_core, d_x, d_y


def peer(k):
    d = lax.axis_index("dp")
    lo = lax.rem(d, 8)
    return d - lo + lax.rem(lo + k, 8)


def greet(z_parts, everyone):
    d, z, _, _, _, d_core, d_x, d_y = places()
    barrier = pltpu.get_barrier_semaphore()
    near = [peer(k) for k in range(1, 8)] if everyone else [d_core, d_x, d_y]
    for who in near:
        pl.semaphore_signal(barrier, inc=1, device_id=(who, z), device_id_type=MESH_ID)
    for step in range(1, z_parts):
        pl.semaphore_signal(
            barrier, inc=1, device_id=(d, lax.rem(z + step, z_parts)), device_id_type=MESH_ID
        )
    return lambda: pl.semaphore_wait(barrier, len(near) + z_parts - 1)


def remote(src, dst, send, recv, who):
    return pltpu.make_async_remote_copy(
        src_ref=src, dst_ref=dst, send_sem=send, recv_sem=recv, device_id=who, device_id_type=MESH_ID
    )


class Gather:
    parts_of_group = 3
    chunks = 12
    ahead = 6

    def __init__(self, mine, wg, z_send, z_recv, s_send, s_recv):
        self.mine, self.wg = mine, wg
        self.z_sems, self.s_sems = (z_send, z_recv), (s_send, s_recv)
        self.parts = wg.shape[1]
        self.place = places()

    def rows(self, k):
        some = self.wg.shape[4] // self.parts_of_group
        return k // self.parts_of_group, pl.ds((k % self.parts_of_group) * some, some)

    def z_copy(self, k, step, part=0):
        d, z, core, x, y, *_ = self.place
        yx = 2 * y + x
        g, rows = self.rows(k)
        mine = self.mine[g]
        src = mine[part].at[core, rows] if isinstance(mine, tuple) else mine.at[yx, core, rows]
        return remote(
            src,
            self.wg.at[g, self.parts - step, yx, core, rows],
            self.z_sems[0].at[k, step - 1],
            self.z_sems[1].at[k, step - 1],
            (d, lax.rem(z + step, self.parts)),
        )

    def s_copy(self, k, n):
        d, z, core, x, y, d_core, d_x, d_y = self.place
        rest = pl.ds(1, self.parts - 1)
        g, rows = self.rows(k)
        width = self.wg.shape[5]
        if n < 2:
            ref = self.wg.at[g, rest, 2 * y + x, core, rows]
            who = (d_x, d_y)[n]
        elif n == 2:
            ref = self.wg.at[g, rest, 2 * y + 1 - x, core, rows, pl.ds(0, width // 2)]
            who = d_y
        elif n == 3:
            ref = self.wg.at[g, rest, 2 * (1 - y) + x, core, rows, pl.ds(width // 2, width // 2)]
            who = d_x
        else:
            ref = self.wg.at[g, rest, :, core, rows]
            who = d_core
        return remote(ref, ref, self.s_sems[0].at[k, n], self.s_sems[1].at[k, n], (who, z))

    def z_start(self, k):
        _, _, _, x, y, *_ = self.place
        if isinstance(self.mine[self.rows(k)[0]], tuple):
            for part in range(4):

                @pl.when(2 * y + x == part)
                def _(part=part):
                    for step in range(1, self.parts):
                        self.z_copy(k, step, part).start()

        else:
            for step in range(1, self.parts):
                self.z_copy(k, step).start()

    def tick(self, k):
        if k < self.chunks:
            for step in range(1, self.parts):
                self.z_copy(k, step).wait_recv()
            self.s_copy(k, 0).start()
            self.s_copy(k, 1).start()
            if k + self.ahead < self.chunks:
                self.z_start(k + self.ahead)
        if 0 <= k - 1 < self.chunks:
            self.s_copy(k - 1, 0).wait_recv()
            self.s_copy(k - 1, 2).start()
            self.s_copy(k - 1, 1).wait_recv()
            self.s_copy(k - 1, 3).start()
        if 0 <= k - 2 < self.chunks:
            self.s_copy(k - 2, 2).wait_recv()
            self.s_copy(k - 2, 3).wait_recv()
            self.s_copy(k - 2, 4).start()

    def arrived(self, g):
        for k in range(self.parts_of_group * g, self.parts_of_group * (g + 1)):
            self.s_copy(k, 4).wait_recv()

    def sent(self):
        for k in range(self.chunks):
            for step in range(1, self.parts):
                self.z_copy(k, step).wait_send()
            for n in range(5):
                self.s_copy(k, n).wait_send()


C_RING = 4
KEEP = 4
OUT_RING = 4
A_RING = 6
B_RING = 6
Z_RING = 6
TICKS = 16


class Scatter:
    def __init__(self, bufs, sems, credit):
        (
            self.c_in, self.a_in, self.b_in, self.z_in,
            self.a_out, self.a_keep, self.b_out, self.b_keep, self.z_out, self.total,
        ) = bufs
        self.sems, self.credit = sems, credit
        self.parts = 4
        self.share = self.z_out.shape[1]
        self.place = places()

    def block(self, t):
        if t < 8:
            return 3 - t // 4, t % 4
        return 3 - t // 4, (t + 1) % 4

    def copy(self, k, t, src, dst, who):
        return remote(src, dst, self.sems.at[0, k, t], self.sems.at[1, k, t], who)

    def c_copy(self, t, src):
        z, d_core = self.place[1], self.place[5]
        return self.copy(0, t, src, self.c_in.at[t % C_RING], (d_core, z))

    def a_copy(self, t, q):
        _, z, *_, d_x, d_y = self.place
        src, dst = self.a_out.at[t % OUT_RING, q], self.a_in.at[t % A_RING, q]
        return self.copy(1 + q, t, src, dst, ((d_x, d_y)[q], z))

    def b_copy(self, t, q):
        _, z, *_, d_x, d_y = self.place
        src, dst = self.b_out.at[t % OUT_RING, q], self.b_in.at[t % B_RING, q]
        return self.copy(3 + q, t, src, dst, ((d_y, d_x)[q], z))

    def z_copy(self, t):
        d, z = self.place[:2]
        who = (d, lax.rem(z + self.block(t)[1], self.parts))
        return self.copy(5, t, self.z_out.at[t % Z_RING], self.z_in.at[t], who)

    def rows(self, q):
        return pl.ds(q * (self.share // 2), self.share // 2)

    def c_start(self, t, src):
        if t >= C_RING:
            pl.semaphore_wait(self.credit.at[0], 1)
        self.c_copy(t, src).start()

    def a_start(self, t, mine, src):
        _, _, _, x, y, d_core, *_ = self.place
        slot, ring, held = t % OUT_RING, t % C_RING, t % KEEP
        if t >= OUT_RING:
            self.a_copy(t - OUT_RING, 0).wait_send()
            self.a_copy(t - OUT_RING, 1).wait_send()
        self.c_copy(t, src).wait_recv()
        for q in range(2):
            rows = self.rows(q)
            for k in range(2):
                send = (2 * k + 1 - x, 2 * (1 - y) + k)[q]
                self.a_out[slot, q, k] = mine[send, rows] + self.c_in[ring, send, rows]
            if t >= A_RING:
                pl.semaphore_wait(self.credit.at[1 + q], 1)
            self.a_copy(t, q).start()
        for q in range(2):
            rows = self.rows(q)
            for k in range(2):
                keep = (2 * k + x, 2 * y + k)[q]
                self.a_keep[held, q, k] = mine[keep, rows] + self.c_in[ring, keep, rows]
        if t < TICKS - C_RING:
            self.free(0, d_core)

    def free(self, k, who):
        pl.semaphore_signal(
            self.credit.at[k], inc=1, device_id=(who, self.place[1]), device_id_type=MESH_ID
        )

    def b_start(self, t):
        _, _, _, x, y, _, d_x, d_y = self.place
        slot, held, ring = t % OUT_RING, t % KEEP, t % A_RING
        if t >= OUT_RING:
            self.b_copy(t - OUT_RING, 0).wait_send()
            self.b_copy(t - OUT_RING, 1).wait_send()
        for q in range(2):
            keep = (y, x)[q]
            send = 1 - keep
            self.a_copy(t, q).wait_recv()
            self.b_out[slot, q] = self.a_keep[held, q, send] + self.a_in[ring, q, send]
            if t >= B_RING:
                pl.semaphore_wait(self.credit.at[3 + q], 1)
            self.b_copy(t, q).start()
            self.b_keep[held, q] = self.a_keep[held, q, keep].astype(F32) + self.a_in[
                ring, q, keep
            ].astype(F32)
            if t < TICKS - A_RING:
                self.free(1 + q, (d_x, d_y)[q])

    def z_start(self, t):
        slot, held = t % Z_RING, t % KEEP
        g, r = self.block(t)
        if t >= Z_RING and self.block(t - Z_RING)[1] > 0:
            self.z_copy(t - Z_RING).wait_send()
        for q in range(2):
            self.b_copy(t, q).wait_recv()
            done = self.b_keep[held, q] + self.b_in[t % B_RING, q].astype(F32)
            if r == 0:
                self.total[g, self.rows(q)] = done
            else:
                self.z_out[slot, self.rows(q)] = low(done)
            if t < TICKS - B_RING:
                self.free(3 + q, self.place[7 - q])
        if r > 0:
            self.z_copy(t).start()

    def finish(self):
        for t in range(TICKS - OUT_RING, TICKS):
            for q in range(2):
                self.a_copy(t, q).wait_send()
                self.b_copy(t, q).wait_send()
        for t in range(TICKS):
            g, r = self.block(t)
            if r > 0:
                if t >= TICKS - Z_RING:
                    self.z_copy(t).wait_send()
                self.z_copy(t).wait_recv()
                self.total[g] += self.z_in[t].astype(F32)


class Sum:
    def __init__(self, near, far, send, recv):
        self.near, self.far = near, far
        self.send, self.recv = send, recv
        self.place = places()
        self.lo = lax.rem(self.place[0], 8)

    def near_copy(self, k):
        ref = self.near.at[self.lo]
        return remote(
            ref, ref, self.send.at[k - 1], self.recv.at[k - 1], (peer(k), self.place[1])
        )

    def far_copy(self, k):
        d, z = self.place[:2]
        ref = self.far.at[z]
        who = (d, lax.rem(z + k, self.far.shape[0]))
        return remote(ref, ref, self.send.at[6 + k], self.recv.at[6 + k], who)

    def start(self, value):
        self.near[self.lo] = value
        for k in range(1, 8):
            self.near_copy(k).start()

    def turn(self):
        for k in range(1, 8):
            self.near_copy(k).wait_send()
            sender = lax.rem(self.lo + 8 - k, 8)
            ref = self.near.at[sender]
            remote(
                ref, ref, self.send.at[k - 1], self.recv.at[k - 1], (peer(8 - k), self.place[1])
            ).wait_recv()
        value = self.near[0]
        for k in range(1, 8):
            value = value + self.near[k]
        self.far[self.place[1]] = value
        for k in range(1, self.far.shape[0]):
            self.far_copy(k).start()

    def result(self):
        d, z = self.place[:2]
        parts = self.far.shape[0]
        for k in range(1, parts):
            self.far_copy(k).wait_send()
            sender = lax.rem(z + parts - k, parts)
            ref = self.far.at[sender]
            remote(
                ref, ref, self.send.at[6 + k], self.recv.at[6 + k], (d, sender)
            ).wait_recv()
        value = self.far[0]
        for k in range(1, parts):
            value = value + self.far[k]
        return value


def layer_kernel(
    halves,
    len_ref, x_ref, cot_ref, enc_own, gain1, gain2, gain3, buckets_ref, table_in,
    sk, sv, sq, so, ck, cv, cq, co, fi, fo,
    result_ref, total_out, small_out, dx_out, denc_out,
    w_hbm, g_hbm, q1_hbm, kv1_hbm, p1_hbm, o1_hbm, l1_hbm, q2_hbm, kv2_hbm, p2_hbm, o2_hbm, l2_hbm,
    w, enc, diag, mask, onehot, spread, xa, table_own, table_far,
    nbuf, n2, n3, q_in, kv_in, p_in, o_in, l_in, x1, x2, hid, slope, acc, dn,
    g_buf, l_buf, rows_t, rows_t2, keys_t, dp_buf, ds_buf, dkv_t, enc_acc, diag_acc,
    dxa_in, denc_in, small,
    c_in, a_in, b_in, z_in, a_out, a_keep, b_out, b_keep, z_out, s_near, s_far,
    w_sem, own_sem, in_sem, ring_sem, keep_sem, store_sem, load_sem, out_sem,
    z_send, z_recv, s_send, s_recv, e_send, e_recv,
    sems, credit, n_send, n_recv,
):
    rows, width_all = x_ref.shape
    width = width_all
    parts = w_hbm.shape[1]
    place = places()
    d, z_me, core = place[:3]
    half = half_of_sequence(halves)
    mate = z_me + 1 - 2 * half
    keys = 2 * enc.shape[1]
    own_keys = 2 * rows
    all_keys = (own_keys, keys)
    entered = greet(parts, True)

    mine = ((sk, sv, sq, so), (ck, cv, cq, co), fi, fo)

    def own_copies(g, k):
        if g >= 2:
            return [pltpu.make_async_copy(mine[g], w.at[0, k], own_sem.at[k, 0])]
        return [
            pltpu.make_async_copy(ref, w.at[0, k, part], own_sem.at[k, part])
            for part, ref in enumerate(mine[g])
        ]

    def own_start(g, k):
        for copy in own_copies(g, k):
            copy.start()

    def far_copy(g, r, slot, k):
        return pltpu.make_async_copy(w_hbm.at[g, r], w.at[slot, k], w_sem.at[slot, k])

    def own_in_slot_one(g, k):
        if g >= 2:
            return [pltpu.make_async_copy(mine[g], w.at[1, k], own_sem.at[k, 0])]
        return [
            pltpu.make_async_copy(ref, w.at[1, k, part], own_sem.at[k, part])
            for part, ref in enumerate(mine[g])
        ]

    def w_wait(g, r, k):
        @pl.when(r == 0)
        def _():
            for copy in own_copies(g, k):
                copy.wait()

        @pl.when(r > 0)
        def _():
            far_copy(g, r, lax.rem(r, 2), k).wait()

    def w_next(g, r, k):
        @pl.when((r > 0) & (r + 1 < parts))
        def _():
            far_copy(g, r + 1, lax.rem(r + 1, 2), k).start()

    def which(i):
        return lax.rem(i + 1, parts)

    kept = (
        (q1_hbm, kv1_hbm, p1_hbm, o1_hbm, l1_hbm),
        (q2_hbm, kv2_hbm, p2_hbm, o2_hbm, l2_hbm),
    )

    def ring(phase, r, slot):
        n = all_keys[phase]
        q, kv, p, o, l = kept[phase]
        return [
            (q.at[r], q_in.at[slot]),
            (kv.at[r], kv_in.at[slot, 0:n]),
            (p.at[pl.ds(3 * r, 3)], p_in.at[slot, :, :, 0:n]),
            (o.at[r], o_in.at[slot]),
            (l.at[r], l_in.at[slot]),
        ]

    def keeps(phase, r):
        slot = lax.rem(r, 2)
        return [
            pltpu.make_async_copy(dst, src, keep_sem.at[k, slot])
            for k, (src, dst) in enumerate(ring(phase, r, slot))
        ]

    def keep_wait(phase, r):
        for copy in keeps(phase, r):
            copy.wait()

    def streams(phase, i):
        slot = lax.rem(i, 2)
        return [
            pltpu.make_async_copy(src, dst, ring_sem.at[k, slot])
            for k, (src, dst) in enumerate(ring(phase, which(i), slot))
        ]

    def back_prefetch(phase, i):
        @pl.when(i < parts - 1)
        def _():
            far_copy(phase, which(i), lax.rem(i, 2), 0).start()

        @pl.when(i == parts - 1)
        def _():
            for copy in own_in_slot_one(phase, 0):
                copy.start()

        for copy in streams(phase, i):
            copy.start()

    def back_wait(phase, i):
        @pl.when(i < parts - 1)
        def _():
            far_copy(phase, which(i), lax.rem(i, 2), 0).wait()

        @pl.when(i == parts - 1)
        def _():
            for copy in own_in_slot_one(phase, 0):
                copy.wait()

        for copy in streams(phase, i):
            copy.wait()

    enc_here = pltpu.make_async_copy(enc_own, enc.at[half], in_sem)
    own_start(0, 0)
    enc_here.start()
    entered()

    gather = Gather(mine, w_hbm, z_send, z_recv, s_send, s_recv)
    scatter = Scatter(
        (c_in, a_in, b_in, z_in, a_out, a_keep, b_out, b_keep, z_out, total_out), sems, credit
    )
    sums = Sum(s_near, s_far, n_send, n_recv)
    x_copy = remote(x_ref, xa, e_send.at[0], e_recv.at[0], (d, mate))
    enc_copy = remote(enc_own, enc.at[half], e_send.at[1], e_recv.at[1], (d, mate))
    dxa_copy = remote(n2, dxa_in, e_send.at[2], e_recv.at[2], (d, mate))
    denc_copy = remote(enc.at[1 - half], denc_in, e_send.at[3], e_recv.at[3], (d, mate))
    tables = [
        remote(
            table_own, table_far.at[parts - step], e_send.at[3 + step], e_recv.at[3 + step],
            (d, lax.rem(z_me + step, parts)),
        )
        for step in range(1, parts)
    ]

    def put(t, value, start=0):
        shape = g_buf.shape[1:4] + (value.shape[1],)
        g_buf[lax.rem(t, 2), :, :, :, start : start + value.shape[1]] = value.reshape(shape)

    def store(t):
        slot = lax.rem(t, 2)
        return pltpu.make_async_copy(g_buf.at[slot], g_hbm.at[t], store_sem.at[slot])

    def away(t):
        return g_hbm.at[t, :, 1 - core]

    def load(t):
        slot = t % 2
        return pltpu.make_async_copy(g_hbm.at[t, :, core], l_buf.at[slot], load_sem.at[slot])

    def c(t):
        scatter.c_start(t, away(t))
        load(t).start()

    def a(t):
        load(t).wait()
        scatter.a_start(t, l_buf.at[t % 2], away(t))

    def leave(t):
        c(t)
        if t >= 1:
            a(t - 1)

    b, z, tick = scatter.b_start, scatter.z_start, gather.tick

    def at(i, step, *moves):
        @pl.when(i == step)
        def _():
            for move, *args in moves:
                move(*args)

    gather.z_start(0)
    table_own[...] = jnp.zeros_like(table_own)
    table_own[0 : table_in.shape[0], 0 : table_in.shape[1]] = table_in[...]
    for copy in tables:
        copy.start()
    gather.z_start(1)

    @pl.when(half == 0)
    def _():
        x_copy.start()

    gather.z_start(2)
    for k in range(3, gather.ahead):
        gather.z_start(k)

    nbuf[rows : 2 * rows, :] = low(norm_rows(x_ref[...].astype(F32), line_of(gain1))[0])
    tick(0)

    slots = buckets_ref.shape[0]
    span = onehot.shape[1]
    here = jnp.concatenate(
        [line_of(buckets_ref), jnp.full((1, span - slots), -1, jnp.int32)], axis=1
    )
    kinds = onehot.shape[0]
    hit = lax.broadcasted_iota(jnp.int32, (kinds, span), 0) == here
    plain = jnp.where(hit, 1.0, 0.0).astype(BF16)
    for start in range(0, span, 128):
        offset = lax.broadcasted_iota(jnp.int32, (span, 128), 0)
        column = lax.broadcasted_iota(jnp.int32, (span, 128), 1) + start
        turn = (offset + column == rows) | (offset + column == rows + span)
        onehot[:, start : start + 128] = mm(plain, jnp.where(turn, 1.0, 0.0).astype(BF16))

    length = len_ref[lax.div(z_me, halves)]
    i = lax.broadcasted_iota(jnp.int32, mask.shape, 0)
    column = lax.broadcasted_iota(jnp.int32, mask.shape, 1)
    own = column - rows
    limit = jnp.where(half > 0, length, 0)
    ok = ((own < 0) & (column < limit)) | ((own >= 0) & (own <= i) & (own + half * rows < length))
    mask[...] = jnp.where(ok, 0.0, MASKED)
    tick(1)
    enc_copy.start()
    for copy in tables:
        copy.wait()
    for r in range(parts):
        table = table_own[...] if r == 0 else table_far[r]
        diag[r] = jnp.dot(
            table[:, 0 : onehot.shape[0]],
            onehot[...],
            precision=lax.Precision.HIGHEST,
            preferred_element_type=F32,
        )

    @pl.when(half == 0)
    def _():
        x_copy.wait_send()
        xa[...] = x_ref[...]

    @pl.when(half == 1)
    def _():
        x_copy.wait_recv()

    nbuf[0:rows, :] = low(norm_rows(xa[...].astype(F32), line_of(gain1))[0])

    def heads(phase, r):
        n = all_keys[phase]
        slot = lax.rem(r, 2)
        outs = []
        for j in range(3):
            q_h = q_in[slot, :, DH * j : DH * (j + 1)]
            k_h = kv_in[slot, 0:n, DH * j : DH * (j + 1)]
            v_h = kv_in[slot, 0:n, DH * (3 + j) : DH * (4 + j)]
            dp_buf[j % 2, :, 0:n] = mm_nt(q_h, k_h)
            for a, m in chunks(rows, 32):
                s = dp_buf[j % 2, a : a + m, 0:n]
                if phase == 0:
                    line = jnp.broadcast_to(diag[r, j : j + 1, :], (m, diag.shape[2]))
                    grid = pltpu.roll(line, a, 1, stride=1, stride_axis=0)
                    s = s + grid[:, 0:n] + mask[a : a + m, :]
                top = jnp.max(s, axis=1, keepdims=True)
                p_in[slot, j, a : a + m, 0:n] = low(jnp.exp(s - top))
            wide = jnp.concatenate([v_h, jnp.ones_like(v_h)], axis=1)
            mixed = mm(p_in[slot, j, :, 0:n], wide)
            outs.append(low(mixed[:, 0:DH] / mixed[:, DH : 2 * DH]))
            l_in[slot, :, 32 * j : 32 * (j + 1)] = mixed[:, DH : DH + 32]
        o_in[slot] = jnp.concatenate(outs, axis=1)

    def attention(phase, r, key_rows, query_rows):
        slot = lax.rem(r, 2)
        w_wait(phase, r, 0)
        w_next(phase, r, 0)

        @pl.when(r >= 2)
        def _():
            keep_wait(phase, r - 2)

        if phase == 1:

            @pl.when(r < 2)
            def _():
                keep_wait(0, r + 2)

        kv_in[slot, 0 : all_keys[phase]] = low(mm_nt(key_rows, block(w, slot, 0, 0, 384)))
        q_in[slot] = low(mm_nt(query_rows, block(w, slot, 0, 384, 576)))
        heads(phase, r)
        acc[...] += mm(o_in[slot], block(w, slot, 0, 576, 768))
        for copy in keeps(phase, r):
            copy.start()

    def take(g, k):
        gather.arrived(g)
        far_copy(g, 1, 1, k).start()

    acc[...] = x_ref[...].astype(F32)

    def self_step(r, carry):
        attention(0, r, nbuf[...], nbuf[rows : 2 * rows, :])
        at(r, 0, (tick, 2), (tick, 3), (tick, 4), (take, 0, 0))
        at(r, 1, (tick, 5))
        at(r, 2, (tick, 6), (own_start, 1, 0))
        at(r, 3, (tick, 7))
        return carry

    lax.fori_loop(0, parts, self_step, 0)
    x1[...] = acc[...]
    n2[...] = low(norm_rows(acc[...], line_of(gain2))[0])

    turns = [onehot[...]] + [pltpu.roll(onehot[...], k, 1) for k in range(1, 8)]
    spread[...] = jnp.transpose(jnp.concatenate(turns, axis=0))

    enc_copy.wait()
    enc_here.wait()

    def cross_step(r, carry):
        attention(1, r, enc[...].reshape(keys, width), n2[...])
        at(r, 0, (tick, 8), (take, 1, 0))
        at(r, 1, (tick, 9))
        at(r, 2, (tick, 10), (own_start, 2, 0))
        at(r, 3, (tick, 11))
        return carry

    lax.fori_loop(0, parts, cross_step, 0)
    x2[...] = acc[...]
    n3[...] = low(norm_rows(acc[...], line_of(gain3))[0])

    own_start(3, 1)
    rows_t[...] = flip(cot_ref[...])

    def inner_step(r, carry):
        slot = lax.rem(r, 2)
        w_wait(2, r, 0)
        w_next(2, r, 0)
        for a, n in chunks(rows, 64):
            v = mm(n3[a : a + n, :], block(w, slot, 0))
            sq = v * v
            t = jnp.tanh(v * (ROOT + ROOT * CUBE * sq))
            cdf = 0.5 + 0.5 * t
            hid[r, a : a + n, :] = low(v * cdf)
            slope[r, a : a + n, :] = low(
                cdf + 0.5 * v * (1.0 - t * t) * (ROOT + 3.0 * ROOT * CUBE * sq)
            )
        put(r, low(mm(rows_t[...], hid[r])))
        store(r).start()
        at(r, 0, (take, 2, 0))
        at(r, 1, (tick, 12))
        at(r, 2, (own_start, 2, 0))
        at(r, 3, (tick, 13))
        store(r).wait()
        at(r, 2, (leave, 0))
        at(r, 3, (leave, 1))
        return carry

    lax.fori_loop(0, parts, inner_step, 0)
    for r in (parts - 2, parts - 1):
        keep_wait(1, r)
    rows_t2[...] = flip(n3[...])
    dn[...] = jnp.zeros_like(dn)
    leave(2)

    def outer_step(r, carry):
        slot = lax.rem(r, 2)
        w_wait(3, r, 1)
        w_next(3, r, 1)
        w_wait(2, r, 0)

        @pl.when(r + 1 < parts)
        def _():
            far_copy(2, r + 1, lax.rem(r + 1, 2), 0).start()

        @pl.when(r + 1 == parts)
        def _():
            back_prefetch(1, jnp.int32(0))

        dh = low(mm_nt(cot_ref[...], block(w, slot, 1)))
        slope[r] = low(dh.astype(F32) * slope[r].astype(F32))
        put(4 + r, low(mm(rows_t2[...], slope[r])))
        store(4 + r).start()
        dn[...] += mm_nt(slope[r], block(w, slot, 0))
        store(4 + r).wait()
        at(r, 0, (leave, 3), (b, 0), (take, 3, 1))
        at(r, 1, (leave, 4), (b, 1), (z, 0))
        at(r, 2, (leave, 5), (b, 2), (z, 1))
        return carry

    lax.fori_loop(0, parts, outer_step, 0)
    def keep_sum(g, value):
        part = width_all // 2
        small[2 * g : 2 * g + 1, :] = value[:, 0:part]
        small[2 * g + 1 : 2 * g + 2, :] = value[:, part:]

    small[...] = jnp.zeros_like(small)
    back, sum3 = norm_back(dn[...], x2[...], line_of(gain3))
    dn[...] = cot_ref[...].astype(F32) + back
    keep_sum(2, sum3)
    leave(6)
    b(3)
    z(2)

    def heads_back(r, do, n, with_diag, between):
        slot = lax.rem(r, 2)
        q, kv, o = q_in[slot], kv_in.at[slot], o_in[slot].astype(F32)
        do_all = []
        delta_all = []
        for j in range(3):
            do_h = do[:, DH * j : DH * (j + 1)]
            inv = 1.0 / l_in[slot, :, 32 * j : 32 * j + 1]
            o_h = o[:, DH * j : DH * (j + 1)]
            delta_all.append(jnp.sum(do_h * o_h * inv, axis=1, keepdims=True))
            do_all.append(do_h * inv)
        do_t = low(jnp.transpose(jnp.concatenate(do_all, axis=1)))
        q_t = flip(q)
        dq = []
        for j in range(3):
            p_h = p_in.at[slot, j]
            k_h = kv[0:n, DH * j : DH * (j + 1)]
            v_h = kv[0:n, DH * (3 + j) : DH * (4 + j)]
            dp_buf[j % 2, :, 0:n] = mm_nt(low(do_all[j]), v_h)
            total = None
            for s, m in chunks(rows, 32):
                ds = low(
                    p_h[s : s + m, 0:n].astype(F32)
                    * (dp_buf[j % 2, s : s + m, 0:n] - delta_all[j][s : s + m, :])
                )
                ds_buf[j % 2, s : s + m, 0:n] = ds
                if with_diag:
                    width = diag_acc.shape[2]
                    wide = jnp.concatenate([ds.astype(F32), jnp.zeros((m, width - n), F32)], axis=1)
                    for b in range(0, m, 8):
                        turned = pltpu.roll(wide[b : b + 8, :], (width - s - b) % width, 1)
                        total = turned if total is None else total + turned
            if with_diag:
                diag_acc[which(r) * 3 + j] = total
            ds_h = ds_buf[j % 2, :, 0:n]
            dq.append(low(mm(ds_h, k_h)))
            dkv_t[DH * j : DH * (j + 1), 0:n] = mm(q_t[DH * j : DH * (j + 1), :], ds_h)
            dkv_t[DH * (3 + j) : DH * (4 + j), 0:n] = mm(
                do_t[DH * j : DH * (j + 1), :], p_h[:, 0:n]
            )
            if j == 1:
                between()
        return jnp.concatenate(dq, axis=1), low(jnp.transpose(dkv_t[:, 0:n]))

    def attention_step(phase, i, middle):
        slot = lax.rem(i, 2)
        n = all_keys[phase]
        t = 12 - 4 * phase + i
        back_wait(phase, i)

        @pl.when(i + 1 < parts)
        def _():
            back_prefetch(phase, i + 1)

        if phase == 1:

            @pl.when(i + 1 == parts)
            def _():
                back_prefetch(0, jnp.int32(0))

        do = low(mm_nt(low(dn[...]), block(w, slot, 0, 576, 768))).astype(F32)
        dq, dkv = heads_back(i, do, n, phase == 0, lambda: middle(i))
        put(t, low(mm(keys_t[:, 0:n], dkv)))
        both = [low(mm(rows_t2[...], dq)), low(mm(rows_t[...], o_in[slot]))]
        put(t, jnp.concatenate(both, axis=1), 384)
        store(t).start()
        acc[...] += mm(dq, block(w, slot, 0, 384, 576))
        enc_acc[0:n, :] += mm(dkv, block(w, slot, 0, 0, 384))
        store(t).wait()

    rows_t[...] = flip(low(dn[...]))
    rows_t2[...] = flip(n2[...])
    keys_t[...] = flip(enc[...].reshape(keys, width_all))
    acc[...] = jnp.zeros_like(acc)
    enc_acc[...] = jnp.zeros_like(enc_acc)

    def cross_back_step(i, carry):
        def middle(i):
            at(i, 0, (leave, 7), (b, 4), (z, 3))
            at(i, 1, (a, 7), (b, 6), (z, 5))
            at(i, 2, (a, 9), (b, 7), (z, 6))
            at(i, 3, (a, 10), (b, 8), (z, 7))

        attention_step(1, i, middle)
        at(i, 0, (c, 8), (b, 5), (z, 4))
        at(i, 1, (a, 8), (c, 9))
        at(i, 2, (c, 10))
        at(i, 3, (c, 11))
        return carry

    lax.fori_loop(0, parts, cross_back_step, 0)
    enc[...] = low(enc_acc[...]).reshape(enc.shape)
    denc_copy.start()
    back, sum2 = norm_back(acc[...], x1[...], line_of(gain2))
    dn[...] += back
    keep_sum(1, sum2)
    b(9)
    z(8)

    own_start(3, 1)
    far_copy(3, 1, 1, 1).start()
    rows_t[...] = flip(low(dn[...]))
    rows_t2[...] = flip(nbuf[rows : 2 * rows, :])
    keys_t[:, 0:own_keys] = flip(nbuf[...])
    acc[...] = jnp.zeros_like(acc)
    enc_acc[0:own_keys, :] = jnp.zeros((own_keys, width_all), F32)

    def self_back_step(i, carry):
        def middle(i):
            at(i, 0, (a, 11), (b, 10), (z, 9))
            at(i, 1, (a, 12), (b, 11), (z, 10))
            at(i, 2, (a, 13), (b, 12), (z, 11))
            at(i, 3, (a, 14), (b, 13), (z, 12))

        attention_step(0, i, middle)
        at(i, 0, (c, 12))
        at(i, 1, (c, 13))
        at(i, 2, (c, 14))
        at(i, 3, (c, 15))
        return carry

    lax.fori_loop(0, parts, self_back_step, 0)
    for r in (2, 3):
        far_copy(3, r, r - 2, 0).start()
    gain = line_of(gain1)
    back, sum1a = norm_back(enc_acc[0:rows, :], xa[...].astype(F32), gain)
    n2[...] = low(back)

    @pl.when(half == 1)
    def _():
        dxa_copy.start()

    a(15)
    b(14)
    z(13)
    back, sum1 = norm_back(
        acc[...] + enc_acc[rows : 2 * rows, :], x_ref[...].astype(F32), gain
    )
    dn[...] += back
    keep_sum(0, sum1 + sum1a)
    count = 8 * diag_acc.shape[0]
    turned = jnp.dot(
        diag_acc[...].reshape(count, diag_acc.shape[2]),
        spread[...],
        precision=lax.Precision.HIGHEST,
        preferred_element_type=F32,
    )
    kinds = onehot.shape[0]
    row = lax.rem(lax.broadcasted_iota(jnp.int32, turned.shape, 0), 8)
    place_of = lax.div(lax.broadcasted_iota(jnp.int32, turned.shape, 1), kinds)
    turned = jnp.where(row == place_of, turned, 0.0)
    turned = jnp.sum(turned.reshape(count // 8, 8, turned.shape[1]), axis=1)
    table = turned[:, 0:kinds]
    for k in range(1, 8):
        table = table + turned[:, kinds * k : kinds * (k + 1)]
    for r in range(parts):
        at = lax.rem(z_me + r, parts)
        for p in range(parts):

            @pl.when(at == p)
            def _(r=r, p=p):
                for j in range(3):
                    lane = kinds * (3 * p + j)
                    small[6:7, lane : lane + kinds] = table[3 * r + j : 3 * r + j + 1]

    sums.start(small[...])
    for copy in own_copies(3, 1):
        copy.wait()
    x2[...] += mm(hid[0], block(w, 0, 1))
    far_copy(3, 1, 1, 1).wait()
    x2[...] += mm(hid[1], block(w, 1, 1))
    sums.turn()
    b(15)
    z(14)
    for r in (2, 3):
        far_copy(3, r, r - 2, 0).wait()
        x2[...] += mm(hid[r], block(w, r - 2, 0))
    result_ref[...] = low(x2[...])
    denc_copy.wait()
    enc[half] = low(enc[half].astype(F32) + denc_in[...].astype(F32))
    denc_done = pltpu.make_async_copy(enc.at[half], denc_out, out_sem.at[0])
    denc_done.start()
    z(15)

    @pl.when(half == 1)
    def _():
        dxa_copy.wait_send()
        n3[...] = low(dn[...])

    @pl.when(half == 0)
    def _():
        dxa_copy.wait_recv()
        n3[...] = low(dn[...] + dxa_in[...].astype(F32))

    dx_done = pltpu.make_async_copy(n3, dx_out, out_sem.at[1])
    dx_done.start()
    scatter.finish()
    small_out[...] = sums.result()
    for t in range(TICKS):
        scatter.c_copy(t, away(t)).wait_send()
    gather.sent()
    denc_done.wait()
    dx_done.wait()


def finish_kernel(
    result_in, dx, denc, total, small,
    result, input_grad, encoder_grad,
    g_gain1, gsq, gsk, gsv, gso, g_gain2, gcq, gck, gcv, gco, g_gain3, gfi, gfo, lines,
):
    result[...] = result_in[...]
    input_grad[...] = dx[...]
    encoder_grad[...] = denc[...]
    width = result.shape[1]
    for g, (k, v, q, o) in enumerate(((gsk, gsv, gsq, gso), (gck, gcv, gcq, gco))):
        k[...] = total[g, :, 0:192]
        v[...] = total[g, :, 192:384]
        q[...] = total[g, :, 384:576]
        o[...] = jnp.transpose(total[g, :, 576:768])
    gfi[...] = total[2]
    gfo[...] = total[3]
    for row, gain in enumerate((g_gain1, g_gain2, g_gain3)):
        part = small[2 * row : 2 * row + 2, :]
        gain[...] = jnp.concatenate([part[0:1], part[1:2]], axis=1).reshape(width)
    z = lax.axis_index("mp")
    for p in range(4):

        @pl.when(z == p)
        def _(p=p):
            kinds = lines.shape[1]
            for j in range(3):
                lane = kinds * (3 * p + j)
                lines[j : j + 1, :] = small[6:7, lane : lane + kinds]


def across(value, axis, n_dp):
    groups = n_dp // 8
    whole = lax.all_gather(value, "dp", axis=0, tiled=False)
    whole = whole.reshape(groups, 8, *value.shape).sum(0)
    whole = jnp.concatenate([whole[k] for k in range(8)], axis=axis)
    share = whole.shape[axis] // n_dp
    return lax.dynamic_slice_in_dim(whole, lax.axis_index("dp") * share, share, axis)


def across_small(value, n_dp):
    whole = lax.all_gather(value, "dp", axis=0, tiled=False)
    return whole.reshape(n_dp // 8, 8, *value.shape)[:, 0].sum(0)


def body(
    inputs, encoded, cotangent, lengths, buckets,
    self_gain, self_query, self_key, self_value, self_output, bias_table,
    cross_gain, cross_query, cross_key, cross_value, cross_output,
    feed_gain, feed_inner, feed_output_weight,
):
    rows, width = inputs.shape
    parts = lax.axis_size("mp")
    n_dp = lax.axis_size("dp")
    halves = parts // lengths.shape[0]
    assert halves == 2 and buckets.shape[0] == 2 * rows and parts == 4
    z = lax.axis_index("mp")
    enc_rows = encoded.shape[0]
    vmem = pl.BlockSpec(memory_space=pltpu.VMEM)
    smem = pl.BlockSpec(memory_space=pltpu.SMEM)
    hbm = pl.BlockSpec(memory_space=pl.ANY)
    sds = jax.ShapeDtypeStruct

    share = width // 8
    diag = 1024
    heads = 3 * parts
    keys = 2 * enc_rows
    gains = [self_gain, cross_gain, feed_gain]
    split = lambda v: v.reshape(2, share, width)
    whole = lambda v: v.reshape(4, 2, share, width)
    kinds = bias_table.shape[0]
    kept = [
        kind
        for n in (2 * rows, keys)
        for kind in (
            sds((parts, rows, 192), BF16),
            sds((parts, n, 384), BF16),
            sds((heads, rows, n), BF16),
            sds((parts, rows, 192), BF16),
            sds((parts, rows, 128), F32),
        )
    ]
    half_share = share // 2
    bf, ff = (lambda *shape: pltpu.VMEM(shape, BF16)), (lambda *shape: pltpu.VMEM(shape, F32))
    dma = lambda *shape: pltpu.SemaphoreType.DMA(shape)
    result, summed, small, input_grad, encoder_grad, *_ = pl.pallas_call(
        functools.partial(layer_kernel, halves),
        out_shape=[
            sds((rows, width), BF16),
            sds((4, share, width), F32),
            sds((8, width // 2), F32),
            sds((rows, width), BF16),
            sds((enc_rows, width), BF16),
            sds((4, parts, 4, 2, share, width), BF16),
            sds((TICKS, 4, 2, share, width), BF16),
            *kept,
        ],
        in_specs=[smem, vmem, vmem, hbm] + [vmem] * 5 + [hbm] * 10,
        out_specs=[vmem] * 3 + [hbm] * (4 + len(kept)),
        scratch_shapes=[
            bf(2, 2, 4, 2, share, width), bf(2, enc_rows, width), ff(parts, 8, diag),
            ff(rows, 2 * rows), ff(kinds, diag), ff(diag, 8 * kinds), bf(rows, width), ff(8, 128), ff(parts, 8, 128),
            bf(2 * rows, width), bf(rows, width), bf(rows, width),
            bf(2, rows, 192), bf(2, keys, 384), bf(2, 3, rows, keys), bf(2, rows, 192),
            ff(2, rows, 128), ff(rows, width), ff(rows, width),
            bf(parts, rows, width), bf(parts, rows, width), ff(rows, width), ff(rows, width),
            bf(2, 4, 2, share, width), bf(2, 4, share, width),
            bf(width, rows), bf(width, rows), bf(width, keys),
            ff(2, rows, keys), bf(2, rows, keys), ff(384, keys), ff(keys, width),
            ff(heads, 8, diag),
            bf(rows, width), bf(enc_rows, width), ff(8, width // 2),
            bf(C_RING, 4, share, width), bf(A_RING, 2, 2, half_share, width),
            bf(B_RING, 2, half_share, width), bf(TICKS, share, width),
            bf(OUT_RING, 2, 2, half_share, width), bf(KEEP, 2, 2, half_share, width),
            bf(OUT_RING, 2, half_share, width), ff(KEEP, 2, half_share, width),
            bf(Z_RING, share, width), ff(8, 8, width // 2), ff(parts, 8, width // 2),
            dma(2, 2), dma(2, 4), pltpu.SemaphoreType.DMA, dma(5, 2), dma(5, 2), dma(2), dma(2),
            dma(2),
            dma(Gather.chunks, parts - 1), dma(Gather.chunks, parts - 1),
            dma(Gather.chunks, 5), dma(Gather.chunks, 5), dma(7), dma(7),
            dma(2, 6, TICKS), pltpu.SemaphoreType.REGULAR((5,)), dma(10), dma(10),
        ],
        compiler_params=pltpu.CompilerParams(
            collective_id=1, has_side_effects=True, vmem_limit_bytes=VMEM_BYTES
        ),
        name="layer",
    )(
        lengths, inputs, cotangent, encoded, *gains, buckets, bias_table.T,
        split(self_key.T), split(self_value.T), split(self_query.T), split(self_output),
        split(cross_key.T), split(cross_value.T), split(cross_query.T), split(cross_output),
        whole(feed_inner), whole(feed_output_weight),
    )

    f32 = lambda *shape: sds(shape, F32)
    outs = pl.pallas_call(
        finish_kernel,
        out_shape=[
            sds((rows, width), BF16), sds((rows, width), BF16), sds((enc_rows, width), BF16),
            f32(width), f32(share, 192), f32(share, 192), f32(share, 192), f32(192, share),
            f32(width), f32(share, 192), f32(share, 192), f32(share, 192), f32(192, share),
            f32(width), f32(share, width), f32(share, width), f32(3, kinds),
        ],
        in_specs=[vmem] * 5,
        out_specs=[vmem] * 17,
        name="finish",
    )(result, input_grad, encoder_grad, summed, small)
    result, input_grad, encoder_grad, *grads, lines = outs
    if n_dp > 8:
        axes = (None, 0, 0, 0, 1, None, 0, 0, 0, 1, None, 0, 0)
        grads = [
            across_small(value, n_dp) if axis is None else across(value, axis, n_dp)
            for value, axis in zip(grads, axes)
        ]
        lines = across_small(lines, n_dp)
    return (result, input_grad, encoder_grad, *grads[0:5], lines.T, *grads[5:-1], grads[-1].T)


def solution(mesh):
    rows = P(("dp", "mp"), None)
    across, down = P(None, "mp"), P("mp", None)
    return jax.shard_map(
        body,
        mesh=mesh,
        in_specs=(
            rows, rows, rows, P("dp"), P(),
            P(), across, across, across, down, across,
            P(), across, across, across, down,
            P(), across, down,
        ),
        out_specs=(
            rows, rows, rows,
            P(), P("dp", "mp"), P("dp", "mp"), P("dp", "mp"), P("mp", "dp"), P(None, "mp"),
            P(), P("dp", "mp"), P("dp", "mp"), P("dp", "mp"), P("mp", "dp"),
            P(), P("dp", "mp"), P("mp", "dp"),
        ),
        check_vma=False,
    )
```
